128 devices in a mesh: seq: 8 (over y, core), head: 16 (over z, x).
Axes of the slice: x: 4, y: 4, z: 4, core: 2. Of those that a mesh axis runs over, the one named last changes fastest.
Arguments:
- inputs: bfloat16 [8192, 6144], P('seq', 'head'), may hold values from -6 to 6
- frozen: bfloat16 [3, 8192, 8192], P(None, 'seq', 'head'), may hold values from -6 to 6
- adapter_down: bfloat16 [3, 6144, 64], P(None, 'head'), may hold values from -0.078125 to 0.078125
- adapter_up: bfloat16 [3, 64, 8192], P(None, None, 'head'), may hold values from -0.75 to 0.75
- out_grad: bfloat16 [8192, 8192], P('seq', 'head'), may hold values from -0.29882812 to 0.29882812
- log_decay: bfloat16 [64, 8192], P('head', 'seq'), may hold values from -2.5 to 0, as said below
- doc_start: int32 [8192], P('seq'), may hold values from 0 to 1, as said below
- lengths: int32 [8], replicated, may hold values from 0 to 1024, as said below
Outputs:
- attn_out: bfloat16 [8192, 8192], P('seq', 'head')
- projection_grad: bfloat16 [3, 8192, 8192], P(None, 'seq', 'head')
- down_grad: float32 [3, 6144, 64], P(None, 'head')
- up_grad: float32 [3, 64, 8192], P(None, None, 'head')
The draws below stay inside these ranges and needn't reach their ends.
Inputs may be any that keep to these rules, and one draw needn't show every extreme that they name: lengths[i] live slots stand at the front of the 1024 slots of the i-th index of seq; they add up to 4096; the sum of the first i of them lies between i * 512 and (i + 1) * 512; one of them equals 1024. `doc_start`: values at slots that are not live are not read. `log_decay`: values at slots that are not live are not read.
All inputs are finite; a program needn't handle non-finite values.
Results may differ from the reference program's by a relative error of at most 0.028.
Values may be sent and summed in bfloat16 or wider, within the bound.
No kernel may reach another device: no remote copies, remote signals or barrier semaphores. Data moves between devices by JAX's collectives and lax.ppermute only.
A program may use at most 128 MiB of HBM per device.

```python
import jax
import jax.numpy as jnp
from jax import lax

D = 6144
HEADS = 64
DH = 128
RANK = 64
TOK_DEV = 512
CAP = 1024
SLAB = 4096
SLOT_TOTAL = 8192
FEATURES = 8192
N_SEQ = 8


def draw_lengths(key, part):
    key = jax.random.fold_in(key, 17)
    first_key, second_key = jax.random.split(key)
    drifts = jax.random.randint(first_key, (N_SEQ + 1,), 0, TOK_DEV + 1).astype(jnp.int32)
    chosen = jax.random.randint(second_key, (), 0, N_SEQ - 1).astype(jnp.int32)
    marker = jnp.arange(N_SEQ + 1, dtype=jnp.int32)
    drifts = jnp.where(marker == chosen, 0, drifts)
    drifts = jnp.where(marker == chosen + 1, TOK_DEV, drifts)
    drifts = jnp.where((marker == 0) | (marker == N_SEQ), 0, drifts)
    return (TOK_DEV + drifts[1:] - drifts[:-1]).astype(jnp.int32)


def draw_doc_start(key, part):
    key = jax.random.fold_in(key, 23)
    first_key, second_key = jax.random.split(key)
    picks = jax.random.randint(first_key, (SLOT_TOTAL,), 0, SLOT_TOTAL)
    forced = jax.random.randint(second_key, (), 1, TOK_DEV).astype(jnp.int32)
    slot_number = jnp.arange(SLOT_TOTAL, dtype=jnp.int32)
    return ((picks < 3) | (slot_number == forced)).astype(jnp.int32)


def draw_log_decay(key, part):
    key = jax.random.fold_in(key, 29)
    random_subkeys = jax.random.split(key, 7)
    quick = jax.random.randint(random_subkeys[0], (HEADS,), 0, 2) == 1
    fast_rate = jax.random.uniform(random_subkeys[1], (HEADS,), jnp.float32, 1.0 / 50.0, 1.0 / 30.0)
    slow_rate = jax.random.uniform(random_subkeys[2], (HEADS,), jnp.float32, 0.02, 0.1) / (TOK_DEV * N_SEQ)
    baseline_rate = jnp.where(quick, fast_rate, slow_rate)
    coarse_estimate = jnp.exp(jax.random.uniform(random_subkeys[3], (HEADS, SLOT_TOTAL), jnp.float32, -0.7, 0.7))
    device_multiplier = jnp.repeat(jnp.exp(jax.random.uniform(random_subkeys[4], (HEADS, N_SEQ), jnp.float32, -0.7, 0.7)), CAP, axis=1)
    spike_position = jax.random.randint(random_subkeys[5], (3,), 0, SLOT_TOTAL)
    spike_strength = jnp.log(jax.random.uniform(random_subkeys[6], (3,), jnp.float32, 0.5, 0.8))
    spike_amount = jnp.sum(jnp.where(jnp.arange(SLOT_TOTAL)[None, :] == spike_position[:, None], spike_strength[:, None], 0.0), axis=0)
    value_rows = -baseline_rate[:, None] * coarse_estimate * device_multiplier + spike_amount[None, :]
    return value_rows.astype(jnp.bfloat16)


def block_levels(own_key, dims, cuts, low, top_value):
    gain, own = 1.0, jax.random.fold_in(own_key, 6)
    for dim, shards_of in cuts:
        steps = jnp.exp(jax.random.uniform(jax.random.fold_in(own, dim), (shards_of,), jnp.float32, low / len(cuts), top_value / len(cuts)))
        gain = gain * jnp.repeat(steps, dims[dim] // shards_of).reshape([-1 if axis == dim else 1 for axis in range(len(dims))])
    return gain


def noise(rng, shape, scale, limit, pieces=(), kind=jnp.bfloat16):
    gain = block_levels(rng, shape, pieces, -0.22, 0.18) if pieces else 1.0
    drawn = jax.random.normal(rng, shape, jnp.float32) * scale * gain
    return jnp.minimum(jnp.maximum(drawn, -limit), limit).astype(kind)


def setup_inputs(seed: int = 0) -> dict:
    splits = jax.random.split(jax.random.key(seed), 9)
    inputs = noise(splits[0], (SLOT_TOTAL, D), 1.0, 6.0, ((0, 8), (1, 16)))
    frozen = noise(splits[1], (3, SLOT_TOTAL, FEATURES), 1.0, 6.0, ((1, 8), (2, 16)))
    adapter_down = noise(splits[2], (3, D, RANK), D ** -0.5, 0.078125, ((1, 16),))
    adapter_up = noise(splits[3], (3, RANK, FEATURES), RANK ** -0.5, 0.75, ((2, 16),))
    out_grad = noise(splits[4], (SLOT_TOTAL, FEATURES), 0.05, 0.29882812, ((0, 8), (1, 16)))
    log_decay = draw_log_decay(jax.random.fold_in(splits[8], 71), 0)
    doc_start = draw_doc_start(jax.random.fold_in(splits[8], 71), 0)
    lengths = draw_lengths(jax.random.fold_in(splits[8], 71), 0)
    return {"inputs": inputs, "frozen": frozen, "adapter_down": adapter_down, "adapter_up": adapter_up, "out_grad": out_grad, "log_decay": log_decay, "doc_start": doc_start, "lengths": lengths}


HIGHEST = lax.Precision.HIGHEST


def block_terms(decay, starts):
    cumulative = jnp.cumsum(decay)
    segment = jnp.cumsum(starts)
    row_count = decay.shape[0]
    causal = jnp.arange(row_count)[:, None] >= jnp.arange(row_count)[None, :]
    allowed = causal & (segment[:, None] == segment[None, :])
    spread = jnp.where(allowed, cumulative[:, None] - cumulative[None, :], 0.0)
    weights = jnp.where(allowed, jnp.exp(spread), 0.0)
    entering = jnp.where(segment == 0, jnp.exp(cumulative), 0.0)
    leaving = jnp.where(segment == segment[-1], jnp.exp(cumulative[-1] - cumulative), 0.0)
    passing = jnp.where(segment[-1] == 0, jnp.exp(cumulative[-1]), 0.0)
    return weights, entering, leaving, passing


def head_pass(queries, keyset, value_rows, grad_out, decay, starts):
    total = queries.shape[0]
    head_size = queries.shape[1]
    block_rows = min(1024, total)
    block_count = total // block_rows
    inverse = 1.0 / head_size
    shaped = tuple(item.reshape((block_count, block_rows) + item.shape[1:]) for item in (queries, keyset, value_rows, grad_out, decay, starts))

    def forward(carried, block):
        block_query, block_key, block_value, block_grad, block_decay, block_start = block
        weights, entering, leaving, passing = block_terms(block_decay, block_start)
        scores = jnp.dot(block_query, block_key.T, preferred_element_type=jnp.float32)
        weighted = (scores * weights * inverse).astype(jnp.bfloat16)
        value_wide = block_value.astype(jnp.float32)
        query_wide = block_query.astype(jnp.float32)
        result = jnp.dot(weighted, block_value, preferred_element_type=jnp.float32) + (entering * inverse)[:, None] * jnp.dot(query_wide, carried, precision=HIGHEST)
        key_wide = block_key.astype(jnp.float32) * leaving[:, None]
        updated = passing * carried + jnp.dot(key_wide.T, value_wide, precision=HIGHEST)
        return updated, (result.astype(jnp.bfloat16), carried)

    zero_state = jnp.zeros((head_size, head_size), jnp.float32)
    final_state, (outputs, before) = lax.scan(forward, zero_state, shaped)

    def backward(later_state, block):
        block_query, block_key, block_value, block_grad, block_decay, block_start, carried = block
        weights, entering, leaving, passing = block_terms(block_decay, block_start)
        scores = jnp.dot(block_query, block_key.T, preferred_element_type=jnp.float32)
        weighted = (scores * weights * inverse).astype(jnp.bfloat16)
        grad_weighted = (jnp.dot(block_grad, block_value.T, preferred_element_type=jnp.float32) * weights * inverse).astype(jnp.bfloat16)
        query_wide = block_query.astype(jnp.float32)
        key_wide = block_key.astype(jnp.float32)
        value_wide = block_value.astype(jnp.float32)
        grad_wide = block_grad.astype(jnp.float32)
        query_grad = jnp.dot(grad_weighted, block_key, preferred_element_type=jnp.float32) + (entering * inverse)[:, None] * jnp.dot(grad_wide, carried.T, precision=HIGHEST)
        key_grad = jnp.dot(grad_weighted.T, block_query, preferred_element_type=jnp.float32) + leaving[:, None] * jnp.dot(value_wide, later_state.T, precision=HIGHEST)
        value_grad = jnp.dot(weighted.T, block_grad, preferred_element_type=jnp.float32) + leaving[:, None] * jnp.dot(key_wide, later_state, precision=HIGHEST)
        scaled_query = query_wide * (entering * inverse)[:, None]
        updated = passing * later_state + jnp.dot(scaled_query.T, grad_wide, precision=HIGHEST)
        return updated, (query_grad.astype(jnp.bfloat16), key_grad.astype(jnp.bfloat16), value_grad.astype(jnp.bfloat16))

    first_state, grads = lax.scan(backward, zero_state, shaped + (before,), reverse=True)
    flat = tuple(item.reshape(total, head_size) for item in (outputs,) + tuple(grads))
    return flat


def to_heads(matrix):
    return matrix.reshape(SLAB, HEADS, DH).transpose(1, 0, 2)


def from_heads(stacked):
    return stacked.transpose(1, 0, 2).reshape(SLAB, HEADS * DH)


def reference(inputs, frozen, adapter_down, adapter_up, out_grad, log_decay, doc_start, lengths):
    lengths_int = lengths.astype(jnp.int32)
    totals = jnp.cumsum(lengths_int).astype(jnp.int32)
    begins = (totals - lengths_int).astype(jnp.int32)
    position = jnp.arange(SLAB, dtype=jnp.int32)
    owner = jnp.sum((position[:, None] >= totals[None, :N_SEQ - 1]).astype(jnp.int32), axis=1).astype(jnp.int32)
    source = (owner * CAP + position - begins[owner]).astype(jnp.int32)
    rows_in = inputs[source]
    grad_rows = out_grad[source]
    decay_rows = log_decay[:, source].astype(jnp.float32)
    start_rows = doc_start[source].astype(jnp.float32)
    lows = []
    projections = []
    for number in range(3):
        low_part = jnp.dot(rows_in, adapter_down[number], preferred_element_type=jnp.float32).astype(jnp.bfloat16)
        lows.append(low_part)
        summed = frozen[number][source].astype(jnp.float32) + jnp.dot(low_part, adapter_up[number], preferred_element_type=jnp.float32)
        projections.append(summed.astype(jnp.bfloat16))

    def per_head(item):
        return head_pass(item[0], item[1], item[2], item[3], item[4], start_rows)

    mapped = lax.map(per_head, (to_heads(projections[0]), to_heads(projections[1]), to_heads(projections[2]), to_heads(grad_rows), decay_rows))
    merged = [from_heads(item) for item in mapped]
    slot_number = jnp.arange(SLOT_TOTAL, dtype=jnp.int32)
    slot_owner = (slot_number // CAP).astype(jnp.int32)
    slot_index = (slot_number % CAP).astype(jnp.int32)
    live = slot_index < lengths_int[slot_owner]
    target = jnp.clip(begins[slot_owner] + slot_index, 0, SLAB - 1).astype(jnp.int32)
    placed = [jnp.where(live[:, None], item[target], jnp.zeros((), jnp.bfloat16)).astype(jnp.bfloat16) for item in merged]
    down_list = []
    up_list = []
    for number in range(3):
        grad_proj = merged[number + 1]
        low_grad = jnp.dot(grad_proj, adapter_up[number].T, preferred_element_type=jnp.float32).astype(jnp.bfloat16)
        up_list.append(jnp.dot(lows[number].T, grad_proj, preferred_element_type=jnp.float32))
        down_list.append(jnp.dot(rows_in.T, low_grad, preferred_element_type=jnp.float32))
    return placed[0], jnp.stack(placed[1:]), jnp.stack(down_list), jnp.stack(up_list)
```

```python
import functools

import jax
import jax.numpy as jnp
from jax import lax
from jax.experimental import pallas as pl
from jax.experimental.pallas import tpu as pltpu
from jax.sharding import PartitionSpec as P

F32 = jnp.float32
BF16 = jnp.bfloat16
CHUNK = 256
VMEM_BYTES = 48 * 1024 * 1024
NEGATIVE = -1e30

CUM, SEG, ENTER, LEAVE, ENTER_ALL, LEAVE_ALL = 0, 4, 8, 12, 16, 20


def dot_nn(a, b):
    return lax.dot_general(a, b, (((1,), (0,)), ((), ())), preferred_element_type=F32)


def dot_nt(a, b):
    return lax.dot_general(a, b, (((1,), (1,)), ((), ())), preferred_element_type=F32)


def dot_tn(a, b):
    return lax.dot_general(a, b, (((0,), (0,)), ((), ())), preferred_element_type=F32)


def params(**more):
    return pltpu.CompilerParams(vmem_limit_bytes=VMEM_BYTES, **more)


def cost(flops, moved):
    return pl.CostEstimate(flops=int(flops), bytes_accessed=int(moved), transcendentals=0)


VMEM = pl.BlockSpec(memory_space=pltpu.VMEM)
SMEM = pl.BlockSpec(memory_space=pltpu.SMEM)


def low_kernel(x_ref, down_ref, out_ref):
    rank = down_ref.shape[2]
    x = x_ref[...]
    for c in range(3):
        out_ref[:, c * rank : (c + 1) * rank] = dot_nn(x, down_ref[c]).astype(BF16)


def partial_low(x, down):
    rows, width = x.shape
    rank = down.shape[2]
    block = min(512, rows)
    return pl.pallas_call(
        low_kernel,
        out_shape=jax.ShapeDtypeStruct((rows, 3 * rank), BF16),
        grid=(rows // block,),
        in_specs=[
            pl.BlockSpec((block, width), lambda i: (i, 0)),
            pl.BlockSpec(down.shape, lambda i: (0, 0, 0)),
        ],
        out_specs=pl.BlockSpec((block, 3 * rank), lambda i: (i, 0)),
        compiler_params=params(),
        name="partial_low",
    )(x, down)


def sum_spread_kernel(in_ref, out_ref):
    count = in_ref.shape[0]
    total = in_ref[0].astype(F32)
    for i in range(1, count):
        total = total + in_ref[i].astype(F32)
    total = total.astype(BF16)
    for i in range(count):
        out_ref[i] = total


def sum_over_head(part):
    count = lax.axis_size("head")
    rows, width = part.shape
    pieces = part.reshape(count, rows // count, width)
    pieces = lax.all_to_all(pieces, "head", 0, 0)
    spread = pl.pallas_call(
        sum_spread_kernel,
        out_shape=jax.ShapeDtypeStruct(pieces.shape, BF16),
        in_specs=[VMEM],
        out_specs=VMEM,
        compiler_params=params(),
        name="sum_spread",
    )(pieces)
    return lax.all_to_all(spread, "head", 0, 0).reshape(rows, width)


def decay_kernel(meta_ref, decay_ref, start_ref, row_ref, col_ref, pass_ref):
    heads, rows = decay_ref.shape
    live = meta_ref[0]
    slot = lax.broadcasted_iota(jnp.int32, (1, rows), 1)
    keep = slot < live
    decay = jnp.where(keep, decay_ref[...].astype(F32), 0.0)
    starts = jnp.where(keep, start_ref[...].astype(F32), 0.0)
    both = jnp.concatenate([decay, starts, jnp.zeros((8 - heads - 1, rows), F32)], axis=0)
    both = both.astype(BF16)
    row_i = lax.broadcasted_iota(jnp.int32, (CHUNK, CHUNK), 0)
    col_i = lax.broadcasted_iota(jnp.int32, (CHUNK, CHUNK), 1)
    upper = jnp.where(row_i <= col_i, 1.0, 0.0).astype(BF16)
    lower = jnp.where(row_i >= col_i, 1.0, 0.0).astype(BF16)
    count = rows // CHUNK
    enters, leaves, passes = [], [], []
    for c in range(count):
        span = slice(c * CHUNK, (c + 1) * CHUNK)
        piece = both[:, span]
        by_row = dot_nn(piece, upper)
        by_col = dot_nt(lower, piece)
        row_ref[:, span] = by_row
        col_ref[span, 0:8] = by_col
        cum = by_col[:, :heads]
        seg = by_col[:, heads : heads + 1]
        cum_end = by_col[CHUNK - 1 : CHUNK, :heads]
        seg_end = by_col[CHUNK - 1 : CHUNK, heads : heads + 1]
        enter = jnp.where(seg == 0.0, jnp.exp(cum), 0.0)
        leave = jnp.where(seg == seg_end, jnp.exp(cum_end - cum), 0.0)
        col_ref[span, ENTER : ENTER + heads] = enter
        col_ref[span, LEAVE : LEAVE + heads] = leave
        enters.append(enter)
        leaves.append(leave)
        passes.append(jnp.where(seg_end == 0.0, jnp.exp(cum_end), 0.0))
        end_row = by_row[:, CHUNK - 1 : CHUNK]
        passing_col = jnp.where(end_row[heads : heads + 1] == 0.0, jnp.exp(end_row[:heads]), 0.0)
        pass_ref[c * heads : (c + 1) * heads, :] = jnp.broadcast_to(passing_col, (heads, 128))
    before = jnp.ones((1, heads), F32)
    for c in range(count):
        span = slice(c * CHUNK, (c + 1) * CHUNK)
        col_ref[span, ENTER_ALL : ENTER_ALL + heads] = enters[c] * before
        before = before * passes[c]
    after = jnp.ones((1, heads), F32)
    for c in reversed(range(count)):
        span = slice(c * CHUNK, (c + 1) * CHUNK)
        col_ref[span, LEAVE_ALL : LEAVE_ALL + heads] = leaves[c] * after
        after = after * passes[c]


def decay_tables(meta, decay, starts):
    heads, rows = decay.shape
    count = rows // CHUNK
    return pl.pallas_call(
        decay_kernel,
        out_shape=(
            jax.ShapeDtypeStruct((8, rows), F32),
            jax.ShapeDtypeStruct((rows, 128), F32),
            jax.ShapeDtypeStruct((count * heads, 128), F32),
        ),
        in_specs=[SMEM, VMEM, VMEM],
        out_specs=(VMEM, VMEM, VMEM),
        compiler_params=params(),
        cost_estimate=cost(4e9, 1e6),
        name="decay_tables",
    )(meta, decay, starts.reshape(1, rows))


def project_kernel(
    meta_ref, frozen_ref, low_ref, up_ref, grad_ref, col_ref, pass_ref,
    moving_ref, before_ref, after_ref, summary_ref,
    own, returning, running,
):
    step = pl.program_id(0)
    count = pl.num_programs(0)
    rank = up_ref.shape[1]
    features = frozen_ref.shape[2]
    heads = features // 128
    live = meta_ref[0]

    @pl.when(step == 0)
    def _():
        own[...] = jnp.zeros_like(own)
        running[...] = jnp.ones_like(running)
        summary_ref[...] = jnp.zeros_like(summary_ref)

    slot = step * CHUNK + lax.broadcasted_iota(jnp.int32, (CHUNK, 1), 0)
    keep = slot < live
    low = low_ref[...]
    for c in range(3):
        lifted = dot_nn(low[:, c * rank : (c + 1) * rank], up_ref[c])
        summed = frozen_ref[c].astype(F32) + lifted
        moving_ref[c] = jnp.where(keep, summed, 0.0).astype(BF16)
    moving_ref[3] = jnp.where(keep, grad_ref[...].astype(F32), 0.0).astype(BF16)
    col = col_ref[...]
    for h in range(heads):
        span = slice(h * 128, (h + 1) * 128)
        passing = pass_ref[pl.ds(step * heads + h, 1), :]
        leave = col[:, LEAVE + h : LEAVE + h + 1]
        enter = col[:, ENTER + h : ENTER + h + 1]
        keyed = (moving_ref[1, :, span].astype(F32) * leave).astype(BF16)
        scaled = (moving_ref[0, :, span].astype(F32) * enter).astype(BF16)
        state = own[h]
        before_ref[0, h] = state.astype(BF16)
        own[h] = passing * state + dot_tn(keyed, moving_ref[2, :, span])
        returning[step, h] = dot_tn(scaled, moving_ref[3, :, span])

    @pl.when(step == count - 1)
    def _():
        chunks = returning.shape[0]
        size = heads * 128
        for h in range(heads):
            back = jnp.zeros((128, 128), F32)
            whole = jnp.ones((1, 128), F32)
            for c in reversed(range(chunks)):
                passing = pass_ref[c * heads + h : c * heads + h + 1, :]
                after_ref[c, h] = back.astype(BF16)
                back = passing * back + returning[c, h]
                whole = whole * passing
            summary_ref[h * 128 : (h + 1) * 128, :] = own[h].astype(BF16)
            summary_ref[size + h * 128 : size + (h + 1) * 128, :] = back.astype(BF16)
            first = whole.astype(BF16)
            rest = whole - first.astype(F32)
            second = rest.astype(BF16)
            third = (rest - second.astype(F32)).astype(BF16)
            tail = jnp.concatenate(
                [first.astype(F32), second.astype(F32), third.astype(F32), jnp.zeros((13, 128), F32)],
                axis=0,
            )
            base = 2 * size + 16 * h
            summary_ref[base : base + 16, :] = tail.astype(BF16)


def project(meta, frozen, low, up, grad, col, passes):
    _, rows, features = frozen.shape
    heads = features // 128
    count = rows // CHUNK
    summary_rows = 2 * features + 16 * heads
    return pl.pallas_call(
        project_kernel,
        out_shape=(
            jax.ShapeDtypeStruct((4, rows, features), BF16),
            jax.ShapeDtypeStruct((count, heads, 128, 128), BF16),
            jax.ShapeDtypeStruct((count, heads, 128, 128), BF16),
            jax.ShapeDtypeStruct((summary_rows, 128), BF16),
        ),
        grid=(count,),
        in_specs=[
            SMEM,
            pl.BlockSpec((3, CHUNK, features), lambda i: (0, i, 0)),
            pl.BlockSpec((CHUNK, low.shape[1]), lambda i: (i, 0)),
            pl.BlockSpec(up.shape, lambda i: (0, 0, 0)),
            pl.BlockSpec((CHUNK, features), lambda i: (i, 0)),
            pl.BlockSpec((CHUNK, 128), lambda i: (i, 0)),
            pl.BlockSpec(passes.shape, lambda i: (0, 0)),
        ],
        out_specs=(
            pl.BlockSpec((4, CHUNK, features), lambda i: (0, i, 0)),
            pl.BlockSpec((1, heads, 128, 128), lambda i: (i, 0, 0, 0)),
            pl.BlockSpec((count, heads, 128, 128), lambda i: (0, 0, 0, 0)),
            pl.BlockSpec((summary_rows, 128), lambda i: (0, 0)),
        ),
        scratch_shapes=[
            pltpu.VMEM((heads, 128, 128), F32),
            pltpu.VMEM((count, heads, 128, 128), F32),
            pltpu.VMEM((heads, 128), F32),
        ],
        compiler_params=params(dimension_semantics=("arbitrary",)),
        cost_estimate=cost(4e9, 10e6),
        name="project",
    )(meta, frozen, low, up, grad, col, passes)


def passing_of(ref, base):
    return (
        ref[base : base + 1, :].astype(F32)
        + ref[base + 1 : base + 2, :].astype(F32)
        + ref[base + 2 : base + 3, :].astype(F32)
    )


def join_kernel(meta_ref, own_ref, mate_ref, *out_refs):
    y = meta_ref[1]
    core = meta_ref[2]
    total = own_ref.shape[0]
    heads = (total - 0) // (2 * 128 + 16)
    size = heads * 128
    chips = len(out_refs) + 1
    second = core == 1
    for h in range(heads):
        rows = slice(h * 128, (h + 1) * 128)
        back_rows = slice(size + h * 128, size + (h + 1) * 128)
        base = 2 * size + 16 * h
        own_pass = passing_of(own_ref, base)
        mate_pass = passing_of(mate_ref, base)
        own_state = own_ref[rows, :].astype(F32)
        mate_state = mate_ref[rows, :].astype(F32)
        own_back = own_ref[back_rows, :].astype(F32)
        mate_back = mate_ref[back_rows, :].astype(F32)
        one = jnp.ones_like(own_pass)
        state = jnp.where(second, own_pass, one) * mate_state + jnp.where(second, one, mate_pass) * own_state
        back = jnp.where(second, one, own_pass) * mate_back + jnp.where(second, mate_pass, one) * own_back
        whole = own_pass * mate_pass
        first = whole.astype(BF16).astype(F32)
        rest = whole - first
        middle = rest.astype(BF16).astype(F32)
        third = (rest - middle).astype(BF16).astype(F32)
        tail = jnp.concatenate([first, middle, third, jnp.zeros((13, 128), F32)], axis=0).astype(BF16)
        for k, out_ref in enumerate(out_refs):
            later = y + (k + 1) < chips
            out_ref[rows, :] = jnp.where(later, state, back).astype(BF16)
            out_ref[size + 16 * h : size + 16 * h + 16, :] = tail


def join(meta, own, mate, chips):
    heads = own.shape[0] // (2 * 128 + 16)
    message = jax.ShapeDtypeStruct((heads * (128 + 16), 128), BF16)
    return pl.pallas_call(
        join_kernel,
        out_shape=(message,) * (chips - 1),
        in_specs=[SMEM, VMEM, VMEM],
        out_specs=(VMEM,) * (chips - 1),
        compiler_params=params(),
        name="join",
    )(meta, own, mate)


def inside_kernel(moving_ref, row_ref, col_ref, before_ref, after_ref, part_ref):
    features = moving_ref.shape[2]
    heads = features // 128
    row_i = lax.broadcasted_iota(jnp.int32, (CHUNK, CHUNK), 0)
    col_i = lax.broadcasted_iota(jnp.int32, (CHUNK, CHUNK), 1)
    col = col_ref[...]
    allowed = (row_i >= col_i) & (col[:, SEG : SEG + 1] == row_ref[SEG : SEG + 1, :])
    shut = jnp.where(allowed, 0.0, NEGATIVE)
    for h in range(heads):
        span = slice(h * 128, (h + 1) * 128)
        q = moving_ref[0, :, span]
        k = moving_ref[1, :, span]
        v = moving_ref[2, :, span]
        g = moving_ref[3, :, span]
        weights = jnp.exp((col[:, h : h + 1] - row_ref[h : h + 1, :]) + shut)
        a = (dot_nt(q, k) * weights).astype(BF16)
        b = (dot_nt(g, v) * weights).astype(BF16)
        enter = col[:, ENTER + h : ENTER + h + 1]
        leave = col[:, LEAVE + h : LEAVE + h + 1]
        before = before_ref[0, h]
        after = after_ref[0, h]
        part_ref[0, :, span] = dot_nn(a, v) + enter * dot_nn(q, before)
        part_ref[1, :, span] = dot_nn(b, k) + enter * dot_nt(g, before)
        part_ref[2, :, span] = dot_tn(b, q) + leave * dot_nt(v, after)
        part_ref[3, :, span] = dot_tn(a, g) + leave * dot_nn(k, after)


def inside(moving, row, col, before, after):
    _, rows, features = moving.shape
    heads = features // 128
    count = rows // CHUNK
    return pl.pallas_call(
        inside_kernel,
        out_shape=jax.ShapeDtypeStruct((4, rows, features), F32),
        grid=(count,),
        in_specs=[
            pl.BlockSpec((4, CHUNK, features), lambda i: (0, i, 0)),
            pl.BlockSpec((8, CHUNK), lambda i: (0, i)),
            pl.BlockSpec((CHUNK, 128), lambda i: (i, 0)),
            pl.BlockSpec((1, heads, 128, 128), lambda i: (i, 0, 0, 0)),
            pl.BlockSpec((1, heads, 128, 128), lambda i: (i, 0, 0, 0)),
        ],
        out_specs=pl.BlockSpec((4, CHUNK, features), lambda i: (0, i, 0)),
        compiler_params=params(dimension_semantics=("arbitrary",)),
        cost_estimate=cost(14e9, 14e6),
        name="inside",
    )(moving, row, col, before, after)


def finish_kernel(chips, meta_ref, moving_ref, part_ref, col_ref, low_ref, up_ref, mate_ref, *refs):
    message_refs = refs[: chips - 1]
    attn_ref, grad_ref, low_grad_ref, up_grad_ref, state_in, back_in, up_sum = refs[chips - 1 :]
    step = pl.program_id(0)
    count = pl.num_programs(0)
    features = moving_ref.shape[2]
    heads = features // 128
    size = heads * 128
    rank = up_ref.shape[1]
    inverse = 1.0 / 128.0

    @pl.when(step == 0)
    def _():
        y = meta_ref[1]
        second = meta_ref[2] == 1
        up_sum[...] = jnp.zeros_like(up_sum)
        for h in range(heads):
            rows = slice(h * 128, (h + 1) * 128)
            factor = jnp.ones((1, 128), F32)
            state = jnp.zeros((128, 128), F32)
            for k in range(1, chips):
                ref = message_refs[k - 1]
                state = state + jnp.where(k <= y, factor, 0.0) * ref[rows, :].astype(F32)
                factor = factor * passing_of(ref, size + 16 * h)
            factor = jnp.ones((1, 128), F32)
            back = jnp.zeros((128, 128), F32)
            for k in reversed(range(1, chips)):
                ref = message_refs[k - 1]
                back = back + jnp.where(k > y, factor, 0.0) * ref[rows, :].astype(F32)
                factor = factor * passing_of(ref, size + 16 * h)
            mate_pass = passing_of(mate_ref, 2 * size + 16 * h)
            mate_state = mate_ref[rows, :].astype(F32)
            mate_back = mate_ref[size + h * 128 : size + (h + 1) * 128, :].astype(F32)
            state_in[h] = jnp.where(second, mate_pass * state + mate_state, state).astype(BF16)
            back_in[h] = jnp.where(second, back, mate_pass * back + mate_back).astype(BF16)

    col = col_ref[...]
    for h in range(heads):
        span = slice(h * 128, (h + 1) * 128)
        q = moving_ref[0, :, span]
        k = moving_ref[1, :, span]
        v = moving_ref[2, :, span]
        g = moving_ref[3, :, span]
        enter = col[:, ENTER_ALL + h : ENTER_ALL + h + 1]
        leave = col[:, LEAVE_ALL + h : LEAVE_ALL + h + 1]
        state = state_in[h]
        back = back_in[h]
        attn_ref[:, span] = ((part_ref[0, :, span] + enter * dot_nn(q, state)) * inverse).astype(BF16)
        grad_ref[0, :, span] = ((part_ref[1, :, span] + enter * dot_nt(g, state)) * inverse).astype(BF16)
        grad_ref[1, :, span] = ((part_ref[2, :, span] + leave * dot_nt(v, back)) * inverse).astype(BF16)
        grad_ref[2, :, span] = ((part_ref[3, :, span] + leave * dot_nn(k, back)) * inverse).astype(BF16)
    low = low_ref[...]
    for c in range(3):
        lanes = slice(c * rank, (c + 1) * rank)
        low_grad_ref[:, lanes] = dot_nt(grad_ref[c], up_ref[c]).astype(BF16)
        up_sum[c] += dot_tn(low[:, lanes], grad_ref[c])

    @pl.when(step == count - 1)
    def _():
        up_grad_ref[...] = up_sum[...].astype(BF16)


def finish(meta, moving, part, col, low, up, mate, messages):
    _, rows, features = moving.shape
    heads = features // 128
    count = rows // CHUNK
    chips = len(messages) + 1
    return pl.pallas_call(
        functools.partial(finish_kernel, chips),
        out_shape=(
            jax.ShapeDtypeStruct((rows, features), BF16),
            jax.ShapeDtypeStruct((3, rows, features), BF16),
            jax.ShapeDtypeStruct(low.shape, BF16),
            jax.ShapeDtypeStruct(up.shape, BF16),
        ),
        grid=(count,),
        in_specs=[
            SMEM,
            pl.BlockSpec((4, CHUNK, features), lambda i: (0, i, 0)),
            pl.BlockSpec((4, CHUNK, features), lambda i: (0, i, 0)),
            pl.BlockSpec((CHUNK, 128), lambda i: (i, 0)),
            pl.BlockSpec((CHUNK, low.shape[1]), lambda i: (i, 0)),
            pl.BlockSpec(up.shape, lambda i: (0, 0, 0)),
            pl.BlockSpec(mate.shape, lambda i: (0, 0)),
        ]
        + [pl.BlockSpec(m.shape, lambda i: (0, 0)) for m in messages],
        out_specs=(
            pl.BlockSpec((CHUNK, features), lambda i: (i, 0)),
            pl.BlockSpec((3, CHUNK, features), lambda i: (0, i, 0)),
            pl.BlockSpec((CHUNK, low.shape[1]), lambda i: (i, 0)),
            pl.BlockSpec(up.shape, lambda i: (0, 0, 0)),
        ),
        scratch_shapes=[
            pltpu.VMEM((heads, 128, 128), BF16),
            pltpu.VMEM((heads, 128, 128), BF16),
            pltpu.VMEM(up.shape, F32),
        ],
        compiler_params=params(dimension_semantics=("arbitrary",)),
        cost_estimate=cost(4e9, 18e6),
        name="finish",
    )(meta, moving, part, col, low, up, mate, *messages)


def down_kernel(x_ref, grad_ref, out_ref):
    out_ref[...] = dot_tn(x_ref[...], grad_ref[...]).astype(BF16)


def partial_down(x, low_grad):
    return pl.pallas_call(
        down_kernel,
        out_shape=jax.ShapeDtypeStruct((x.shape[1], low_grad.shape[1]), BF16),
        in_specs=[VMEM, VMEM],
        out_specs=VMEM,
        compiler_params=params(),
        name="partial_down",
    )(x, low_grad)


def add_kernel(*refs):
    total = refs[0][...].astype(F32)
    for ref in refs[1:-1]:
        total = total + ref[...].astype(F32)
    refs[-1][...] = total.astype(refs[-1].dtype)


def add_all(arrays, dtype):
    return pl.pallas_call(
        add_kernel,
        out_shape=jax.ShapeDtypeStruct(arrays[0].shape, dtype),
        in_specs=[VMEM] * len(arrays),
        out_specs=VMEM,
        compiler_params=params(),
        name="add_all",
    )(*arrays)


def split_kernel(*refs):
    total = refs[0][...].astype(F32)
    for ref in refs[1:-1]:
        total = total + ref[...].astype(F32)
    out_ref = refs[-1]
    rank = out_ref.shape[2]
    for c in range(out_ref.shape[0]):
        out_ref[c] = total[:, c * rank : (c + 1) * rank]


def add_split(arrays, count):
    rows, width = arrays[0].shape
    return pl.pallas_call(
        split_kernel,
        out_shape=jax.ShapeDtypeStruct((count, rows, width // count), F32),
        in_specs=[VMEM] * len(arrays),
        out_specs=VMEM,
        compiler_params=params(),
        name="add_split",
    )(*arrays)


def to_mate(a):
    return lax.ppermute(a, "seq", [(i, i ^ 1) for i in range(lax.axis_size("seq"))])


def along_y(a, k):
    count = lax.axis_size("seq")
    return lax.ppermute(a, "seq", [(i, (i + 2 * k) % count) for i in range(count)])


def local(inputs, frozen, adapter_down, adapter_up, out_grad, log_decay, doc_start, lengths):
    device = lax.axis_index("seq")
    chips = lax.axis_size("seq") // 2
    meta = jnp.stack([lengths[device], device // 2, device % 2]).astype(jnp.int32)
    row, col, passes = decay_tables(meta, log_decay, doc_start)
    low = sum_over_head(partial_low(inputs, adapter_down))
    moving, before, after, summary = project(meta, frozen, low, adapter_up, out_grad, col, passes)
    mate = to_mate(summary)
    outgoing = join(meta, summary, mate, chips)
    messages = [along_y(m, k + 1) for k, m in enumerate(outgoing)]
    part = inside(moving, row, col, before, after)
    attn, grads, low_grad_part, up_part = finish(
        meta, moving, part, col, low, adapter_up, mate, messages
    )
    up_chip = add_all([up_part, to_mate(up_part)], BF16)
    up_total = add_all([up_chip] + [along_y(up_chip, k) for k in range(1, chips)], F32)
    low_grad = sum_over_head(low_grad_part)
    down_part = partial_down(inputs, low_grad)
    down_chip = add_all([down_part, to_mate(down_part)], BF16)
    down_total = add_split([down_chip] + [along_y(down_chip, k) for k in range(1, chips)], 3)
    return (attn, grads, down_total, up_total)


def solution(mesh):
    in_specs = (
        P("seq", "head"),
        P(None, "seq", "head"),
        P(None, "head", None),
        P(None, None, "head"),
        P("seq", "head"),
        P("head", "seq"),
        P("seq"),
        P(),
    )
    out_specs = (
        P("seq", "head"),
        P(None, "seq", "head"),
        P(None, "head", None),
        P(None, None, "head"),
    )
    return jax.shard_map(local, mesh=mesh, in_specs=in_specs, out_specs=out_specs, check_vma=False)
```

```python
import functools

import jax
import jax.numpy as jnp
from jax import lax
from jax.experimental import pallas as pl
from jax.experimental.pallas import tpu as pltpu
from jax.sharding import PartitionSpec as P

F32 = jnp.float32
BF16 = jnp.bfloat16
CHUNK = 256
VMEM_BYTES = 20 * 1024 * 1024
NEGATIVE = -1e30

CUM, SEG, ENTER, LEAVE, ENTER_ALL, LEAVE_ALL = 0, 4, 8, 12, 16, 20


def dot_nn(a, b):
    return lax.dot_general(a, b, (((1,), (0,)), ((), ())), preferred_element_type=F32)


def dot_nt(a, b):
    return lax.dot_general(a, b, (((1,), (1,)), ((), ())), preferred_element_type=F32)


def dot_tn(a, b):
    return lax.dot_general(a, b, (((0,), (0,)), ((), ())), preferred_element_type=F32)


def params(**more):
    return pltpu.CompilerParams(vmem_limit_bytes=VMEM_BYTES, **more)


def cost(flops, moved):
    return pl.CostEstimate(flops=int(flops), bytes_accessed=int(moved), transcendentals=0)


VMEM = pl.BlockSpec(memory_space=pltpu.VMEM)
SMEM = pl.BlockSpec(memory_space=pltpu.SMEM)


def low_kernel(x_ref, down_ref, out_ref):
    rank = down_ref.shape[1]
    x = x_ref[...]
    for c in range(3):
        out_ref[:, c * rank : (c + 1) * rank] = dot_nt(x, down_ref[c]).astype(BF16)


def partial_low(x, down):
    rows, width = x.shape
    rank = down.shape[1]
    block = min(512, rows)
    return pl.pallas_call(
        low_kernel,
        out_shape=jax.ShapeDtypeStruct((rows, 3 * rank), BF16),
        grid=(rows // block,),
        in_specs=[
            pl.BlockSpec((block, width), lambda i: (i, 0)),
            pl.BlockSpec(down.shape, lambda i: (0, 0, 0)),
        ],
        out_specs=pl.BlockSpec((block, 3 * rank), lambda i: (i, 0)),
        compiler_params=params(),
        name="partial_low",
    )(x, down)


def sum_spread_kernel(in_ref, out_ref):
    count = in_ref.shape[0]
    total = in_ref[0].astype(F32)
    for i in range(1, count):
        total = total + in_ref[i].astype(F32)
    total = total.astype(BF16)
    for i in range(count):
        out_ref[i] = total


def to_pieces(part):
    count = lax.axis_size("head")
    rows, width = part.shape
    return lax.all_to_all(part.reshape(count, rows // count, width), "head", 0, 0)


def sum_spread(pieces):
    count, rows, width = pieces.shape
    return pl.pallas_call(
        sum_spread_kernel,
        out_shape=jax.ShapeDtypeStruct(pieces.shape, BF16),
        in_specs=[VMEM],
        out_specs=VMEM,
        compiler_params=params(),
        name="sum_spread",
    )(pieces)


def decay_kernel(meta_ref, decay_ref, start_ref, row_ref, col_ref, pass_ref):
    heads, rows = decay_ref.shape
    live = meta_ref[0]
    slot = lax.broadcasted_iota(jnp.int32, (1, rows), 1)
    keep = slot < live
    decay = jnp.where(keep, decay_ref[...].astype(F32), 0.0)
    starts = jnp.where(keep, start_ref[...].astype(F32), 0.0)
    both = jnp.concatenate([decay, starts, jnp.zeros((8 - heads - 1, rows), F32)], axis=0)
    both = both.astype(BF16)
    row_i = lax.broadcasted_iota(jnp.int32, (CHUNK, CHUNK), 0)
    col_i = lax.broadcasted_iota(jnp.int32, (CHUNK, CHUNK), 1)
    upper = jnp.where(row_i <= col_i, 1.0, 0.0).astype(BF16)
    lower = jnp.where(row_i >= col_i, 1.0, 0.0).astype(BF16)
    count = rows // CHUNK
    enters, leaves, passes = [], [], []
    for c in range(count):
        span = slice(c * CHUNK, (c + 1) * CHUNK)
        piece = both[:, span]
        by_row = dot_nn(piece, upper)
        by_col = dot_nt(lower, piece)
        row_ref[:, span] = by_row
        col_ref[span, 0:8] = by_col
        cum = by_col[:, :heads]
        seg = by_col[:, heads : heads + 1]
        cum_end = by_col[CHUNK - 1 : CHUNK, :heads]
        seg_end = by_col[CHUNK - 1 : CHUNK, heads : heads + 1]
        enter = jnp.where(seg == 0.0, jnp.exp(cum), 0.0)
        leave = jnp.where(seg == seg_end, jnp.exp(cum_end - cum), 0.0)
        col_ref[span, ENTER : ENTER + heads] = enter
        col_ref[span, LEAVE : LEAVE + heads] = leave
        enters.append(enter)
        leaves.append(leave)
        passes.append(jnp.where(seg_end == 0.0, jnp.exp(cum_end), 0.0))
        end_row = by_row[:, CHUNK - 1 : CHUNK]
        passing_col = jnp.where(end_row[heads : heads + 1] == 0.0, jnp.exp(end_row[:heads]), 0.0)
        pass_ref[c * heads : (c + 1) * heads, :] = jnp.broadcast_to(passing_col, (heads, 128))
    before = jnp.ones((1, heads), F32)
    for c in range(count):
        span = slice(c * CHUNK, (c + 1) * CHUNK)
        col_ref[span, ENTER_ALL : ENTER_ALL + heads] = enters[c] * before
        before = before * passes[c]
    after = jnp.ones((1, heads), F32)
    for c in reversed(range(count)):
        span = slice(c * CHUNK, (c + 1) * CHUNK)
        col_ref[span, LEAVE_ALL : LEAVE_ALL + heads] = leaves[c] * after
        after = after * passes[c]


def decay_tables(meta, decay, starts):
    heads, rows = decay.shape
    count = rows // CHUNK
    return pl.pallas_call(
        decay_kernel,
        out_shape=(
            jax.ShapeDtypeStruct((8, rows), F32),
            jax.ShapeDtypeStruct((rows, 128), F32),
            jax.ShapeDtypeStruct((count * heads, 128), F32),
        ),
        in_specs=[SMEM, VMEM, VMEM],
        out_specs=(VMEM, VMEM, VMEM),
        compiler_params=params(),
        cost_estimate=cost(4e9, 1e6),
        name="decay_tables",
    )(meta, decay, starts.reshape(1, rows))


def project_kernel(
    meta_ref, frozen_ref, low_ref, up_ref, grad_ref, col_ref, pass_ref,
    moving_ref, before_ref, after_ref, summary_ref,
    own, returning, running,
):
    step = pl.program_id(0)
    count = pl.num_programs(0)
    rank = up_ref.shape[1]
    features = frozen_ref.shape[2]
    heads = features // 128
    live = meta_ref[0]

    @pl.when(step == 0)
    def _():
        own[...] = jnp.zeros_like(own)
        running[...] = jnp.ones_like(running)
        summary_ref[...] = jnp.zeros_like(summary_ref)

    slot = step * CHUNK + lax.broadcasted_iota(jnp.int32, (CHUNK, 1), 0)
    keep = slot < live
    low = low_ref[...]
    for c in range(3):
        lifted = dot_nn(low[:, c * rank : (c + 1) * rank], up_ref[c])
        summed = frozen_ref[c].astype(F32) + lifted
        moving_ref[c] = jnp.where(keep, summed, 0.0).astype(BF16)
    moving_ref[3] = jnp.where(keep, grad_ref[...].astype(F32), 0.0).astype(BF16)
    col = col_ref[...]
    for h in range(heads):
        span = slice(h * 128, (h + 1) * 128)
        passing = pass_ref[pl.ds(step * heads + h, 1), :]
        leave = col[:, LEAVE + h : LEAVE + h + 1]
        enter = col[:, ENTER + h : ENTER + h + 1]
        keyed = (moving_ref[1, :, span].astype(F32) * leave).astype(BF16)
        scaled = (moving_ref[0, :, span].astype(F32) * enter).astype(BF16)
        state = own[h]
        before_ref[0, h] = state.astype(BF16)
        own[h] = passing * state + dot_tn(keyed, moving_ref[2, :, span])
        returning[step, h] = dot_tn(scaled, moving_ref[3, :, span])

    @pl.when(step == count - 1)
    def _():
        chunks = returning.shape[0]
        size = heads * 128
        for h in range(heads):
            back = jnp.zeros((128, 128), F32)
            whole = jnp.ones((1, 128), F32)
            for c in reversed(range(chunks)):
                passing = pass_ref[c * heads + h : c * heads + h + 1, :]
                after_ref[c, h] = back.astype(BF16)
                back = passing * back + returning[c, h]
                whole = whole * passing
            summary_ref[h * 128 : (h + 1) * 128, :] = own[h].astype(BF16)
            summary_ref[size + h * 128 : size + (h + 1) * 128, :] = back.astype(BF16)
            first = whole.astype(BF16)
            rest = whole - first.astype(F32)
            second = rest.astype(BF16)
            third = (rest - second.astype(F32)).astype(BF16)
            tail = jnp.concatenate(
                [first.astype(F32), second.astype(F32), third.astype(F32), jnp.zeros((13, 128), F32)],
                axis=0,
            )
            base = 2 * size + 16 * h
            summary_ref[base : base + 16, :] = tail.astype(BF16)


def project(meta, frozen, low, up, grad, col, passes):
    _, rows, features = frozen.shape
    heads = features // 128
    count = rows // CHUNK
    summary_rows = 2 * features + 16 * heads
    return pl.pallas_call(
        project_kernel,
        out_shape=(
            jax.ShapeDtypeStruct((4, rows, features), BF16),
            jax.ShapeDtypeStruct((count, heads, 128, 128), BF16),
            jax.ShapeDtypeStruct((count, heads, 128, 128), BF16),
            jax.ShapeDtypeStruct((summary_rows, 128), BF16),
        ),
        grid=(count,),
        in_specs=[
            SMEM,
            pl.BlockSpec((3, CHUNK, features), lambda i: (0, i, 0)),
            pl.BlockSpec((CHUNK, low.shape[1]), lambda i: (i, 0)),
            pl.BlockSpec(up.shape, lambda i: (0, 0, 0)),
            pl.BlockSpec((CHUNK, features), lambda i: (i, 0)),
            pl.BlockSpec((CHUNK, 128), lambda i: (i, 0)),
            pl.BlockSpec(passes.shape, lambda i: (0, 0)),
        ],
        out_specs=(
            pl.BlockSpec((4, CHUNK, features), lambda i: (0, i, 0)),
            pl.BlockSpec((1, heads, 128, 128), lambda i: (i, 0, 0, 0)),
            pl.BlockSpec((count, heads, 128, 128), lambda i: (0, 0, 0, 0)),
            pl.BlockSpec((summary_rows, 128), lambda i: (0, 0)),
        ),
        scratch_shapes=[
            pltpu.VMEM((heads, 128, 128), F32),
            pltpu.VMEM((count, heads, 128, 128), F32),
            pltpu.VMEM((heads, 128), F32),
        ],
        compiler_params=params(dimension_semantics=("arbitrary",)),
        cost_estimate=cost(4e9, 10e6),
        name="project",
    )(meta, frozen, low, up, grad, col, passes)


def passing_of(ref, base):
    return (
        ref[base : base + 1, :].astype(F32)
        + ref[base + 1 : base + 2, :].astype(F32)
        + ref[base + 2 : base + 3, :].astype(F32)
    )


def join_kernel(meta_ref, own_ref, mate_ref, *out_refs):
    y = meta_ref[1]
    core = meta_ref[2]
    total = own_ref.shape[0]
    heads = (total - 0) // (2 * 128 + 16)
    size = heads * 128
    chips = len(out_refs) + 1
    second = core == 1
    for h in range(heads):
        rows = slice(h * 128, (h + 1) * 128)
        back_rows = slice(size + h * 128, size + (h + 1) * 128)
        base = 2 * size + 16 * h
        own_pass = passing_of(own_ref, base)
        mate_pass = passing_of(mate_ref, base)
        own_state = own_ref[rows, :].astype(F32)
        mate_state = mate_ref[rows, :].astype(F32)
        own_back = own_ref[back_rows, :].astype(F32)
        mate_back = mate_ref[back_rows, :].astype(F32)
        one = jnp.ones_like(own_pass)
        state = jnp.where(second, own_pass, one) * mate_state + jnp.where(second, one, mate_pass) * own_state
        back = jnp.where(second, one, own_pass) * mate_back + jnp.where(second, mate_pass, one) * own_back
        whole = own_pass * mate_pass
        first = whole.astype(BF16).astype(F32)
        rest = whole - first
        middle = rest.astype(BF16).astype(F32)
        third = (rest - middle).astype(BF16).astype(F32)
        tail = jnp.concatenate([first, middle, third, jnp.zeros((13, 128), F32)], axis=0).astype(BF16)
        for k, out_ref in enumerate(out_refs):
            later = y + (k + 1) < chips
            out_ref[rows, :] = jnp.where(later, state, back).astype(BF16)
            out_ref[size + 16 * h : size + 16 * h + 16, :] = tail


def join(meta, own, mate, chips):
    heads = own.shape[0] // (2 * 128 + 16)
    message = jax.ShapeDtypeStruct((heads * (128 + 16), 128), BF16)
    return pl.pallas_call(
        join_kernel,
        out_shape=(message,) * (chips - 1),
        in_specs=[SMEM, VMEM, VMEM],
        out_specs=(VMEM,) * (chips - 1),
        compiler_params=params(),
        name="join",
    )(meta, own, mate)


def inside_kernel(moving_ref, row_ref, col_ref, before_ref, after_ref, part_ref):
    features = moving_ref.shape[2]
    heads = features // 128
    row_i = lax.broadcasted_iota(jnp.int32, (CHUNK, CHUNK), 0)
    col_i = lax.broadcasted_iota(jnp.int32, (CHUNK, CHUNK), 1)
    col = col_ref[...]
    allowed = (row_i <= col_i) & (col[:, SEG : SEG + 1] == row_ref[SEG : SEG + 1, :])
    shut = jnp.where(allowed, 0.0, NEGATIVE)
    for h in range(heads):
        span = slice(h * 128, (h + 1) * 128)
        q = moving_ref[0, :, span]
        k = moving_ref[1, :, span]
        v = moving_ref[2, :, span]
        g = moving_ref[3, :, span]
        weights = jnp.exp((row_ref[h : h + 1, :] - col[:, h : h + 1]) + shut)
        a = (dot_nt(k, q) * weights).astype(BF16)
        b = (dot_nt(v, g) * weights).astype(BF16)
        enter = col[:, ENTER + h : ENTER + h + 1]
        leave = col[:, LEAVE + h : LEAVE + h + 1]
        before = before_ref[0, h]
        after = after_ref[0, h]
        part_ref[0, :, span] = dot_tn(b, k) + enter * dot_nt(g, before)
        part_ref[1, :, span] = dot_nn(b, q) + leave * dot_nt(v, after)
        part_ref[2, :, span] = dot_nn(a, g) + leave * dot_nn(k, after)


def inside(moving, row, col, before, after):
    _, rows, features = moving.shape
    heads = features // 128
    count = rows // CHUNK
    return pl.pallas_call(
        inside_kernel,
        out_shape=jax.ShapeDtypeStruct((3, rows, features), F32),
        grid=(count,),
        in_specs=[
            pl.BlockSpec((4, CHUNK, features), lambda i: (0, i, 0)),
            pl.BlockSpec((8, CHUNK), lambda i: (0, i)),
            pl.BlockSpec((CHUNK, 128), lambda i: (i, 0)),
            pl.BlockSpec((1, heads, 128, 128), lambda i: (i, 0, 0, 0)),
            pl.BlockSpec((1, heads, 128, 128), lambda i: (i, 0, 0, 0)),
        ],
        out_specs=pl.BlockSpec((3, CHUNK, features), lambda i: (0, i, 0)),
        compiler_params=params(dimension_semantics=("arbitrary",)),
        cost_estimate=cost(12e9, 12e6),
        name="inside",
    )(moving, row, col, before, after)


def late_kernel(
    moving_ref, row_ref, col_ref, before_ref, state_ref, low_ref, grad_ref, attn_ref, up_grad_ref, up_sum
):
    step = pl.program_id(0)
    count = pl.num_programs(0)
    features = moving_ref.shape[2]
    heads = features // 128
    rank = up_sum.shape[1]
    inverse = 1.0 / 128.0

    @pl.when(step == 0)
    def _():
        up_sum[...] = jnp.zeros_like(up_sum)

    row_i = lax.broadcasted_iota(jnp.int32, (CHUNK, CHUNK), 0)
    col_i = lax.broadcasted_iota(jnp.int32, (CHUNK, CHUNK), 1)
    col = col_ref[...]
    allowed = (row_i >= col_i) & (col[:, SEG : SEG + 1] == row_ref[SEG : SEG + 1, :])
    shut = jnp.where(allowed, 0.0, NEGATIVE)
    for h in range(heads):
        span = slice(h * 128, (h + 1) * 128)
        q = moving_ref[0, :, span]
        weights = jnp.exp((col[:, h : h + 1] - row_ref[h : h + 1, :]) + shut)
        a = (dot_nt(q, moving_ref[1, :, span]) * weights).astype(BF16)
        enter = col[:, ENTER + h : ENTER + h + 1]
        enter_all = col[:, ENTER_ALL + h : ENTER_ALL + h + 1]
        out = dot_nn(a, moving_ref[2, :, span])
        out = out + enter * dot_nn(q, before_ref[0, h]) + enter_all * dot_nn(q, state_ref[h])
        attn_ref[:, span] = (out * inverse).astype(BF16)
    low = low_ref[...]
    for c in range(3):
        up_sum[c] += dot_tn(low[:, c * rank : (c + 1) * rank], grad_ref[c])

    @pl.when(step == count - 1)
    def _():
        up_grad_ref[...] = up_sum[...].astype(BF16)


def late(moving, row, col, before, state, low, grads, up_shape):
    _, rows, features = moving.shape
    heads = features // 128
    count = rows // CHUNK
    return pl.pallas_call(
        late_kernel,
        out_shape=(
            jax.ShapeDtypeStruct((rows, features), BF16),
            jax.ShapeDtypeStruct(up_shape, BF16),
        ),
        grid=(count,),
        in_specs=[
            pl.BlockSpec((3, CHUNK, features), lambda i: (0, i, 0)),
            pl.BlockSpec((8, CHUNK), lambda i: (0, i)),
            pl.BlockSpec((CHUNK, 128), lambda i: (i, 0)),
            pl.BlockSpec((1, heads, 128, 128), lambda i: (i, 0, 0, 0)),
            pl.BlockSpec(state.shape, lambda i: (0, 0, 0)),
            pl.BlockSpec((CHUNK, low.shape[1]), lambda i: (i, 0)),
            pl.BlockSpec((3, CHUNK, features), lambda i: (0, i, 0)),
        ],
        out_specs=(
            pl.BlockSpec((CHUNK, features), lambda i: (i, 0)),
            pl.BlockSpec(up_shape, lambda i: (0, 0, 0)),
        ),
        scratch_shapes=[pltpu.VMEM(up_shape, F32)],
        compiler_params=params(dimension_semantics=("arbitrary",)),
        cost_estimate=cost(6e9, 10e6),
        name="late",
    )(moving, row, col, before, state, low, grads)


def finish_kernel(chips, meta_ref, moving_ref, part_ref, col_ref, up_ref, mate_ref, *refs):
    message_refs = refs[: chips - 1]
    grad_ref, low_grad_ref, state_in, back_in = refs[chips - 1 :]
    step = pl.program_id(0)
    features = moving_ref.shape[2]
    heads = features // 128
    size = heads * 128
    rank = up_ref.shape[1]
    inverse = 1.0 / 128.0

    @pl.when(step == 0)
    def _():
        y = meta_ref[1]
        second = meta_ref[2] == 1
        for h in range(heads):
            rows = slice(h * 128, (h + 1) * 128)
            factor = jnp.ones((1, 128), F32)
            state = jnp.zeros((128, 128), F32)
            for k in range(1, chips):
                ref = message_refs[k - 1]
                state = state + jnp.where(k <= y, factor, 0.0) * ref[rows, :].astype(F32)
                factor = factor * passing_of(ref, size + 16 * h)
            factor = jnp.ones((1, 128), F32)
            back = jnp.zeros((128, 128), F32)
            for k in reversed(range(1, chips)):
                ref = message_refs[k - 1]
                back = back + jnp.where(k > y, factor, 0.0) * ref[rows, :].astype(F32)
                factor = factor * passing_of(ref, size + 16 * h)
            mate_pass = passing_of(mate_ref, 2 * size + 16 * h)
            mate_state = mate_ref[rows, :].astype(F32)
            mate_back = mate_ref[size + h * 128 : size + (h + 1) * 128, :].astype(F32)
            state_in[h] = jnp.where(second, mate_pass * state + mate_state, state).astype(BF16)
            back_in[h] = jnp.where(second, back, mate_pass * back + mate_back).astype(BF16)

    col = col_ref[...]
    for h in range(heads):
        span = slice(h * 128, (h + 1) * 128)
        k = moving_ref[1, :, span]
        v = moving_ref[2, :, span]
        g = moving_ref[3, :, span]
        enter = col[:, ENTER_ALL + h : ENTER_ALL + h + 1]
        leave = col[:, LEAVE_ALL + h : LEAVE_ALL + h + 1]
        state = state_in[h]
        back = back_in[h]
        grad_ref[0, :, span] = ((part_ref[0, :, span] + enter * dot_nt(g, state)) * inverse).astype(BF16)
        grad_ref[1, :, span] = ((part_ref[1, :, span] + leave * dot_nt(v, back)) * inverse).astype(BF16)
        grad_ref[2, :, span] = ((part_ref[2, :, span] + leave * dot_nn(k, back)) * inverse).astype(BF16)
    for c in range(3):
        lanes = slice(c * rank, (c + 1) * rank)
        low_grad_ref[:, lanes] = dot_nt(grad_ref[c], up_ref[c]).astype(BF16)


def finish(meta, moving, part, col, up, mate, messages):
    _, rows, features = moving.shape
    heads = features // 128
    count = rows // CHUNK
    chips = len(messages) + 1
    width = up.shape[0] * up.shape[1]
    return pl.pallas_call(
        functools.partial(finish_kernel, chips),
        out_shape=(
            jax.ShapeDtypeStruct((3, rows, features), BF16),
            jax.ShapeDtypeStruct((rows, width), BF16),
            jax.ShapeDtypeStruct((heads, 128, 128), BF16),
        ),
        grid=(count,),
        in_specs=[
            SMEM,
            pl.BlockSpec((4, CHUNK, features), lambda i: (0, i, 0)),
            pl.BlockSpec((3, CHUNK, features), lambda i: (0, i, 0)),
            pl.BlockSpec((CHUNK, 128), lambda i: (i, 0)),
            pl.BlockSpec(up.shape, lambda i: (0, 0, 0)),
            pl.BlockSpec(mate.shape, lambda i: (0, 0)),
        ]
        + [pl.BlockSpec(m.shape, lambda i: (0, 0)) for m in messages],
        out_specs=(
            pl.BlockSpec((3, CHUNK, features), lambda i: (0, i, 0)),
            pl.BlockSpec((CHUNK, width), lambda i: (i, 0)),
            pl.BlockSpec((heads, 128, 128), lambda i: (0, 0, 0)),
        ),
        scratch_shapes=[pltpu.VMEM((heads, 128, 128), BF16)],
        compiler_params=params(dimension_semantics=("arbitrary",)),
        cost_estimate=cost(4e9, 14e6),
        name="finish",
    )(meta, moving, part, col, up, mate, *messages)


def down_kernel(x_ref, grad_ref, out_ref):
    out_ref[...] = dot_tn(grad_ref[...], x_ref[...]).astype(BF16)


def partial_down(x, low_grad):
    return pl.pallas_call(
        down_kernel,
        out_shape=jax.ShapeDtypeStruct((low_grad.shape[1], x.shape[1]), BF16),
        in_specs=[VMEM, VMEM],
        out_specs=VMEM,
        compiler_params=params(),
        name="partial_down",
    )(x, low_grad)


def add_kernel(*refs):
    total = refs[0][...].astype(F32)
    for ref in refs[1:-1]:
        total = total + ref[...].astype(F32)
    refs[-1][...] = total.astype(refs[-1].dtype)


def add_all(arrays, dtype):
    return pl.pallas_call(
        add_kernel,
        out_shape=jax.ShapeDtypeStruct(arrays[0].shape, dtype),
        in_specs=[VMEM] * len(arrays),
        out_specs=VMEM,
        compiler_params=params(),
        name="add_all",
    )(*arrays)


def to_mate(a):
    return lax.ppermute(a, "seq", [(i, i ^ 1) for i in range(lax.axis_size("seq"))])


def along_y(a, k):
    count = lax.axis_size("seq")
    return lax.ppermute(a, "seq", [(i, (i + 2 * k) % count) for i in range(count)])


def local(inputs, frozen, adapter_down, adapter_up, out_grad, log_decay, doc_start, lengths):
    device = lax.axis_index("seq")
    chips = lax.axis_size("seq") // 2
    rank = adapter_up.shape[1]
    meta = jnp.stack([lengths[device], device // 2, device % 2]).astype(jnp.int32)
    row, col, passes = decay_tables(meta, log_decay, doc_start)
    spread = sum_spread(to_pieces(partial_low(inputs, jnp.swapaxes(adapter_down, 1, 2))))
    low = lax.all_to_all(spread, "head", 0, 0).reshape(inputs.shape[0], 3 * rank)
    moving, before, after, summary = project(meta, frozen, low, adapter_up, out_grad, col, passes)
    mate = to_mate(summary)
    outgoing = join(meta, summary, mate, chips)
    messages = [along_y(m, k + 1) for k, m in enumerate(outgoing)]
    part = inside(moving, row, col, before, after)
    grads, low_grad_part, state = finish(meta, moving, part, col, adapter_up, mate, messages)
    attn, up_part = late(moving, row, col, before, state, low, grads, adapter_up.shape)
    pieces, up_mate = lax.optimization_barrier((to_pieces(low_grad_part), to_mate(up_part)))
    spread = sum_spread(pieces)
    up_chip = add_all([up_part, up_mate], BF16)
    low_grad, *up_others = lax.optimization_barrier(
        [lax.all_to_all(spread, "head", 0, 0)] + [along_y(up_chip, k) for k in range(1, chips)]
    )
    low_grad = low_grad.reshape(inputs.shape[0], 3 * rank)
    up_total = add_all([up_chip] + up_others, F32)
    down_part = partial_down(inputs, low_grad)
    down_chip = add_all([down_part, to_mate(down_part)], BF16)
    down_total = add_all([down_chip] + [along_y(down_chip, k) for k in range(1, chips)], F32)
    down_total = jnp.swapaxes(down_total.reshape(3, rank, inputs.shape[1]), 1, 2)
    return (attn, grads, down_total, up_total)


def solution(mesh):
    in_specs = (
        P("seq", "head"),
        P(None, "seq", "head"),
        P(None, "head", None),
        P(None, None, "head"),
        P("seq", "head"),
        P("head", "seq"),
        P("seq"),
        P(),
    )
    out_specs = (
        P("seq", "head"),
        P(None, "seq", "head"),
        P(None, "head", None),
        P(None, None, "head"),
    )
    return jax.shard_map(local, mesh=mesh, in_specs=in_specs, out_specs=out_specs, check_vma=False)
```

```python
import functools

import jax
import jax.numpy as jnp
from jax import lax
from jax.experimental import pallas as pl
from jax.experimental.pallas import tpu as pltpu
from jax.sharding import PartitionSpec as P

F32 = jnp.float32
BF16 = jnp.bfloat16
CHUNK = 256
VMEM_BYTES = 20 * 1024 * 1024
NEGATIVE = -1e30

CUM, SEG, ENTER, LEAVE, ENTER_ALL, LEAVE_ALL = 0, 4, 8, 12, 16, 20


def dot_nn(a, b):
    return lax.dot_general(a, b, (((1,), (0,)), ((), ())), preferred_element_type=F32)


def dot_nt(a, b):
    return lax.dot_general(a, b, (((1,), (1,)), ((), ())), preferred_element_type=F32)


def dot_tn(a, b):
    return lax.dot_general(a, b, (((0,), (0,)), ((), ())), preferred_element_type=F32)


def params(limit=VMEM_BYTES, **more):
    return pltpu.CompilerParams(vmem_limit_bytes=limit, **more)


def chunk_rows(c):
    return pl.ds(pl.multiple_of(c * CHUNK, CHUNK), CHUNK)


def cost(flops, moved):
    return pl.CostEstimate(flops=int(flops), bytes_accessed=int(moved), transcendentals=0)


VMEM = pl.BlockSpec(memory_space=pltpu.VMEM)
SMEM = pl.BlockSpec(memory_space=pltpu.SMEM)


def store_pieces(out_ref, value):
    half = value.shape[0] // 2
    for r in range(2):
        for l in range(2):
            out_ref[2 * r + l] = value[r * half : (r + 1) * half, l * 128 : (l + 1) * 128]


def load_pieces(ref):
    rows = [jnp.concatenate([ref[2 * r], ref[2 * r + 1]], axis=1) for r in range(2)]
    return jnp.concatenate(rows, axis=0)


def piece_shape(rows, width):
    return (rows // CHUNK * 4, width // 2, CHUNK // 2)


def piece_spec(width):
    return pl.BlockSpec((4, width // 2, CHUNK // 2), lambda i: (i, 0, 0))


def low_kernel(x_ref, down_ref, out_ref, x_held, down_held, sems):
    count = x_ref.shape[0] // CHUNK
    first = pltpu.make_async_copy(down_ref, down_held, sems.at[count])
    first.start()
    copies = []
    for c in range(count):
        rows = pl.ds(c * CHUNK, CHUNK)
        copies.append(pltpu.make_async_copy(x_ref.at[rows], x_held.at[rows], sems.at[c]))
        copies[c].start()
    first.wait()
    for c in range(count):
        copies[c].wait()
        part = dot_nt(down_held[...], x_held[c * CHUNK : (c + 1) * CHUNK, :])
        store_pieces(out_ref.at[pl.ds(4 * c, 4)], part.astype(BF16))


def partial_low(x, down):
    rows, _ = x.shape
    far = pl.BlockSpec(memory_space=pltpu.HBM)
    return pl.pallas_call(
        low_kernel,
        out_shape=jax.ShapeDtypeStruct(piece_shape(rows, down.shape[0]), BF16),
        in_specs=[far, far],
        out_specs=VMEM,
        scratch_shapes=[
            pltpu.VMEM(x.shape, BF16),
            pltpu.VMEM(down.shape, BF16),
            pltpu.SemaphoreType.DMA((rows // CHUNK + 1,)),
        ],
        compiler_params=params(),
        name="partial_low",
    )(*(pltpu.with_memory_space_constraint(a, pltpu.HBM) for a in (x, down)))


def sum_spread_kernel(in_ref, out_ref):
    count = in_ref.shape[0]
    total = in_ref[0].astype(F32)
    for i in range(1, count):
        total = total + in_ref[i].astype(F32)
    total = total.astype(BF16)
    for i in range(count):
        out_ref[i] = total


def exchange(pieces):
    return lax.all_to_all(pieces, "head", 0, 0)


def sum_spread(pieces):
    count, rows, width = pieces.shape
    return pl.pallas_call(
        sum_spread_kernel,
        out_shape=jax.ShapeDtypeStruct(pieces.shape, BF16),
        in_specs=[VMEM],
        out_specs=VMEM,
        compiler_params=params(),
        name="sum_spread",
    )(pieces)


def decay_kernel(meta_ref, decay_ref, start_ref, row_ref, col_ref, pass_ref):
    heads, rows = decay_ref.shape
    live = meta_ref[0]
    slot = lax.broadcasted_iota(jnp.int32, (1, rows), 1)
    keep = slot < live
    decay = jnp.where(keep, decay_ref[...].astype(F32), 0.0)
    starts = jnp.where(keep, start_ref[...].astype(F32), 0.0)
    both = jnp.concatenate([decay, starts, jnp.zeros((8 - heads - 1, rows), F32)], axis=0)
    both = both.astype(BF16)
    row_i = lax.broadcasted_iota(jnp.int32, (CHUNK, CHUNK), 0)
    col_i = lax.broadcasted_iota(jnp.int32, (CHUNK, CHUNK), 1)
    upper = jnp.where(row_i <= col_i, 1.0, 0.0).astype(BF16)
    lower = jnp.where(row_i >= col_i, 1.0, 0.0).astype(BF16)
    count = rows // CHUNK
    enters, leaves, passes = [], [], []
    for c in range(count):
        span = slice(c * CHUNK, (c + 1) * CHUNK)
        piece = both[:, span]
        by_row = dot_nn(piece, upper)
        by_col = dot_nt(lower, piece)
        here = keep[:, span]
        here_col = c * CHUNK + lax.broadcasted_iota(jnp.int32, (CHUNK, 1), 0) < live
        head_row = lax.broadcasted_iota(jnp.int32, (8, CHUNK), 0)
        head_lane = lax.broadcasted_iota(jnp.int32, (CHUNK, 8), 1)
        row_ref[:, span] = jnp.where(here | (head_row != heads), by_row, -1.0)
        col_ref[span, 0:8] = jnp.where(here_col | (head_lane != heads), by_col, -2.0)
        cum = by_col[:, :heads]
        seg = by_col[:, heads : heads + 1]
        cum_end = by_col[CHUNK - 1 : CHUNK, :heads]
        seg_end = by_col[CHUNK - 1 : CHUNK, heads : heads + 1]
        enter = jnp.where((seg == 0.0) & here_col, jnp.exp(cum), 0.0)
        leave = jnp.where((seg == seg_end) & here_col, jnp.exp(cum_end - cum), 0.0)
        col_ref[span, ENTER : ENTER + heads] = enter
        col_ref[span, LEAVE : LEAVE + heads] = leave
        enters.append(enter)
        leaves.append(leave)
        passes.append(jnp.where(seg_end == 0.0, jnp.exp(cum_end), 0.0))
        end_row = by_row[:, CHUNK - 1 : CHUNK]
        passing_col = jnp.where(end_row[heads : heads + 1] == 0.0, jnp.exp(end_row[:heads]), 0.0)
        pass_ref[c * heads : (c + 1) * heads, :] = jnp.broadcast_to(passing_col, (heads, 128))
    before = jnp.ones((1, heads), F32)
    for c in range(count):
        span = slice(c * CHUNK, (c + 1) * CHUNK)
        col_ref[span, ENTER_ALL : ENTER_ALL + heads] = enters[c] * before
        before = before * passes[c]
    after = jnp.ones((1, heads), F32)
    for c in reversed(range(count)):
        span = slice(c * CHUNK, (c + 1) * CHUNK)
        col_ref[span, LEAVE_ALL : LEAVE_ALL + heads] = leaves[c] * after
        after = after * passes[c]


def decay_tables(meta, decay, starts):
    heads, rows = decay.shape
    count = rows // CHUNK
    return pl.pallas_call(
        decay_kernel,
        out_shape=(
            jax.ShapeDtypeStruct((8, rows), F32),
            jax.ShapeDtypeStruct((rows, 128), F32),
            jax.ShapeDtypeStruct((count * heads, 128), F32),
        ),
        in_specs=[SMEM, VMEM, VMEM],
        out_specs=(VMEM, VMEM, VMEM),
        compiler_params=params(),
        cost_estimate=cost(4e9, 1e6),
        name="decay_tables",
    )(meta, decay, starts.reshape(1, rows))


def project_kernel(
    frozen_ref, low_ref, up_ref, grad_ref, col_ref, pass_ref,
    moving_ref, before_ref, after_ref, summary_ref, returning, held, sems,
):
    chunks = returning.shape[0]
    rank = up_ref.shape[1]
    features = frozen_ref.shape[2]
    heads = features // 128
    size = heads * 128
    copies = []
    for c in range(chunks):
        rows = pl.ds(c * CHUNK, CHUNK)
        copies.append(pltpu.make_async_copy(frozen_ref.at[:, rows], held.at[:, rows], sems.at[c]))
        copies[c].start()
    states = [jnp.zeros((128, 128), F32)] * heads
    for c in range(chunks):
        rows = pl.ds(c * CHUNK, CHUNK)
        low = load_pieces(low_ref.at[pl.ds(4 * c, 4)])
        copies[c].wait()
        for i in range(3):
            lifted = dot_tn(low[i * rank : (i + 1) * rank, :], up_ref[i])
            moving_ref[i, rows, :] = (held[i, rows, :].astype(F32) + lifted).astype(BF16)
        col = col_ref[rows, :]
        for h in range(heads):
            span = slice(h * 128, (h + 1) * 128)
            passing = pass_ref[c * heads + h : c * heads + h + 1, :]
            leave = col[:, LEAVE + h : LEAVE + h + 1]
            enter = col[:, ENTER + h : ENTER + h + 1]
            keyed = (moving_ref[1, rows, span].astype(F32) * leave).astype(BF16)
            scaled = (moving_ref[0, rows, span].astype(F32) * enter).astype(BF16)
            before_ref[c, h] = states[h].astype(BF16)
            states[h] = passing * states[h] + dot_tn(keyed, moving_ref[2, rows, span])
            returning[c, h] = dot_tn(scaled, grad_ref[rows, span])
    for h in range(heads):
        back = jnp.zeros((128, 128), F32)
        whole = jnp.ones((1, 128), F32)
        for c in reversed(range(chunks)):
            passing = pass_ref[c * heads + h : c * heads + h + 1, :]
            after_ref[c, h] = back.astype(BF16)
            back = passing * back + returning[c, h]
            whole = whole * passing
        summary_ref[h * 128 : (h + 1) * 128, :] = states[h].astype(BF16)
        summary_ref[size + h * 128 : size + (h + 1) * 128, :] = back.astype(BF16)
        summary_ref[2 * size + 16 * h : 2 * size + 16 * h + 16, :] = passing_rows(whole)


def passing_rows(row):
    first = row.astype(BF16).astype(F32)
    rest = row - first
    second = rest.astype(BF16).astype(F32)
    third = (rest - second).astype(BF16).astype(F32)
    return jnp.concatenate([first, second, third, jnp.zeros((13, 128), F32)], axis=0).astype(BF16)


def project(frozen, low, up, grad, col, passes):
    _, rows, features = frozen.shape
    heads = features // 128
    count = rows // CHUNK
    summary_rows = 2 * features + 16 * heads
    states = jax.ShapeDtypeStruct((count, heads, 128, 128), BF16)
    return pl.pallas_call(
        project_kernel,
        out_shape=(
            jax.ShapeDtypeStruct((3, rows, features), BF16),
            states,
            states,
            jax.ShapeDtypeStruct((summary_rows, 128), BF16),
        ),
        in_specs=[pl.BlockSpec(memory_space=pltpu.HBM)] + [VMEM] * 5,
        out_specs=(VMEM,) * 4,
        scratch_shapes=[
            pltpu.VMEM(states.shape, F32),
            pltpu.VMEM(frozen.shape, BF16),
            pltpu.SemaphoreType.DMA((count,)),
        ],
        compiler_params=params(),
        cost_estimate=cost(4e9, 10e6),
        name="project",
    )(pltpu.with_memory_space_constraint(frozen, pltpu.HBM), low, up, grad, col, passes)


def passing_of(ref, base):
    return (
        ref[base : base + 1, :].astype(F32)
        + ref[base + 1 : base + 2, :].astype(F32)
        + ref[base + 2 : base + 3, :].astype(F32)
    )


def join_kernel(meta_ref, own_ref, mate_ref, *out_refs):
    y = meta_ref[1]
    core = meta_ref[2]
    total = own_ref.shape[0]
    heads = total // (2 * 128 + 16)
    size = heads * 128
    chips = len(out_refs) + 1
    second = core == 1
    for h in range(heads):
        rows = slice(h * 128, (h + 1) * 128)
        back_rows = slice(size + h * 128, size + (h + 1) * 128)
        base = 2 * size + 16 * h
        own_pass = passing_of(own_ref, base)
        mate_pass = passing_of(mate_ref, base)
        own_state = own_ref[rows, :].astype(F32)
        mate_state = mate_ref[rows, :].astype(F32)
        own_back = own_ref[back_rows, :].astype(F32)
        mate_back = mate_ref[back_rows, :].astype(F32)
        one = jnp.ones_like(own_pass)
        state = jnp.where(second, own_pass, one) * mate_state + jnp.where(second, one, mate_pass) * own_state
        back = jnp.where(second, one, own_pass) * mate_back + jnp.where(second, mate_pass, one) * own_back
        tail = passing_rows(own_pass * mate_pass)
        for k, out_ref in enumerate(out_refs):
            later = y + (k + 1) < chips
            out_ref[rows, :] = jnp.where(later, state, back).astype(BF16)
            out_ref[size + 16 * h : size + 16 * h + 16, :] = tail


def join(meta, own, mate, chips):
    heads = own.shape[0] // (2 * 128 + 16)
    message = jax.ShapeDtypeStruct((heads * (128 + 16), 128), BF16)
    return pl.pallas_call(
        join_kernel,
        out_shape=(message,) * (chips - 1),
        in_specs=[SMEM, VMEM, VMEM],
        out_specs=(VMEM,) * (chips - 1),
        compiler_params=params(),
        name="join",
    )(meta, own, mate)


def inside_kernel(moving_ref, grad_ref, row_ref, col_ref, before_ref, after_ref, part_ref):
    features = moving_ref.shape[2]
    heads = features // 128
    row_i = lax.broadcasted_iota(jnp.int32, (CHUNK, CHUNK), 0)
    col_i = lax.broadcasted_iota(jnp.int32, (CHUNK, CHUNK), 1)

    @pl.loop(0, moving_ref.shape[1] // CHUNK)
    def _(c):
        rows = chunk_rows(c)
        col = col_ref[rows, :]
        row = row_ref[:, rows]
        allowed = (row_i <= col_i) & (col[:, SEG : SEG + 1] == row[SEG : SEG + 1, :])
        shut = jnp.where(allowed, 0.0, NEGATIVE)
        for h in range(heads):
            span = slice(h * 128, (h + 1) * 128)
            q = moving_ref[0, rows, span]
            k = moving_ref[1, rows, span]
            v = moving_ref[2, rows, span]
            g = grad_ref[rows, span]
            weights = jnp.exp((row[h : h + 1, :] - col[:, h : h + 1]) + shut)
            a = (dot_nt(k, q) * weights).astype(BF16)
            b = (dot_nt(v, g) * weights).astype(BF16)
            enter = col[:, ENTER + h : ENTER + h + 1]
            leave = col[:, LEAVE + h : LEAVE + h + 1]
            before = before_ref[c, h]
            after = after_ref[c, h]
            part_ref[0, rows, span] = dot_tn(b, k) + enter * dot_nt(g, before)
            part_ref[1, rows, span] = dot_nn(b, q) + leave * dot_nt(v, after)
            part_ref[2, rows, span] = dot_nn(a, g) + leave * dot_nn(k, after)


def inside(moving, grad, row, col, before, after):
    return pl.pallas_call(
        inside_kernel,
        out_shape=jax.ShapeDtypeStruct(moving.shape, F32),
        in_specs=[VMEM] * 6,
        out_specs=VMEM,
        compiler_params=params(),
        cost_estimate=cost(12e9, 12e6),
        name="inside",
    )(moving, grad, row, col, before, after)


def late_kernel(moving_ref, row_ref, col_ref, before_ref, state_ref, attn_ref):
    features = moving_ref.shape[2]
    heads = features // 128
    inverse = 1.0 / 128.0
    row_i = lax.broadcasted_iota(jnp.int32, (CHUNK, CHUNK), 0)
    col_i = lax.broadcasted_iota(jnp.int32, (CHUNK, CHUNK), 1)
    col = col_ref[...]
    allowed = (row_i >= col_i) & (col[:, SEG : SEG + 1] == row_ref[SEG : SEG + 1, :])
    shut = jnp.where(allowed, 0.0, NEGATIVE)
    for h in range(heads):
        span = slice(h * 128, (h + 1) * 128)
        q = moving_ref[0, :, span]
        weights = jnp.exp((col[:, h : h + 1] - row_ref[h : h + 1, :]) + shut)
        a = (dot_nt(q, moving_ref[1, :, span]) * weights).astype(BF16)
        enter = col[:, ENTER + h : ENTER + h + 1]
        enter_all = col[:, ENTER_ALL + h : ENTER_ALL + h + 1]
        out = dot_nn(a, moving_ref[2, :, span])
        out = out + enter * dot_nn(q, before_ref[0, h]) + enter_all * dot_nn(q, state_ref[h])
        attn_ref[:, span] = (out * inverse).astype(BF16)


def late(moving, row, col, before, state):
    _, rows, features = moving.shape
    heads = features // 128
    count = rows // CHUNK
    return pl.pallas_call(
        late_kernel,
        out_shape=jax.ShapeDtypeStruct((rows, features), BF16),
        grid=(count,),
        in_specs=[
            pl.BlockSpec((3, CHUNK, features), lambda i: (0, i, 0)),
            pl.BlockSpec((8, CHUNK), lambda i: (0, i)),
            pl.BlockSpec((CHUNK, 128), lambda i: (i, 0)),
            pl.BlockSpec((1, heads, 128, 128), lambda i: (i, 0, 0, 0)),
            pl.BlockSpec(state.shape, lambda i: (0, 0, 0)),
        ],
        out_specs=pl.BlockSpec((CHUNK, features), lambda i: (i, 0)),
        compiler_params=params(dimension_semantics=("arbitrary",)),
        cost_estimate=cost(6e9, 6e6),
        name="late",
    )(moving, row, col, before, state)


def store_halves(core, total, keep_ref, send_ref):
    half = total.shape[0] // 2
    keep_ref[...] = total[pl.ds(pl.multiple_of(core * half, 16), half), :].astype(BF16)
    send_ref[...] = total[pl.ds(pl.multiple_of((1 - core) * half, 16), half), :].astype(BF16)


def up_kernel(meta_ref, low_ref, grad_ref, keep_ref, send_ref, total):
    step = pl.program_id(0)
    rank = total.shape[0] // 3

    @pl.when(step == 0)
    def _():
        total[...] = jnp.zeros_like(total)

    low = load_pieces(low_ref)
    for c in range(3):
        rows = slice(c * rank, (c + 1) * rank)
        total[rows, :] += dot_nn(low[rows, :], grad_ref[c])

    @pl.when(step == pl.num_programs(0) - 1)
    def _():
        store_halves(meta_ref[2], total, keep_ref, send_ref)


def partial_up(meta, low, grads):
    _, rows, features = grads.shape
    width = 2 * low.shape[1]
    half = jax.ShapeDtypeStruct((width // 2, features), BF16)
    return pl.pallas_call(
        up_kernel,
        out_shape=(half, half),
        grid=(rows // CHUNK,),
        in_specs=[
            SMEM,
            piece_spec(width),
            pl.BlockSpec((3, CHUNK, features), lambda i: (0, i, 0)),
        ],
        out_specs=(pl.BlockSpec(half.shape, lambda i: (0, 0)),) * 2,
        scratch_shapes=[pltpu.VMEM((width, features), F32)],
        compiler_params=params(dimension_semantics=("arbitrary",)),
        cost_estimate=cost(2e9, 4e6),
        name="partial_up",
    )(meta, low, grads)


def finish_kernel(chips, meta_ref, moving_ref, g_ref, part_ref, col_ref, up_ref, mate_ref, *refs):
    message_refs = refs[: chips - 1]
    out_ref, low_grad_ref, state_in, back_in, grad_ref, sems = refs[chips - 1 :]
    features = moving_ref.shape[2]
    heads = features // 128
    size = heads * 128
    count = moving_ref.shape[1] // CHUNK
    inverse = 1.0 / 128.0
    y = meta_ref[1]
    second = meta_ref[2] == 1
    for h in range(heads):
        rows = slice(h * 128, (h + 1) * 128)
        factor = jnp.ones((1, 128), F32)
        state = jnp.zeros((128, 128), F32)
        for k in range(1, chips):
            ref = message_refs[k - 1]
            state = state + jnp.where(k <= y, factor, 0.0) * ref[rows, :].astype(F32)
            factor = factor * passing_of(ref, size + 16 * h)
        factor = jnp.ones((1, 128), F32)
        back = jnp.zeros((128, 128), F32)
        for k in reversed(range(1, chips)):
            ref = message_refs[k - 1]
            back = back + jnp.where(k > y, factor, 0.0) * ref[rows, :].astype(F32)
            factor = factor * passing_of(ref, size + 16 * h)
        mate_pass = passing_of(mate_ref, 2 * size + 16 * h)
        mate_state = mate_ref[rows, :].astype(F32)
        mate_back = mate_ref[size + h * 128 : size + (h + 1) * 128, :].astype(F32)
        state_in[h] = jnp.where(second, mate_pass * state + mate_state, state).astype(BF16)
        back_in[h] = jnp.where(second, back, mate_pass * back + mate_back).astype(BF16)
    copies = []
    for c in range(count):
        rows = pl.ds(c * CHUNK, CHUNK)
        col = col_ref[rows, :]
        for h in range(heads):
            span = slice(h * 128, (h + 1) * 128)
            k = moving_ref[1, rows, span]
            v = moving_ref[2, rows, span]
            g = g_ref[rows, span]
            enter = col[:, ENTER_ALL + h : ENTER_ALL + h + 1]
            leave = col[:, LEAVE_ALL + h : LEAVE_ALL + h + 1]
            state = state_in[h]
            back = back_in[h]
            query = part_ref[0, rows, span] + enter * dot_nt(g, state)
            key = part_ref[1, rows, span] + leave * dot_nt(v, back)
            value = part_ref[2, rows, span] + leave * dot_nn(k, back)
            for i, result in enumerate((query, key, value)):
                grad_ref[i, rows, span] = (result * inverse).astype(BF16)
        copies.append(pltpu.make_async_copy(grad_ref.at[:, rows], out_ref.at[:, rows], sems.at[c]))
        copies[c].start()
        low_grad = [dot_nt(up_ref[i], grad_ref[i, rows, :]).astype(BF16) for i in range(3)]
        store_pieces(low_grad_ref.at[pl.ds(4 * c, 4)], jnp.concatenate(low_grad, axis=0))
    for copy in copies:
        copy.wait()


def finish(meta, moving, grad, part, col, up, mate, messages):
    _, rows, features = moving.shape
    heads = features // 128
    chips = len(messages) + 1
    width = up.shape[0] * up.shape[1]
    return pl.pallas_call(
        functools.partial(finish_kernel, chips),
        out_shape=(
            jax.ShapeDtypeStruct(moving.shape, BF16),
            jax.ShapeDtypeStruct(piece_shape(rows, width), BF16),
            jax.ShapeDtypeStruct((heads, 128, 128), BF16),
        ),
        in_specs=[SMEM] + [VMEM] * (6 + len(messages)),
        out_specs=(pl.BlockSpec(memory_space=pltpu.HBM), VMEM, VMEM),
        scratch_shapes=[
            pltpu.VMEM((heads, 128, 128), BF16),
            pltpu.VMEM(moving.shape, BF16),
            pltpu.SemaphoreType.DMA((rows // CHUNK,)),
        ],
        compiler_params=params(),
        cost_estimate=cost(4e9, 14e6),
        name="finish",
    )(meta, moving, grad, part, col, up, mate, *messages)


def down_kernel(meta_ref, x_ref, grad_ref, keep_ref, send_ref, total):
    value = jnp.zeros(total.shape, F32)
    for c in range(x_ref.shape[0] // CHUNK):
        low_grad = load_pieces(grad_ref.at[pl.ds(4 * c, 4)])
        value = value + dot_nn(low_grad, x_ref[c * CHUNK : (c + 1) * CHUNK, :])
    total[...] = value
    store_halves(meta_ref[2], total, keep_ref, send_ref)


def partial_down(meta, x, low_grad):
    width = 2 * low_grad.shape[1]
    half = jax.ShapeDtypeStruct((width // 2, x.shape[1]), BF16)
    return pl.pallas_call(
        down_kernel,
        out_shape=(half, half),
        in_specs=[SMEM, VMEM, VMEM],
        out_specs=(VMEM, VMEM),
        scratch_shapes=[pltpu.VMEM((width, x.shape[1]), F32)],
        compiler_params=params(),
        name="partial_down",
    )(meta, x, low_grad)


def halves_kernel(meta_ref, own_ref, mate_ref, out_ref):
    core = meta_ref[2]
    half = own_ref.shape[0]
    out_ref[pl.ds(pl.multiple_of(core * half, 8), half), :] = own_ref[...]
    out_ref[pl.ds(pl.multiple_of((1 - core) * half, 8), half), :] = mate_ref[...]


def join_halves(meta, own, mate):
    return pl.pallas_call(
        halves_kernel,
        out_shape=jax.ShapeDtypeStruct((2 * own.shape[0], own.shape[1]), F32),
        in_specs=[SMEM, VMEM, VMEM],
        out_specs=VMEM,
        compiler_params=params(),
        name="join_halves",
    )(meta, own, mate)


def add_kernel(*refs):
    total = refs[0][...].astype(F32)
    for ref in refs[1:-1]:
        total = total + ref[...].astype(F32)
    refs[-1][...] = total.astype(refs[-1].dtype)


def add_all(arrays, dtype):
    return pl.pallas_call(
        add_kernel,
        out_shape=jax.ShapeDtypeStruct(arrays[0].shape, dtype),
        in_specs=[VMEM] * len(arrays),
        out_specs=VMEM,
        compiler_params=params(),
        name="add_all",
    )(*arrays)


def to_mate(a):
    return lax.ppermute(a, "seq", [(i, i ^ 1) for i in range(lax.axis_size("seq"))])


def along_y(a, k):
    count = lax.axis_size("seq")
    return lax.ppermute(a, "seq", [(i, (i + 2 * k) % count) for i in range(count)])


def local(inputs, frozen, adapter_down, adapter_up, out_grad, log_decay, doc_start, lengths):
    device = lax.axis_index("seq")
    chips = lax.axis_size("seq") // 2
    rank = adapter_up.shape[1]
    meta = jnp.stack([lengths[device], device // 2, device % 2]).astype(jnp.int32)
    down = jnp.swapaxes(adapter_down, 1, 2).reshape(3 * rank, inputs.shape[1])
    row, col, passes = decay_tables(meta, log_decay, doc_start)
    low = exchange(sum_spread(exchange(partial_low(inputs, down))))
    moving, before, after, summary = project(frozen, low, adapter_up, out_grad, col, passes)
    mate = to_mate(summary)
    outgoing = join(meta, summary, mate, chips)
    messages = [along_y(m, k + 1) for k, m in enumerate(outgoing)]
    part = inside(moving, out_grad, row, col, before, after)
    grads, low_grad_part, state = finish(meta, moving, out_grad, part, col, adapter_up, mate, messages)
    up_keep, up_send = partial_up(meta, low, grads)
    attn = late(moving, row, col, before, state)
    up_chip = add_all([up_keep, to_mate(up_send)], BF16)
    pieces, up_chip, attn = lax.optimization_barrier((exchange(low_grad_part), up_chip, attn))
    up_parts = [up_chip] + [along_y(up_chip, k) for k in range(1, chips)]
    low_grad, *up_parts = lax.optimization_barrier([exchange(sum_spread(pieces))] + up_parts)
    down_keep, down_send = partial_down(meta, inputs, low_grad)
    down_chip = add_all([down_keep, to_mate(down_send)], BF16)
    down_chip, *up_parts = lax.optimization_barrier([down_chip] + up_parts)
    down_parts = [down_chip] + [along_y(down_chip, k) for k in range(1, chips)]
    up_half = add_all(up_parts, F32)
    up_total = join_halves(meta, up_half, to_mate(up_half))
    up_total, *down_parts = lax.optimization_barrier([up_total] + down_parts)
    down_half = add_all(down_parts, F32)
    down_total = join_halves(meta, down_half, to_mate(down_half))
    down_total = jnp.swapaxes(down_total.reshape(3, rank, inputs.shape[1]), 1, 2)
    return (attn, grads, down_total, up_total.reshape(adapter_up.shape))


def solution(mesh):
    in_specs = (
        P("seq", "head"),
        P(None, "seq", "head"),
        P(None, "head", None),
        P(None, None, "head"),
        P("seq", "head"),
        P("head", "seq"),
        P("seq"),
        P(),
    )
    out_specs = (
        P("seq", "head"),
        P(None, "seq", "head"),
        P(None, "head", None),
        P(None, None, "head"),
    )
    return jax.shard_map(local, mesh=mesh, in_specs=in_specs, out_specs=out_specs, check_vma=False)
```

```python
import functools

import jax
import jax.numpy as jnp
from jax import lax
from jax.experimental import pallas as pl
from jax.experimental.pallas import tpu as pltpu
from jax.sharding import PartitionSpec as P

F32 = jnp.float32
BF16 = jnp.bfloat16
CHUNK = 128
BLOCK = 256
VMEM_BYTES = 20 * 1024 * 1024
NEGATIVE = -1e30

CUM, SEG, ENTER, LEAVE, ENTER_ALL, LEAVE_ALL = 0, 4, 8, 12, 16, 20


def dot_nn(a, b):
    return lax.dot_general(a, b, (((1,), (0,)), ((), ())), preferred_element_type=F32)


def dot_nt(a, b):
    return lax.dot_general(a, b, (((1,), (1,)), ((), ())), preferred_element_type=F32)


def dot_tn(a, b):
    return lax.dot_general(a, b, (((0,), (0,)), ((), ())), preferred_element_type=F32)


def params(limit=VMEM_BYTES, **more):
    return pltpu.CompilerParams(vmem_limit_bytes=limit, **more)


def chunk_rows(c):
    return pl.ds(pl.multiple_of(c * CHUNK, CHUNK), CHUNK)


def diagonal(a, b):
    zero = jnp.zeros_like(a)
    return jnp.concatenate(
        [jnp.concatenate([a, zero], axis=1), jnp.concatenate([zero, b], axis=1)], axis=0
    )


def diagonal_of(pair):
    return diagonal(pair[:, :128], pair[:, 128:])


def widen(table, lane):
    shape = (table.shape[0], 128)
    return jnp.concatenate(
        [jnp.broadcast_to(table[:, i : i + 1], shape) for i in (lane, lane + 1)], axis=1
    )


def cost(flops, moved):
    return pl.CostEstimate(flops=int(flops), bytes_accessed=int(moved), transcendentals=0)


VMEM = pl.BlockSpec(memory_space=pltpu.VMEM)
SMEM = pl.BlockSpec(memory_space=pltpu.SMEM)


def store_pieces(out_ref, value):
    half = value.shape[0] // 2
    for r in range(2):
        for l in range(2):
            out_ref[2 * r + l] = value[r * half : (r + 1) * half, l * 128 : (l + 1) * 128]


def load_pieces(ref):
    rows = [jnp.concatenate([ref[2 * r], ref[2 * r + 1]], axis=1) for r in range(2)]
    return jnp.concatenate(rows, axis=0)


def piece_shape(rows, width):
    return (rows // BLOCK * 4, width // 2, BLOCK // 2)


def piece_spec(width):
    return pl.BlockSpec((4, width // 2, BLOCK // 2), lambda i: (i, 0, 0))


def low_kernel(x_ref, down_ref, out_ref, x_held, down_held, sems):
    count = x_ref.shape[0] // BLOCK
    first = pltpu.make_async_copy(down_ref, down_held, sems.at[count])
    first.start()
    copies = []
    for c in range(count):
        rows = pl.ds(c * BLOCK, BLOCK)
        copies.append(pltpu.make_async_copy(x_ref.at[rows], x_held.at[rows], sems.at[c]))
        copies[c].start()
    first.wait()
    for c in range(count):
        copies[c].wait()
        part = dot_nt(down_held[...], x_held[c * BLOCK : (c + 1) * BLOCK, :])
        store_pieces(out_ref.at[pl.ds(4 * c, 4)], part.astype(BF16))


def partial_low(x, down):
    rows, _ = x.shape
    far = pl.BlockSpec(memory_space=pltpu.HBM)
    return pl.pallas_call(
        low_kernel,
        out_shape=jax.ShapeDtypeStruct(piece_shape(rows, down.shape[0]), BF16),
        in_specs=[far, far],
        out_specs=VMEM,
        scratch_shapes=[
            pltpu.VMEM(x.shape, BF16),
            pltpu.VMEM(down.shape, BF16),
            pltpu.SemaphoreType.DMA((rows // BLOCK + 1,)),
        ],
        compiler_params=params(),
        name="partial_low",
    )(*(pltpu.with_memory_space_constraint(a, pltpu.HBM) for a in (x, down)))


def sum_spread_kernel(in_ref, out_ref):
    count = in_ref.shape[0]
    total = in_ref[0].astype(F32)
    for i in range(1, count):
        total = total + in_ref[i].astype(F32)
    total = total.astype(BF16)
    for i in range(count):
        out_ref[i] = total


def exchange(pieces):
    return lax.all_to_all(pieces, ("z", "x"), 0, 0)


def sum_spread(pieces):
    count, rows, width = pieces.shape
    return pl.pallas_call(
        sum_spread_kernel,
        out_shape=jax.ShapeDtypeStruct(pieces.shape, BF16),
        in_specs=[VMEM],
        out_specs=VMEM,
        compiler_params=params(),
        name="sum_spread",
    )(pieces)


def decay_kernel(meta_ref, decay_ref, start_ref, row_ref, col_ref, pass_ref):
    heads, rows = decay_ref.shape
    live = meta_ref[0]
    slot = lax.broadcasted_iota(jnp.int32, (1, rows), 1)
    keep = slot < live
    decay = jnp.where(keep, decay_ref[...].astype(F32), 0.0)
    starts = jnp.where(keep, start_ref[...].astype(F32), 0.0)
    both = jnp.concatenate([decay, starts, jnp.zeros((8 - heads - 1, rows), F32)], axis=0)
    both = both.astype(BF16)
    row_i = lax.broadcasted_iota(jnp.int32, (CHUNK, CHUNK), 0)
    col_i = lax.broadcasted_iota(jnp.int32, (CHUNK, CHUNK), 1)
    upper = jnp.where(row_i <= col_i, 1.0, 0.0).astype(BF16)
    lower = jnp.where(row_i >= col_i, 1.0, 0.0).astype(BF16)
    count = rows // CHUNK
    enters, leaves, passes = [], [], []
    prefix = jnp.ones((heads, 128), F32)
    for c in range(count):
        span = slice(c * CHUNK, (c + 1) * CHUNK)
        piece = both[:, span]
        by_row = dot_nn(piece, upper)
        by_col = dot_nt(lower, piece)
        here = keep[:, span]
        here_col = c * CHUNK + lax.broadcasted_iota(jnp.int32, (CHUNK, 1), 0) < live
        head_row = lax.broadcasted_iota(jnp.int32, (8, CHUNK), 0)
        head_lane = lax.broadcasted_iota(jnp.int32, (CHUNK, 8), 1)
        row_ref[:, span] = jnp.where(here | (head_row != heads), by_row, -1.0)
        col_ref[span, 0:8] = jnp.where(here_col | (head_lane != heads), by_col, -2.0)
        cum = by_col[:, :heads]
        seg = by_col[:, heads : heads + 1]
        cum_end = by_col[CHUNK - 1 : CHUNK, :heads]
        seg_end = by_col[CHUNK - 1 : CHUNK, heads : heads + 1]
        enter = jnp.where((seg == 0.0) & here_col, jnp.exp(cum), 0.0)
        leave = jnp.where((seg == seg_end) & here_col, jnp.exp(cum_end - cum), 0.0)
        col_ref[span, ENTER : ENTER + heads] = enter
        col_ref[span, LEAVE : LEAVE + heads] = leave
        enters.append(enter)
        leaves.append(leave)
        passes.append(jnp.where(seg_end == 0.0, jnp.exp(cum_end), 0.0))
        end_row = by_row[:, CHUNK - 1 : CHUNK]
        passing_col = jnp.where(end_row[heads : heads + 1] == 0.0, jnp.exp(end_row[:heads]), 0.0)
        passing_rows_here = jnp.broadcast_to(passing_col, (heads, 128))
        pass_ref[c * heads : (c + 1) * heads, :] = passing_rows_here
        first = (count + c) * heads
        pass_ref[first : first + heads, :] = prefix
        prefix = prefix * passing_rows_here
    before = jnp.ones((1, heads), F32)
    for c in range(count):
        span = slice(c * CHUNK, (c + 1) * CHUNK)
        col_ref[span, ENTER_ALL : ENTER_ALL + heads] = enters[c] * before
        before = before * passes[c]
    after = jnp.ones((1, heads), F32)
    for c in reversed(range(count)):
        span = slice(c * CHUNK, (c + 1) * CHUNK)
        col_ref[span, LEAVE_ALL : LEAVE_ALL + heads] = leaves[c] * after
        after = after * passes[c]


def decay_tables(meta, decay, starts):
    heads, rows = decay.shape
    count = rows // CHUNK
    return pl.pallas_call(
        decay_kernel,
        out_shape=(
            jax.ShapeDtypeStruct((8, rows), F32),
            jax.ShapeDtypeStruct((rows, 128), F32),
            jax.ShapeDtypeStruct((2 * count * heads, 128), F32),
        ),
        in_specs=[SMEM, VMEM, VMEM],
        out_specs=(VMEM, VMEM, VMEM),
        compiler_params=params(),
        cost_estimate=cost(4e9, 1e6),
        name="decay_tables",
    )(meta, decay, starts.reshape(1, rows))


def project_kernel(
    frozen_ref, low_ref, up_ref, grad_ref, col_ref, pass_ref,
    moving_ref, before_ref, after_ref, summary_ref, returning, held, sems,
):
    chunks = returning.shape[0]
    rank = up_ref.shape[1]
    features = frozen_ref.shape[2]
    heads = features // 128
    size = heads * 128
    copies = []
    for n in range(frozen_ref.shape[1] // BLOCK):
        rows = pl.ds(n * BLOCK, BLOCK)
        copies.append(pltpu.make_async_copy(frozen_ref.at[:, rows], held.at[:, rows], sems.at[n]))
        copies[n].start()
    states = [jnp.zeros((128, 128), F32)] * heads
    for n, copy in enumerate(copies):
        low = load_pieces(low_ref.at[pl.ds(4 * n, 4)])
        copy.wait()
        rows = pl.ds(n * BLOCK, BLOCK)
        for i in range(3):
            lifted = dot_tn(low[i * rank : (i + 1) * rank, :], up_ref[i])
            moving_ref[i, rows, :] = (held[i, rows, :].astype(F32) + lifted).astype(BF16)
        for c in range(n * BLOCK // CHUNK, (n + 1) * BLOCK // CHUNK):
            rows = pl.ds(c * CHUNK, CHUNK)
            col = col_ref[rows, :]
            for h in range(heads):
                span = slice(h * 128, (h + 1) * 128)
                passing = pass_ref[c * heads + h : c * heads + h + 1, :]
                leave = col[:, LEAVE + h : LEAVE + h + 1]
                enter = col[:, ENTER + h : ENTER + h + 1]
                keyed = (moving_ref[1, rows, span].astype(F32) * leave).astype(BF16)
                scaled = (moving_ref[0, rows, span].astype(F32) * enter).astype(BF16)
                before_ref[c, h] = states[h].astype(BF16)
                states[h] = passing * states[h] + dot_tn(keyed, moving_ref[2, rows, span])
                returning[c, h] = dot_tn(scaled, grad_ref[rows, span])
    for h in range(heads):
        back = jnp.zeros((128, 128), F32)
        whole = jnp.ones((1, 128), F32)
        for c in reversed(range(chunks)):
            passing = pass_ref[c * heads + h : c * heads + h + 1, :]
            after_ref[c, h] = back.astype(BF16)
            back = passing * back + returning[c, h]
            whole = whole * passing
        summary_ref[h * 128 : (h + 1) * 128, :] = states[h].astype(BF16)
        summary_ref[size + h * 128 : size + (h + 1) * 128, :] = back.astype(BF16)
        summary_ref[2 * size + 16 * h : 2 * size + 16 * h + 16, :] = passing_rows(whole)


def passing_rows(row):
    first = row.astype(BF16).astype(F32)
    rest = row - first
    second = rest.astype(BF16).astype(F32)
    third = (rest - second).astype(BF16).astype(F32)
    return jnp.concatenate([first, second, third, jnp.zeros((13, 128), F32)], axis=0).astype(BF16)


def project(frozen, low, up, grad, col, passes):
    _, rows, features = frozen.shape
    heads = features // 128
    count = rows // CHUNK
    summary_rows = 2 * features + 16 * heads
    states = jax.ShapeDtypeStruct((count, heads, 128, 128), BF16)
    return pl.pallas_call(
        project_kernel,
        out_shape=(
            jax.ShapeDtypeStruct((3, rows, features), BF16),
            states,
            states,
            jax.ShapeDtypeStruct((summary_rows, 128), BF16),
        ),
        in_specs=[pl.BlockSpec(memory_space=pltpu.HBM)] + [VMEM] * 5,
        out_specs=(VMEM,) * 4,
        scratch_shapes=[
            pltpu.VMEM(states.shape, F32),
            pltpu.VMEM(frozen.shape, BF16),
            pltpu.SemaphoreType.DMA((rows // BLOCK,)),
        ],
        compiler_params=params(),
        cost_estimate=cost(4e9, 10e6),
        name="project",
    )(pltpu.with_memory_space_constraint(frozen, pltpu.HBM), low, up, grad, col, passes)


def passing_of(ref, base):
    return (
        ref[base : base + 1, :].astype(F32)
        + ref[base + 1 : base + 2, :].astype(F32)
        + ref[base + 2 : base + 3, :].astype(F32)
    )


def join_kernel(meta_ref, own_ref, mate_ref, *out_refs):
    y = meta_ref[1]
    core = meta_ref[2]
    total = own_ref.shape[0]
    heads = total // (2 * 128 + 16)
    size = heads * 128
    chips = len(out_refs) + 1
    second = core == 1
    for h in range(heads):
        rows = slice(h * 128, (h + 1) * 128)
        back_rows = slice(size + h * 128, size + (h + 1) * 128)
        base = 2 * size + 16 * h
        own_pass = passing_of(own_ref, base)
        mate_pass = passing_of(mate_ref, base)
        own_state = own_ref[rows, :].astype(F32)
        mate_state = mate_ref[rows, :].astype(F32)
        own_back = own_ref[back_rows, :].astype(F32)
        mate_back = mate_ref[back_rows, :].astype(F32)
        one = jnp.ones_like(own_pass)
        state = jnp.where(second, own_pass, one) * mate_state + jnp.where(second, one, mate_pass) * own_state
        back = jnp.where(second, one, own_pass) * mate_back + jnp.where(second, mate_pass, one) * own_back
        tail = passing_rows(own_pass * mate_pass)
        for k, out_ref in enumerate(out_refs):
            later = y + (k + 1) < chips
            out_ref[rows, :] = jnp.where(later, state, back).astype(BF16)
            out_ref[size + 16 * h : size + 16 * h + 16, :] = tail


def join(meta, own, mate, chips):
    heads = own.shape[0] // (2 * 128 + 16)
    message = jax.ShapeDtypeStruct((heads * (128 + 16), 128), BF16)
    return pl.pallas_call(
        join_kernel,
        out_shape=(message,) * (chips - 1),
        in_specs=[SMEM, VMEM, VMEM],
        out_specs=(VMEM,) * (chips - 1),
        compiler_params=params(),
        name="join",
    )(meta, own, mate)


def inside_kernel(moving_ref, grad_ref, row_ref, col_ref, before_ref, after_ref, part_ref):
    features = moving_ref.shape[2]
    heads = features // 128
    row_i = lax.broadcasted_iota(jnp.int32, (CHUNK, CHUNK), 0)
    col_i = lax.broadcasted_iota(jnp.int32, (CHUNK, CHUNK), 1)

    @pl.loop(0, moving_ref.shape[1] // CHUNK, unroll=4)
    def _(c):
        rows = chunk_rows(c)
        col = col_ref[rows, :]
        row = row_ref[:, rows]
        allowed = (row_i <= col_i) & (col[:, SEG : SEG + 1] == row[SEG : SEG + 1, :])
        shut = jnp.where(allowed, 0.0, NEGATIVE)
        for h in range(0, heads, 2):
            span = slice(h * 128, (h + 2) * 128)
            q = moving_ref[0, rows, span]
            k = moving_ref[1, rows, span]
            v = moving_ref[2, rows, span]
            g = grad_ref[rows, span]
            weights = jnp.exp(
                jnp.concatenate(
                    [(row[i : i + 1, :] - col[:, i : i + 1]) + shut for i in (h, h + 1)], axis=1
                )
            )
            queries = diagonal_of(q)
            cotangents = diagonal_of(g)
            before = diagonal(before_ref[c, h], before_ref[c, h + 1])
            after = diagonal(after_ref[c, h], after_ref[c, h + 1])
            enter = widen(col, ENTER + h)
            leave = widen(col, LEAVE + h)
            a = (dot_nt(k, queries) * weights).astype(BF16)
            b = (dot_nt(v, cotangents) * weights).astype(BF16)
            turned = jnp.concatenate([b[:, :128].T, b[:, 128:].T], axis=1)
            part_ref[0, rows, span] = dot_nn(turned, diagonal_of(k)) + enter * dot_nt(g, before)
            part_ref[1, rows, span] = dot_nn(b, queries) + leave * dot_nt(v, after)
            part_ref[2, rows, span] = dot_nn(a, cotangents) + leave * dot_nn(k, after)


def inside(moving, grad, row, col, before, after):
    return pl.pallas_call(
        inside_kernel,
        out_shape=jax.ShapeDtypeStruct(moving.shape, F32),
        in_specs=[VMEM] * 6,
        out_specs=VMEM,
        compiler_params=params(),
        cost_estimate=cost(12e9, 12e6),
        name="inside",
    )(moving, grad, row, col, before, after)


def late_kernel(first_block, moving_ref, row_ref, col_ref, pass_ref, before_ref, state_ref, *refs):
    attn_ref = refs[-1]
    features = moving_ref.shape[2]
    heads = features // 128
    inverse = 1.0 / 128.0
    step = first_block + pl.program_id(0)
    prefix_base = pass_ref.shape[0] // 2
    row_i = lax.broadcasted_iota(jnp.int32, (CHUNK, CHUNK), 0)
    col_i = lax.broadcasted_iota(jnp.int32, (CHUNK, CHUNK), 1)
    for n in range(BLOCK // CHUNK):
        rows = pl.ds(n * CHUNK, CHUNK)
        col = col_ref[rows, :]
        row = row_ref[:, rows]
        allowed = (row_i >= col_i) & (col[:, SEG : SEG + 1] == row[SEG : SEG + 1, :])
        shut = jnp.where(allowed, 0.0, NEGATIVE)
        first = prefix_base + (step * (BLOCK // CHUNK) + n) * heads
        states = []
        for h in range(heads):
            prefix = pass_ref[pl.ds(first + h, 1), :]
            state = before_ref[n, h].astype(F32) + prefix * state_ref[h].astype(F32)
            states.append(state.astype(BF16))
        for h in range(0, heads, 2):
            span = slice(h * 128, (h + 2) * 128)
            q = moving_ref[0, rows, span]
            weights = jnp.exp(
                jnp.concatenate(
                    [(col[:, i : i + 1] - row[i : i + 1, :]) + shut for i in (h, h + 1)], axis=1
                )
            )
            a = (dot_nt(q, diagonal_of(moving_ref[1, rows, span])) * weights).astype(BF16)
            out = dot_nn(a, diagonal_of(moving_ref[2, rows, span]))
            out = out + widen(col, ENTER + h) * dot_nn(q, diagonal(states[h], states[h + 1]))
            attn_ref[rows, span] = (out * inverse).astype(BF16)


def late(moving, row, col, passes, before, state, first_block, block_count, earlier=None):
    _, rows, features = moving.shape
    heads = features // 128
    far = pl.BlockSpec(memory_space=pltpu.HBM)
    return pl.pallas_call(
        functools.partial(late_kernel, first_block),
        out_shape=jax.ShapeDtypeStruct((rows, features), BF16),
        grid=(block_count,),
        in_specs=[
            pl.BlockSpec((3, BLOCK, features), lambda i: (0, first_block + i, 0)),
            pl.BlockSpec((8, BLOCK), lambda i: (0, first_block + i)),
            pl.BlockSpec((BLOCK, 128), lambda i: (first_block + i, 0)),
            pl.BlockSpec(passes.shape, lambda i: (0, 0)),
            pl.BlockSpec((BLOCK // CHUNK, heads, 128, 128), lambda i: (first_block + i, 0, 0, 0)),
            pl.BlockSpec(state.shape, lambda i: (0, 0, 0)),
        ]
        + ([] if earlier is None else [far]),
        out_specs=pl.BlockSpec((BLOCK, features), lambda i: (first_block + i, 0)),
        input_output_aliases={} if earlier is None else {6: 0},
        compiler_params=params(dimension_semantics=("arbitrary",)),
        cost_estimate=cost(6e9, 6e6),
        name="late",
    )(
        pltpu.with_memory_space_constraint(moving, pltpu.HBM),
        row, col, passes,
        pltpu.with_memory_space_constraint(before, pltpu.HBM),
        state,
        *([] if earlier is None else [earlier]),
    )


def store_halves(core, total, keep_ref, send_ref):
    half = total.shape[0] // 2
    keep_ref[...] = total[pl.ds(pl.multiple_of(core * half, 16), half), :].astype(BF16)
    send_ref[...] = total[pl.ds(pl.multiple_of((1 - core) * half, 16), half), :].astype(BF16)


def finish_kernel(
    chips, meta_ref, moving_ref, g_ref, part_ref, col_ref, low_ref, up_ref, mate_ref, *refs
):
    message_refs = refs[: chips - 1]
    out_ref, low_grad_ref, state_in, keep_ref, send_ref = refs[chips - 1 : chips + 4]
    back_in, grad_ref, total, sems = refs[chips + 4 :]
    rank = up_ref.shape[1]
    features = moving_ref.shape[2]
    heads = features // 128
    size = heads * 128
    count = moving_ref.shape[1] // BLOCK
    inverse = 1.0 / 128.0
    y = meta_ref[1]
    second = meta_ref[2] == 1
    for h in range(heads):
        rows = slice(h * 128, (h + 1) * 128)
        factor = jnp.ones((1, 128), F32)
        state = jnp.zeros((128, 128), F32)
        for k in range(1, chips):
            ref = message_refs[k - 1]
            state = state + jnp.where(k <= y, factor, 0.0) * ref[rows, :].astype(F32)
            factor = factor * passing_of(ref, size + 16 * h)
        factor = jnp.ones((1, 128), F32)
        back = jnp.zeros((128, 128), F32)
        for k in reversed(range(1, chips)):
            ref = message_refs[k - 1]
            back = back + jnp.where(k > y, factor, 0.0) * ref[rows, :].astype(F32)
            factor = factor * passing_of(ref, size + 16 * h)
        mate_pass = passing_of(mate_ref, 2 * size + 16 * h)
        mate_state = mate_ref[rows, :].astype(F32)
        mate_back = mate_ref[size + h * 128 : size + (h + 1) * 128, :].astype(F32)
        state_in[h] = jnp.where(second, mate_pass * state + mate_state, state).astype(BF16)
        back_in[h] = jnp.where(second, back, mate_pass * back + mate_back).astype(BF16)
    copies = []
    for n in range(count):
        rows = pl.ds(n * BLOCK, BLOCK)
        col = col_ref[rows, :]
        for h in range(0, heads, 2):
            span = slice(h * 128, (h + 2) * 128)
            enter = widen(col, ENTER_ALL + h)
            leave = widen(col, LEAVE_ALL + h)
            state = diagonal(state_in[h], state_in[h + 1])
            back = diagonal(back_in[h], back_in[h + 1])
            query = part_ref[0, rows, span] + enter * dot_nt(g_ref[rows, span], state)
            key = part_ref[1, rows, span] + leave * dot_nt(moving_ref[2, rows, span], back)
            value = part_ref[2, rows, span] + leave * dot_nn(moving_ref[1, rows, span], back)
            for i, result in enumerate((query, key, value)):
                grad_ref[i, rows, span] = (result * inverse).astype(BF16)
        copies.append(pltpu.make_async_copy(grad_ref.at[:, rows], out_ref.at[:, rows], sems.at[n]))
        copies[n].start()
        low_grad = [dot_nt(up_ref[i], grad_ref[i, rows, :]).astype(BF16) for i in range(3)]
        store_pieces(low_grad_ref.at[pl.ds(4 * n, 4)], jnp.concatenate(low_grad, axis=0))
        low = load_pieces(low_ref.at[pl.ds(4 * n, 4)])
        for i in range(3):
            lanes = slice(i * rank, (i + 1) * rank)
            term = dot_nn(low[lanes, :], grad_ref[i, rows, :])
            total[lanes, :] = term if n == 0 else total[lanes, :] + term
    store_halves(meta_ref[2], total, keep_ref, send_ref)
    for copy in copies:
        copy.wait()


def finish(meta, moving, grad, part, col, low, up, mate, messages):
    _, rows, features = moving.shape
    heads = features // 128
    width = up.shape[0] * up.shape[1]
    half = jax.ShapeDtypeStruct((width // 2, features), BF16)
    chips = len(messages) + 1
    return pl.pallas_call(
        functools.partial(finish_kernel, chips),
        out_shape=(
            jax.ShapeDtypeStruct(moving.shape, BF16),
            jax.ShapeDtypeStruct(piece_shape(rows, width), BF16),
            jax.ShapeDtypeStruct((heads, 128, 128), BF16),
            half,
            half,
        ),
        in_specs=[SMEM] + [VMEM] * (7 + len(messages)),
        out_specs=(pl.BlockSpec(memory_space=pltpu.HBM),) + (VMEM,) * 4,
        scratch_shapes=[
            pltpu.VMEM((heads, 128, 128), BF16),
            pltpu.VMEM(moving.shape, BF16),
            pltpu.VMEM((width, features), F32),
            pltpu.SemaphoreType.DMA((rows // BLOCK,)),
        ],
        compiler_params=params(),
        cost_estimate=cost(4e9, 14e6),
        name="finish",
    )(meta, moving, grad, part, col, low, up, mate, *messages)


def down_kernel(meta_ref, x_ref, grad_ref, keep_ref, send_ref, total):
    value = jnp.zeros(total.shape, F32)
    for c in range(x_ref.shape[0] // BLOCK):
        low_grad = load_pieces(grad_ref.at[pl.ds(4 * c, 4)])
        value = value + dot_nn(low_grad, x_ref[c * BLOCK : (c + 1) * BLOCK, :])
    total[...] = value
    store_halves(meta_ref[2], total, keep_ref, send_ref)


def partial_down(meta, x, low_grad):
    width = 2 * low_grad.shape[1]
    half = jax.ShapeDtypeStruct((width // 2, x.shape[1]), BF16)
    return pl.pallas_call(
        down_kernel,
        out_shape=(half, half),
        in_specs=[SMEM, VMEM, VMEM],
        out_specs=(VMEM, VMEM),
        scratch_shapes=[pltpu.VMEM((width, x.shape[1]), F32)],
        compiler_params=params(),
        name="partial_down",
    )(meta, x, low_grad)


def halves_kernel(meta_ref, own_ref, mate_ref, out_ref):
    core = meta_ref[2]
    half = own_ref.shape[0]
    out_ref[pl.ds(pl.multiple_of(core * half, 8), half), :] = own_ref[...]
    out_ref[pl.ds(pl.multiple_of((1 - core) * half, 8), half), :] = mate_ref[...]


def join_halves(meta, own, mate):
    return pl.pallas_call(
        halves_kernel,
        out_shape=jax.ShapeDtypeStruct((2 * own.shape[0], own.shape[1]), F32),
        in_specs=[SMEM, VMEM, VMEM],
        out_specs=VMEM,
        compiler_params=params(),
        name="join_halves",
    )(meta, own, mate)


def add_kernel(*refs):
    total = refs[0][...].astype(F32)
    for ref in refs[1:-1]:
        total = total + ref[...].astype(F32)
    refs[-1][...] = total.astype(refs[-1].dtype)


def add_all(arrays, dtype):
    return pl.pallas_call(
        add_kernel,
        out_shape=jax.ShapeDtypeStruct(arrays[0].shape, dtype),
        in_specs=[VMEM] * len(arrays),
        out_specs=VMEM,
        compiler_params=params(),
        name="add_all",
    )(*arrays)


def to_mate(a):
    return lax.ppermute(a, "core", [(0, 1), (1, 0)])


def along_y(a, k):
    count = lax.axis_size("y")
    return lax.ppermute(a, "y", [(i, (i + k) % count) for i in range(count)])


def local(inputs, frozen, adapter_down, adapter_up, out_grad, log_decay, doc_start, lengths):
    y, core = lax.axis_index("y"), lax.axis_index("core")
    chips = lax.axis_size("y")
    rank = adapter_up.shape[1]
    meta = jnp.stack([lengths[2 * y + core], y, core]).astype(jnp.int32)
    down = jnp.swapaxes(adapter_down, 1, 2).reshape(3 * rank, inputs.shape[1])
    row, col, passes = decay_tables(meta, log_decay, doc_start)
    low = exchange(sum_spread(exchange(partial_low(inputs, down))))
    moving, before, after, summary = project(frozen, low, adapter_up, out_grad, col, passes)
    mate = to_mate(summary)
    messages = [along_y(m, k + 1) for k, m in enumerate(join(meta, summary, mate, chips))]
    part = inside(moving, out_grad, row, col, before, after)
    grads, low_grad_part, state, up_keep, up_send = finish(
        meta, moving, out_grad, part, col, low, adapter_up, mate, messages
    )
    up_chip = add_all([up_keep, to_mate(up_send)], BF16)
    up_parts = [up_chip] + [along_y(up_chip, k) for k in range(1, chips)]
    pieces, up_chip = lax.optimization_barrier((exchange(low_grad_part), up_chip))
    half = inputs.shape[0] // BLOCK // 2
    first_half = late(moving, row, col, passes, before, state, 0, half)
    low_grad, first_half, *up_parts = lax.optimization_barrier(
        [exchange(sum_spread(pieces)), first_half] + up_parts
    )
    down_keep, down_send = partial_down(meta, inputs, low_grad)
    down_chip = add_all([down_keep, to_mate(down_send)], BF16)
    down_chip, state, *up_parts = lax.optimization_barrier([down_chip, state] + up_parts)
    down_parts = [down_chip] + [along_y(down_chip, k) for k in range(1, chips)]
    up_half = add_all(up_parts, F32)
    up_total = join_halves(meta, up_half, to_mate(up_half))
    attn = late(moving, row, col, passes, before, state, half, half, first_half)
    up_total, attn, *down_parts = lax.optimization_barrier([up_total, attn] + down_parts)
    down_half = add_all(down_parts, F32)
    down_total = join_halves(meta, down_half, to_mate(down_half))
    down_total = jnp.swapaxes(down_total.reshape(3, rank, inputs.shape[1]), 1, 2)
    return (attn, grads, down_total, up_total.reshape(adapter_up.shape))


def solution(mesh):
    seq, head = mesh.shape["seq"], mesh.shape["head"]
    side = 1
    while side * side < head:
        side *= 2
    mesh = jax.sharding.Mesh(
        mesh.devices.reshape(seq // 2, 2, head // side, side), ("y", "core", "z", "x")
    )
    seq, head = ("y", "core"), ("z", "x")
    in_specs = (
        P(seq, head),
        P(None, seq, head),
        P(None, head, None),
        P(None, None, head),
        P(seq, head),
        P(head, seq),
        P(seq),
        P(),
    )
    out_specs = (
        P(seq, head),
        P(None, seq, head),
        P(None, head, None),
        P(None, None, head),
    )
    return jax.shard_map(local, mesh=mesh, in_specs=in_specs, out_specs=out_specs, check_vma=False)
```

```python
import functools

import jax
import jax.numpy as jnp
from jax import lax
from jax.experimental import pallas as pl
from jax.experimental.pallas import tpu as pltpu
from jax.sharding import PartitionSpec as P

F32 = jnp.float32
BF16 = jnp.bfloat16
CHUNK = 128
BLOCK = 256
VMEM_BYTES = 20 * 1024 * 1024
NEGATIVE = -1e30
UNROLL = 8

CUM, SEG, ENTER, LEAVE, ENTER_ALL, LEAVE_ALL, ENTER_SHUT, LEAVE_SHUT = 0, 4, 8, 12, 16, 20, 24, 25
ROW_ENTER, ROW_LEAVE = 8, 12


def dot_nn(a, b):
    return lax.dot_general(a, b, (((1,), (0,)), ((), ())), preferred_element_type=F32)


def dot_nt(a, b):
    return lax.dot_general(a, b, (((1,), (1,)), ((), ())), preferred_element_type=F32)


def dot_tn(a, b):
    return lax.dot_general(a, b, (((0,), (0,)), ((), ())), preferred_element_type=F32)


def params(limit=VMEM_BYTES, **more):
    return pltpu.CompilerParams(vmem_limit_bytes=limit, **more)


def chunk_rows(c):
    return pl.ds(pl.multiple_of(c * CHUNK, CHUNK), CHUNK)


def diagonal(a, b):
    zero = jnp.zeros_like(a)
    return jnp.concatenate(
        [jnp.concatenate([a, zero], axis=1), jnp.concatenate([zero, b], axis=1)], axis=0
    )


def diagonal_of(pair):
    return diagonal(pair[:, :128], pair[:, 128:])


def pair_nt(a, b):
    return jnp.concatenate(
        [dot_nt(a[:, :128], b[:, :128]), dot_nt(a[:, 128:], b[:, 128:])], axis=1
    )


def widen(table, lane):
    shape = (table.shape[0], 128)
    return jnp.concatenate(
        [jnp.broadcast_to(table[:, i : i + 1], shape) for i in (lane, lane + 1)], axis=1
    )


def cost(flops, moved):
    return pl.CostEstimate(flops=int(flops), bytes_accessed=int(moved), transcendentals=0)


VMEM = pl.BlockSpec(memory_space=pltpu.VMEM)
SMEM = pl.BlockSpec(memory_space=pltpu.SMEM)


def store_pieces(out_ref, value):
    half = value.shape[0] // 2
    for r in range(2):
        for l in range(2):
            out_ref[2 * r + l] = value[r * half : (r + 1) * half, l * 128 : (l + 1) * 128]


def load_pieces(ref):
    rows = [jnp.concatenate([ref[2 * r], ref[2 * r + 1]], axis=1) for r in range(2)]
    return jnp.concatenate(rows, axis=0)


def piece_shape(rows, width):
    return (rows // BLOCK * 4, width // 2, BLOCK // 2)


def piece_spec(width):
    return pl.BlockSpec((4, width // 2, BLOCK // 2), lambda i: (i, 0, 0))


def low_kernel(x_ref, down_ref, out_ref, x_held, down_held, sems):
    count = x_ref.shape[0] // BLOCK
    first = pltpu.make_async_copy(down_ref, down_held, sems.at[count])
    first.start()
    copies = []
    for c in range(count):
        rows = pl.ds(c * BLOCK, BLOCK)
        copies.append(pltpu.make_async_copy(x_ref.at[rows], x_held.at[rows], sems.at[c]))
        copies[c].start()
    first.wait()
    for c in range(count):
        copies[c].wait()
        part = dot_nt(down_held[...], x_held[c * BLOCK : (c + 1) * BLOCK, :])
        store_pieces(out_ref.at[pl.ds(4 * c, 4)], part.astype(BF16))


def partial_low(x, down):
    rows, _ = x.shape
    far = pl.BlockSpec(memory_space=pltpu.HBM)
    return pl.pallas_call(
        low_kernel,
        out_shape=jax.ShapeDtypeStruct(piece_shape(rows, down.shape[0]), BF16),
        in_specs=[far, far],
        out_specs=VMEM,
        scratch_shapes=[
            pltpu.VMEM(x.shape, BF16),
            pltpu.VMEM(down.shape, BF16),
            pltpu.SemaphoreType.DMA((rows // BLOCK + 1,)),
        ],
        compiler_params=params(),
        name="partial_low",
    )(*(pltpu.with_memory_space_constraint(a, pltpu.HBM) for a in (x, down)))


def sum_spread_kernel(in_ref, out_ref):
    count = in_ref.shape[0]
    total = in_ref[0].astype(F32)
    for i in range(1, count):
        total = total + in_ref[i].astype(F32)
    total = total.astype(BF16)
    for i in range(count):
        out_ref[i] = total


def exchange(pieces):
    return lax.all_to_all(pieces, ("z", "x"), 0, 0)


def sum_spread(pieces):
    count, rows, width = pieces.shape
    return pl.pallas_call(
        sum_spread_kernel,
        out_shape=jax.ShapeDtypeStruct(pieces.shape, BF16),
        in_specs=[VMEM],
        out_specs=VMEM,
        compiler_params=params(),
        name="sum_spread",
    )(pieces)


def decay_kernel(meta_ref, decay_ref, start_ref, row_ref, col_ref, pass_ref):
    heads, rows = decay_ref.shape
    live = meta_ref[0]
    slot = lax.broadcasted_iota(jnp.int32, (1, rows), 1)
    keep = slot < live
    decay = jnp.where(keep, decay_ref[...].astype(F32), 0.0)
    starts = jnp.where(keep, start_ref[...].astype(F32), 0.0)
    both = jnp.concatenate([decay, starts, jnp.zeros((8 - heads - 1, rows), F32)], axis=0)
    both = both.astype(BF16)
    row_i = lax.broadcasted_iota(jnp.int32, (CHUNK, CHUNK), 0)
    col_i = lax.broadcasted_iota(jnp.int32, (CHUNK, CHUNK), 1)
    upper = jnp.where(row_i <= col_i, 1.0, 0.0).astype(BF16)
    lower = jnp.where(row_i >= col_i, 1.0, 0.0).astype(BF16)
    count = rows // CHUNK
    enters, leaves, passes = [], [], []
    prefix = jnp.ones((heads, 128), F32)
    for c in range(count):
        span = slice(c * CHUNK, (c + 1) * CHUNK)
        piece = both[:, span]
        by_row = dot_nn(piece, upper)
        by_col = dot_nt(lower, piece)
        here = keep[:, span]
        here_col = c * CHUNK + lax.broadcasted_iota(jnp.int32, (CHUNK, 1), 0) < live
        head_row = lax.broadcasted_iota(jnp.int32, (8, CHUNK), 0)
        head_lane = lax.broadcasted_iota(jnp.int32, (CHUNK, 8), 1)
        row_ref[0:8, span] = jnp.where(here | (head_row != heads), by_row, -1.0)
        end_row = by_row[:, CHUNK - 1 : CHUNK]
        row_seg = by_row[heads : heads + 1]
        row_ref[ROW_ENTER : ROW_ENTER + heads, span] = jnp.where(
            (row_seg == 0.0) & here, jnp.exp(by_row[:heads]), 0.0
        )
        row_ref[ROW_LEAVE : ROW_LEAVE + heads, span] = jnp.where(
            (row_seg == end_row[heads : heads + 1]) & here, jnp.exp(end_row[:heads] - by_row[:heads]), 0.0
        )
        col_ref[span, 0:8] = jnp.where(here_col | (head_lane != heads), by_col, -2.0)
        cum = by_col[:, :heads]
        seg = by_col[:, heads : heads + 1]
        cum_end = by_col[CHUNK - 1 : CHUNK, :heads]
        seg_end = by_col[CHUNK - 1 : CHUNK, heads : heads + 1]
        may_enter = (seg == 0.0) & here_col
        may_leave = (seg == seg_end) & here_col
        enter = jnp.where(may_enter, jnp.exp(cum), 0.0)
        leave = jnp.where(may_leave, jnp.exp(cum_end - cum), 0.0)
        col_ref[span, ENTER_SHUT : ENTER_SHUT + 1] = jnp.where(may_enter, 0.0, NEGATIVE)
        col_ref[span, LEAVE_SHUT : LEAVE_SHUT + 1] = jnp.where(may_leave, 0.0, NEGATIVE)
        col_ref[span, ENTER : ENTER + heads] = enter
        col_ref[span, LEAVE : LEAVE + heads] = leave
        enters.append(enter)
        leaves.append(leave)
        passes.append(jnp.where(seg_end == 0.0, jnp.exp(cum_end), 0.0))
        passing_col = jnp.where(end_row[heads : heads + 1] == 0.0, jnp.exp(end_row[:heads]), 0.0)
        passing_rows_here = jnp.broadcast_to(passing_col, (heads, 128))
        pass_ref[c * heads : (c + 1) * heads, :] = passing_rows_here
        first = (count + c) * heads
        pass_ref[first : first + heads, :] = prefix
        first = (2 * count + c) * heads
        pass_ref[first : first + heads, :] = jnp.broadcast_to(end_row[:heads], (heads, 128))
        prefix = prefix * passing_rows_here
    before = jnp.ones((1, heads), F32)
    for c in range(count):
        span = slice(c * CHUNK, (c + 1) * CHUNK)
        col_ref[span, ENTER_ALL : ENTER_ALL + heads] = enters[c] * before
        before = before * passes[c]
    after = jnp.ones((1, heads), F32)
    for c in reversed(range(count)):
        span = slice(c * CHUNK, (c + 1) * CHUNK)
        col_ref[span, LEAVE_ALL : LEAVE_ALL + heads] = leaves[c] * after
        after = after * passes[c]


def decay_tables(meta, decay, starts):
    heads, rows = decay.shape
    count = rows // CHUNK
    return pl.pallas_call(
        decay_kernel,
        out_shape=(
            jax.ShapeDtypeStruct((16, rows), F32),
            jax.ShapeDtypeStruct((rows, 128), F32),
            jax.ShapeDtypeStruct((3 * count * heads, 128), F32),
        ),
        in_specs=[SMEM, VMEM, VMEM],
        out_specs=(VMEM, VMEM, VMEM),
        compiler_params=params(),
        cost_estimate=cost(4e9, 1e6),
        name="decay_tables",
    )(meta, decay, starts.reshape(1, rows))


def project_kernel(
    frozen_ref, low_ref, up_ref, grad_ref, row_ref, pass_ref,
    moving_ref, before_ref, after_ref, summary_ref, returning, held, sems,
):
    chunks = returning.shape[0]
    rank = up_ref.shape[1]
    features = frozen_ref.shape[2]
    heads = features // 128
    size = heads * 128
    copies = []
    for n in range(frozen_ref.shape[1] // BLOCK):
        rows = pl.ds(n * BLOCK, BLOCK)
        copies.append(pltpu.make_async_copy(frozen_ref.at[:, rows], held.at[:, rows], sems.at[n]))
        copies[n].start()
    states = [jnp.zeros((128, 128), F32)] * heads
    for n, copy in enumerate(copies):
        low = load_pieces(low_ref.at[pl.ds(4 * n, 4)])
        lifted = [dot_tn(low[i * rank : (i + 1) * rank, :], up_ref[i]) for i in range(3)]
        copy.wait()
        rows = pl.ds(n * BLOCK, BLOCK)
        for i in range(3):
            moving_ref[i, rows, :] = (held[i, rows, :].astype(F32) + lifted[i]).astype(BF16)
        for c in range(n * BLOCK // CHUNK, (n + 1) * BLOCK // CHUNK):
            rows = pl.ds(c * CHUNK, CHUNK)
            for h in range(heads):
                span = slice(h * 128, (h + 1) * 128)
                passing = pass_ref[c * heads + h : c * heads + h + 1, :]
                leave = row_ref[ROW_LEAVE + h : ROW_LEAVE + h + 1, rows]
                enter = row_ref[ROW_ENTER + h : ROW_ENTER + h + 1, rows]
                valued = (moving_ref[2, rows, span].T.astype(F32) * leave).astype(BF16)
                scaled = (moving_ref[0, rows, span].T.astype(F32) * enter).astype(BF16)
                before_ref[c, h] = states[h].astype(BF16)
                states[h] = passing * states[h] + dot_nn(valued, moving_ref[1, rows, span])
                returning[c, h] = dot_nn(scaled, grad_ref[rows, span])
    for h in range(heads):
        back = jnp.zeros((128, 128), F32)
        whole = jnp.ones((1, 128), F32)
        for c in reversed(range(chunks)):
            passing = pass_ref[c * heads + h : c * heads + h + 1, :]
            after_ref[c, h] = back.astype(BF16)
            back = passing * back + returning[c, h]
            whole = whole * passing
        summary_ref[h * 128 : (h + 1) * 128, :] = states[h].astype(BF16)
        summary_ref[size + h * 128 : size + (h + 1) * 128, :] = back.astype(BF16)
        summary_ref[2 * size + 16 * h : 2 * size + 16 * h + 16, :] = passing_rows(whole)


def passing_rows(row):
    first = row.astype(BF16).astype(F32)
    rest = row - first
    second = rest.astype(BF16).astype(F32)
    third = (rest - second).astype(BF16).astype(F32)
    return jnp.concatenate([first, second, third, jnp.zeros((13, 128), F32)], axis=0).astype(BF16)


def project(frozen, low, up, grad, row, passes):
    _, rows, features = frozen.shape
    heads = features // 128
    count = rows // CHUNK
    summary_rows = 2 * features + 16 * heads
    states = jax.ShapeDtypeStruct((count, heads, 128, 128), BF16)
    return pl.pallas_call(
        project_kernel,
        out_shape=(
            jax.ShapeDtypeStruct((3, rows, features), BF16),
            states,
            states,
            jax.ShapeDtypeStruct((summary_rows, 128), BF16),
        ),
        in_specs=[pl.BlockSpec(memory_space=pltpu.HBM)] + [VMEM] * 5,
        out_specs=(VMEM,) * 4,
        scratch_shapes=[
            pltpu.VMEM(states.shape, F32),
            pltpu.VMEM(frozen.shape, BF16),
            pltpu.SemaphoreType.DMA((rows // BLOCK,)),
        ],
        compiler_params=params(),
        cost_estimate=cost(4e9, 10e6),
        name="project",
    )(pltpu.with_memory_space_constraint(frozen, pltpu.HBM), low, up, grad, row, passes)


def passing_of(ref, base):
    return (
        ref[base : base + 1, :].astype(F32)
        + ref[base + 1 : base + 2, :].astype(F32)
        + ref[base + 2 : base + 3, :].astype(F32)
    )


def join_kernel(meta_ref, own_ref, mate_ref, *out_refs):
    y = meta_ref[1]
    core = meta_ref[2]
    total = own_ref.shape[0]
    heads = total // (2 * 128 + 16)
    size = heads * 128
    chips = len(out_refs) + 1
    second = core == 1
    for h in range(heads):
        rows = slice(h * 128, (h + 1) * 128)
        back_rows = slice(size + h * 128, size + (h + 1) * 128)
        base = 2 * size + 16 * h
        own_pass = passing_of(own_ref, base)
        mate_pass = passing_of(mate_ref, base)
        own_state = own_ref[rows, :].astype(F32)
        mate_state = mate_ref[rows, :].astype(F32)
        own_back = own_ref[back_rows, :].astype(F32)
        mate_back = mate_ref[back_rows, :].astype(F32)
        one = jnp.ones_like(own_pass)
        state = jnp.where(second, own_pass, one) * mate_state + jnp.where(second, one, mate_pass) * own_state
        back = jnp.where(second, one, own_pass) * mate_back + jnp.where(second, mate_pass, one) * own_back
        tail = passing_rows(own_pass * mate_pass)
        for k, out_ref in enumerate(out_refs):
            later = y + (k + 1) < chips
            out_ref[rows, :] = jnp.where(later, state, back).astype(BF16)
            out_ref[size + 16 * h : size + 16 * h + 16, :] = tail


def join(meta, own, mate, chips):
    heads = own.shape[0] // (2 * 128 + 16)
    message = jax.ShapeDtypeStruct((heads * (128 + 16), 128), BF16)
    return pl.pallas_call(
        join_kernel,
        out_shape=(message,) * (chips - 1),
        in_specs=[SMEM, VMEM, VMEM],
        out_specs=(VMEM,) * (chips - 1),
        compiler_params=params(),
        name="join",
    )(meta, own, mate)


def inside_kernel(moving_ref, grad_ref, row_ref, col_ref, pass_ref, before_ref, after_ref, part_ref):
    features = moving_ref.shape[2]
    heads = features // 128
    square = (CHUNK, CHUNK)
    row_i = lax.broadcasted_iota(jnp.int32, square, 0)
    col_i = lax.broadcasted_iota(jnp.int32, square, 1)
    end_base = pass_ref.shape[0] // 3 * 2

    def paired(make, h):
        return jnp.concatenate([make(h), make(h + 1)], axis=1)

    @pl.loop(0, moving_ref.shape[1] // CHUNK, unroll=UNROLL)
    def _(c):
        rows = chunk_rows(c)
        col = col_ref[rows, :]
        row = row_ref[0:8, rows]
        same = col[:, SEG : SEG + 1] == row[SEG : SEG + 1, :]
        shut = jnp.where(same & (row_i <= col_i), 0.0, NEGATIVE)
        shut_turned = jnp.where(same & (row_i >= col_i), 0.0, NEGATIVE)
        enter_shut = jnp.broadcast_to(col[:, ENTER_SHUT : ENTER_SHUT + 1], square)
        leave_shut = jnp.broadcast_to(col[:, LEAVE_SHUT : LEAVE_SHUT + 1], square)
        sums = [jnp.broadcast_to(col[:, h : h + 1], square) for h in range(heads)]
        ends = pass_ref[pl.ds(end_base + c * heads, heads), :]
        for h in range(0, heads, 2):
            span = slice(h * 128, (h + 2) * 128)
            q = moving_ref[0, rows, span]
            k = moving_ref[1, rows, span]
            v = moving_ref[2, rows, span]
            g = grad_ref[rows, span]
            weights = paired(lambda i: jnp.exp((row[i : i + 1, :] - sums[i]) + shut), h)
            turned = paired(lambda i: jnp.exp((sums[i] - row[i : i + 1, :]) + shut_turned), h)
            enter = paired(lambda i: jnp.exp(sums[i] + enter_shut), h)
            leave = paired(lambda i: jnp.exp((ends[i : i + 1, :] - sums[i]) + leave_shut), h)
            queries = diagonal_of(q)
            cotangents = diagonal_of(g)
            before = diagonal(before_ref[c, h], before_ref[c, h + 1])
            after = diagonal(after_ref[c, h], after_ref[c, h + 1])
            a = (pair_nt(k, q) * weights).astype(BF16)
            b = (pair_nt(v, g) * weights).astype(BF16)
            b_turned = (pair_nt(g, v) * turned).astype(BF16)
            part_ref[0, rows, span] = dot_nn(b_turned, diagonal_of(k)) + enter * dot_nn(g, before)
            part_ref[1, rows, span] = dot_nn(b, queries) + leave * dot_nt(v, after)
            part_ref[2, rows, span] = dot_nn(a, cotangents) + leave * dot_nn(k, after)


def inside(moving, grad, row, col, passes, before, after):
    return pl.pallas_call(
        inside_kernel,
        out_shape=jax.ShapeDtypeStruct(moving.shape, F32),
        in_specs=[VMEM] * 7,
        out_specs=VMEM,
        compiler_params=params(),
        cost_estimate=cost(12e9, 12e6),
        name="inside",
    )(moving, grad, row, col, passes, before, after)


def late_kernel(moving_ref, row_ref, col_ref, pass_ref, before_ref, state_ref, attn_ref):
    features = moving_ref.shape[2]
    heads = features // 128
    inverse = 1.0 / 128.0
    step = pl.program_id(0)
    prefix_base = pass_ref.shape[0] // 3
    row_i = lax.broadcasted_iota(jnp.int32, (CHUNK, CHUNK), 0)
    col_i = lax.broadcasted_iota(jnp.int32, (CHUNK, CHUNK), 1)
    for n in range(BLOCK // CHUNK):
        rows = pl.ds(n * CHUNK, CHUNK)
        col = col_ref[rows, :]
        row = row_ref[:, rows]
        allowed = (row_i >= col_i) & (col[:, SEG : SEG + 1] == row[SEG : SEG + 1, :])
        shut = jnp.where(allowed, 0.0, NEGATIVE)
        first = prefix_base + (step * (BLOCK // CHUNK) + n) * heads
        states = []
        for h in range(heads):
            prefix = pass_ref[pl.ds(first + h, 1), :]
            state = before_ref[n, h].astype(F32) + prefix * state_ref[h].astype(F32)
            states.append(state.astype(BF16))
        for h in range(0, heads, 2):
            span = slice(h * 128, (h + 2) * 128)
            q = moving_ref[0, rows, span]
            weights = jnp.exp(
                jnp.concatenate(
                    [(col[:, i : i + 1] - row[i : i + 1, :]) + shut for i in (h, h + 1)], axis=1
                )
            )
            a = (dot_nt(q, diagonal_of(moving_ref[1, rows, span])) * weights).astype(BF16)
            out = dot_nn(a, diagonal_of(moving_ref[2, rows, span]))
            out = out + widen(col, ENTER + h) * dot_nt(q, diagonal(states[h], states[h + 1]))
            attn_ref[rows, span] = (out * inverse).astype(BF16)


def late(moving, row, col, passes, before, state):
    _, rows, features = moving.shape
    heads = features // 128
    moving, before = (pltpu.with_memory_space_constraint(a, pltpu.HBM) for a in (moving, before))
    return pl.pallas_call(
        late_kernel,
        out_shape=jax.ShapeDtypeStruct((rows, features), BF16),
        grid=(rows // BLOCK,),
        in_specs=[
            pl.BlockSpec((3, BLOCK, features), lambda i: (0, i, 0)),
            pl.BlockSpec((8, BLOCK), lambda i: (0, i)),
            pl.BlockSpec((BLOCK, 128), lambda i: (i, 0)),
            pl.BlockSpec(passes.shape, lambda i: (0, 0)),
            pl.BlockSpec((BLOCK // CHUNK, heads, 128, 128), lambda i: (i, 0, 0, 0)),
            pl.BlockSpec(state.shape, lambda i: (0, 0, 0)),
        ],
        out_specs=pl.BlockSpec((BLOCK, features), lambda i: (i, 0)),
        compiler_params=params(dimension_semantics=("arbitrary",)),
        cost_estimate=cost(6e9, 6e6),
        name="late",
    )(moving, row, col, passes, before, state)


def store_halves(core, total, keep_ref, send_ref):
    half = total.shape[0] // 2
    keep_ref[...] = total[pl.ds(pl.multiple_of(core * half, 16), half), :].astype(BF16)
    send_ref[...] = total[pl.ds(pl.multiple_of((1 - core) * half, 16), half), :].astype(BF16)


def finish_kernel(
    chips, meta_ref, moving_ref, g_ref, part_ref, col_ref, low_ref, up_ref, mate_ref, *refs
):
    message_refs = refs[: chips - 1]
    out_ref, low_grad_ref, state_in, keep_ref, send_ref = refs[chips - 1 : chips + 4]
    back_in, grad_ref, total, sems = refs[chips + 4 :]
    rank = up_ref.shape[1]
    features = moving_ref.shape[2]
    heads = features // 128
    size = heads * 128
    count = moving_ref.shape[1] // BLOCK
    inverse = 1.0 / 128.0
    y = meta_ref[1]
    second = meta_ref[2] == 1
    for h in range(heads):
        rows = slice(h * 128, (h + 1) * 128)
        factor = jnp.ones((1, 128), F32)
        state = jnp.zeros((128, 128), F32)
        for k in range(1, chips):
            ref = message_refs[k - 1]
            state = state + jnp.where(k <= y, factor, 0.0) * ref[rows, :].astype(F32)
            factor = factor * passing_of(ref, size + 16 * h)
        factor = jnp.ones((1, 128), F32)
        back = jnp.zeros((128, 128), F32)
        for k in reversed(range(1, chips)):
            ref = message_refs[k - 1]
            back = back + jnp.where(k > y, factor, 0.0) * ref[rows, :].astype(F32)
            factor = factor * passing_of(ref, size + 16 * h)
        mate_pass = passing_of(mate_ref, 2 * size + 16 * h)
        mate_state = mate_ref[rows, :].astype(F32)
        mate_back = mate_ref[size + h * 128 : size + (h + 1) * 128, :].astype(F32)
        state_in[h] = jnp.where(second, mate_pass * state + mate_state, state).astype(BF16)
        back_in[h] = jnp.where(second, back, mate_pass * back + mate_back).astype(BF16)
    copies = []
    for n in range(count):
        rows = pl.ds(n * BLOCK, BLOCK)
        col = col_ref[rows, :]
        for h in range(0, heads, 2):
            span = slice(h * 128, (h + 2) * 128)
            enter = widen(col, ENTER_ALL + h)
            leave = widen(col, LEAVE_ALL + h)
            state = diagonal(state_in[h], state_in[h + 1])
            back = diagonal(back_in[h], back_in[h + 1])
            query = part_ref[0, rows, span] + enter * dot_nn(g_ref[rows, span], state)
            key = part_ref[1, rows, span] + leave * dot_nt(moving_ref[2, rows, span], back)
            value = part_ref[2, rows, span] + leave * dot_nn(moving_ref[1, rows, span], back)
            for i, result in enumerate((query, key, value)):
                grad_ref[i, rows, span] = (result * inverse).astype(BF16)
        copies.append(pltpu.make_async_copy(grad_ref.at[:, rows], out_ref.at[:, rows], sems.at[n]))
        copies[n].start()
        low_grad = [dot_nt(up_ref[i], grad_ref[i, rows, :]).astype(BF16) for i in range(3)]
        store_pieces(low_grad_ref.at[pl.ds(4 * n, 4)], jnp.concatenate(low_grad, axis=0))
        low = load_pieces(low_ref.at[pl.ds(4 * n, 4)])
        for i in range(3):
            lanes = slice(i * rank, (i + 1) * rank)
            term = dot_nn(low[lanes, :], grad_ref[i, rows, :])
            total[lanes, :] = term if n == 0 else total[lanes, :] + term
    store_halves(meta_ref[2], total, keep_ref, send_ref)
    for copy in copies:
        copy.wait()


def finish(meta, moving, grad, part, col, low, up, mate, messages):
    _, rows, features = moving.shape
    heads = features // 128
    width = up.shape[0] * up.shape[1]
    half = jax.ShapeDtypeStruct((width // 2, features), BF16)
    chips = len(messages) + 1
    return pl.pallas_call(
        functools.partial(finish_kernel, chips),
        out_shape=(
            jax.ShapeDtypeStruct(moving.shape, BF16),
            jax.ShapeDtypeStruct(piece_shape(rows, width), BF16),
            jax.ShapeDtypeStruct((heads, 128, 128), BF16),
            half,
            half,
        ),
        in_specs=[SMEM] + [VMEM] * (7 + len(messages)),
        out_specs=(pl.BlockSpec(memory_space=pltpu.HBM),) + (VMEM,) * 4,
        scratch_shapes=[
            pltpu.VMEM((heads, 128, 128), BF16),
            pltpu.VMEM(moving.shape, BF16),
            pltpu.VMEM((width, features), F32),
            pltpu.SemaphoreType.DMA((rows // BLOCK,)),
        ],
        compiler_params=params(),
        cost_estimate=cost(4e9, 14e6),
        name="finish",
    )(meta, moving, grad, part, col, low, up, mate, *messages)


def down_kernel(meta_ref, x_ref, grad_ref, keep_ref, send_ref, total):
    value = jnp.zeros(total.shape, F32)
    for c in range(x_ref.shape[0] // BLOCK):
        low_grad = load_pieces(grad_ref.at[pl.ds(4 * c, 4)])
        value = value + dot_nn(low_grad, x_ref[c * BLOCK : (c + 1) * BLOCK, :])
    total[...] = value
    store_halves(meta_ref[2], total, keep_ref, send_ref)


def partial_down(meta, x, low_grad):
    width = 2 * low_grad.shape[1]
    half = jax.ShapeDtypeStruct((width // 2, x.shape[1]), BF16)
    return pl.pallas_call(
        down_kernel,
        out_shape=(half, half),
        in_specs=[SMEM, VMEM, VMEM],
        out_specs=(VMEM, VMEM),
        scratch_shapes=[pltpu.VMEM((width, x.shape[1]), F32)],
        compiler_params=params(),
        name="partial_down",
    )(meta, x, low_grad)


def halves_kernel(meta_ref, own_ref, mate_ref, out_ref):
    core = meta_ref[2]
    half = own_ref.shape[0]
    out_ref[pl.ds(pl.multiple_of(core * half, 8), half), :] = own_ref[...]
    out_ref[pl.ds(pl.multiple_of((1 - core) * half, 8), half), :] = mate_ref[...]


def join_halves(meta, own, mate):
    return pl.pallas_call(
        halves_kernel,
        out_shape=jax.ShapeDtypeStruct((2 * own.shape[0], own.shape[1]), F32),
        in_specs=[SMEM, VMEM, VMEM],
        out_specs=VMEM,
        compiler_params=params(),
        name="join_halves",
    )(meta, own, mate)


def add_kernel(*refs):
    total = refs[0][...].astype(F32)
    for ref in refs[1:-1]:
        total = total + ref[...].astype(F32)
    refs[-1][...] = total.astype(refs[-1].dtype)


def add_all(arrays, dtype):
    return pl.pallas_call(
        add_kernel,
        out_shape=jax.ShapeDtypeStruct(arrays[0].shape, dtype),
        in_specs=[VMEM] * len(arrays),
        out_specs=VMEM,
        compiler_params=params(),
        name="add_all",
    )(*arrays)


def to_mate(a):
    return lax.ppermute(a, "core", [(0, 1), (1, 0)])


def along_y(a, k):
    count = lax.axis_size("y")
    return lax.ppermute(a, "y", [(i, (i + k) % count) for i in range(count)])


def local(inputs, frozen, adapter_down, adapter_up, out_grad, log_decay, doc_start, lengths):
    y, core = lax.axis_index("y"), lax.axis_index("core")
    chips = lax.axis_size("y")
    rank = adapter_up.shape[1]
    meta = jnp.stack([lengths[2 * y + core], y, core]).astype(jnp.int32)
    down = jnp.swapaxes(adapter_down, 1, 2).reshape(3 * rank, inputs.shape[1])
    row, col, passes = decay_tables(meta, log_decay, doc_start)
    low = exchange(sum_spread(exchange(partial_low(inputs, down))))
    moving, before, after, summary = project(frozen, low, adapter_up, out_grad, row, passes)
    mate = to_mate(summary)
    messages = [along_y(m, k + 1) for k, m in enumerate(join(meta, summary, mate, chips))]
    part = inside(moving, out_grad, row, col, passes, before, after)
    grads, low_grad_part, state, up_keep, up_send = finish(
        meta, moving, out_grad, part, col, low, adapter_up, mate, messages
    )
    up_chip = add_all([up_keep, to_mate(up_send)], BF16)
    up_parts = [up_chip] + [along_y(up_chip, k) for k in range(1, chips)]
    pieces, up_chip = lax.optimization_barrier((exchange(low_grad_part), up_chip))
    attn = late(moving, row, col, passes, before, state)
    low_grad, attn, *up_parts = lax.optimization_barrier(
        [exchange(sum_spread(pieces)), attn] + up_parts
    )
    down_keep, down_send = partial_down(meta, inputs, low_grad)
    down_chip = add_all([down_keep, to_mate(down_send)], BF16)
    down_chip, *up_parts = lax.optimization_barrier([down_chip] + up_parts)
    down_parts = [down_chip] + [along_y(down_chip, k) for k in range(1, chips)]
    up_half = add_all(up_parts, F32)
    up_total = join_halves(meta, up_half, to_mate(up_half))
    up_total, *down_parts = lax.optimization_barrier([up_total] + down_parts)
    down_half = add_all(down_parts, F32)
    down_total = join_halves(meta, down_half, to_mate(down_half))
    down_total = jnp.swapaxes(down_total.reshape(3, rank, inputs.shape[1]), 1, 2)
    return (attn, grads, down_total, up_total.reshape(adapter_up.shape))


def solution(mesh):
    seq, head = mesh.shape["seq"], mesh.shape["head"]
    side = 1
    while side * side < head:
        side *= 2
    mesh = jax.sharding.Mesh(
        mesh.devices.reshape(seq // 2, 2, head // side, side), ("y", "core", "z", "x")
    )
    seq, head = ("y", "core"), ("z", "x")
    in_specs = (
        P(seq, head),
        P(None, seq, head),
        P(None, head, None),
        P(None, None, head),
        P(seq, head),
        P(head, seq),
        P(seq),
        P(),
    )
    out_specs = (
        P(seq, head),
        P(None, seq, head),
        P(None, head, None),
        P(None, None, head),
    )
    return jax.shard_map(local, mesh=mesh, in_specs=in_specs, out_specs=out_specs, check_vma=False)
```

```python
import functools

import jax
import jax.numpy as jnp
from jax import lax
from jax.experimental import pallas as pl
from jax.experimental.pallas import tpu as pltpu
from jax.sharding import PartitionSpec as P

F32 = jnp.float32
BF16 = jnp.bfloat16
CHUNK = 128
BLOCK = 256
VMEM_BYTES = 20 * 1024 * 1024
NEGATIVE = -1e30
UNROLL = 8

CUM, SEG, ENTER, LEAVE, ENTER_ALL, LEAVE_ALL, ENTER_SHUT, LEAVE_SHUT = 0, 4, 8, 12, 16, 20, 24, 25
ROW_ENTER, ROW_LEAVE = 8, 12


def dot_nn(a, b):
    return lax.dot_general(a, b, (((1,), (0,)), ((), ())), preferred_element_type=F32)


def dot_nt(a, b):
    return lax.dot_general(a, b, (((1,), (1,)), ((), ())), preferred_element_type=F32)


def dot_tn(a, b):
    return lax.dot_general(a, b, (((0,), (0,)), ((), ())), preferred_element_type=F32)


def params(limit=VMEM_BYTES, **more):
    return pltpu.CompilerParams(vmem_limit_bytes=limit, **more)


def chunk_rows(c):
    return pl.ds(pl.multiple_of(c * CHUNK, CHUNK), CHUNK)


def diagonal(a, b):
    zero = jnp.zeros_like(a)
    return jnp.concatenate(
        [jnp.concatenate([a, zero], axis=1), jnp.concatenate([zero, b], axis=1)], axis=0
    )


def diagonal_of(pair):
    return diagonal(pair[:, :128], pair[:, 128:])


def pair_nt(a, b):
    return jnp.concatenate(
        [dot_nt(a[:, :128], b[:, :128]), dot_nt(a[:, 128:], b[:, 128:])], axis=1
    )


def widen(table, lane):
    shape = (table.shape[0], 128)
    return jnp.concatenate(
        [jnp.broadcast_to(table[:, i : i + 1], shape) for i in (lane, lane + 1)], axis=1
    )


def cost(flops, moved):
    return pl.CostEstimate(flops=int(flops), bytes_accessed=int(moved), transcendentals=0)


VMEM = pl.BlockSpec(memory_space=pltpu.VMEM)
SMEM = pl.BlockSpec(memory_space=pltpu.SMEM)


def store_pieces(out_ref, value):
    half = value.shape[0] // 2
    for r in range(2):
        for l in range(2):
            out_ref[2 * r + l] = value[r * half : (r + 1) * half, l * 128 : (l + 1) * 128]


def load_pieces(ref):
    rows = [jnp.concatenate([ref[2 * r], ref[2 * r + 1]], axis=1) for r in range(2)]
    return jnp.concatenate(rows, axis=0)


def piece_shape(rows, width):
    return (rows // BLOCK * 4, width // 2, BLOCK // 2)


def piece_spec(width):
    return pl.BlockSpec((4, width // 2, BLOCK // 2), lambda i: (i, 0, 0))


def low_kernel(x_ref, down_ref, out_ref, x_held, down_held, out_held, sems, out_sems):
    count = x_ref.shape[0] // BLOCK
    first = pltpu.make_async_copy(down_ref, down_held, sems.at[count])
    first.start()
    copies, results = [], []
    for c in range(count):
        rows = pl.ds(c * BLOCK, BLOCK)
        copies.append(pltpu.make_async_copy(x_ref.at[rows], x_held.at[rows], sems.at[c]))
        copies[c].start()
    first.wait()
    for c in range(count):
        copies[c].wait()
        part = dot_nt(down_held[...], x_held[c * BLOCK : (c + 1) * BLOCK, :]).astype(BF16)
        pieces = pl.ds(4 * c, 4)
        store_pieces(out_held.at[pieces], part)
        results.append(pltpu.make_async_copy(out_held.at[pieces], out_ref.at[pieces], out_sems.at[c]))
        results[c].start()
    for result in results:
        result.wait()


def partial_low(x, down):
    rows, _ = x.shape
    far = pl.BlockSpec(memory_space=pltpu.HBM)
    shape = piece_shape(rows, down.shape[0])
    return pl.pallas_call(
        low_kernel,
        out_shape=jax.ShapeDtypeStruct(shape, BF16),
        in_specs=[far, far],
        out_specs=far,
        scratch_shapes=[
            pltpu.VMEM(x.shape, BF16),
            pltpu.VMEM(down.shape, BF16),
            pltpu.VMEM(shape, BF16),
            pltpu.SemaphoreType.DMA((rows // BLOCK + 1,)),
            pltpu.SemaphoreType.DMA((rows // BLOCK,)),
        ],
        compiler_params=params(),
        name="partial_low",
    )(*(pltpu.with_memory_space_constraint(a, pltpu.HBM) for a in (x, down)))


def sum_spread_kernel(in_ref, out_ref, held, sems):
    count = in_ref.shape[0]
    total = in_ref[0].astype(F32)
    for i in range(1, count):
        total = total + in_ref[i].astype(F32)
    held[...] = total.astype(BF16)
    copies = [pltpu.make_async_copy(held, out_ref.at[i], sems.at[i]) for i in range(count)]
    for copy in copies:
        copy.start()
    for copy in copies:
        copy.wait()


def exchange(pieces):
    return lax.all_to_all(pieces, ("z", "x"), 0, 0)


def sum_spread(pieces):
    return pl.pallas_call(
        sum_spread_kernel,
        out_shape=jax.ShapeDtypeStruct(pieces.shape, BF16),
        in_specs=[VMEM],
        out_specs=pl.BlockSpec(memory_space=pltpu.HBM),
        scratch_shapes=[
            pltpu.VMEM(pieces.shape[1:], BF16),
            pltpu.SemaphoreType.DMA((pieces.shape[0],)),
        ],
        compiler_params=params(),
        name="sum_spread",
    )(pieces)


def decay_kernel(meta_ref, decay_ref, start_ref, row_ref, col_ref, pass_ref):
    heads, rows = decay_ref.shape
    live = meta_ref[0]
    slot = lax.broadcasted_iota(jnp.int32, (1, rows), 1)
    keep = slot < live
    decay = jnp.where(keep, decay_ref[...].astype(F32), 0.0)
    starts = jnp.where(keep, start_ref[...].astype(F32), 0.0)
    both = jnp.concatenate([decay, starts, jnp.zeros((8 - heads - 1, rows), F32)], axis=0)
    both = both.astype(BF16)
    row_i = lax.broadcasted_iota(jnp.int32, (CHUNK, CHUNK), 0)
    col_i = lax.broadcasted_iota(jnp.int32, (CHUNK, CHUNK), 1)
    upper = jnp.where(row_i <= col_i, 1.0, 0.0).astype(BF16)
    lower = jnp.where(row_i >= col_i, 1.0, 0.0).astype(BF16)
    count = rows // CHUNK
    enters, leaves, passes = [], [], []
    prefix = jnp.ones((heads, 128), F32)
    for c in range(count):
        span = slice(c * CHUNK, (c + 1) * CHUNK)
        piece = both[:, span]
        by_row = dot_nn(piece, upper)
        by_col = dot_nt(lower, piece)
        here = keep[:, span]
        here_col = c * CHUNK + lax.broadcasted_iota(jnp.int32, (CHUNK, 1), 0) < live
        head_row = lax.broadcasted_iota(jnp.int32, (8, CHUNK), 0)
        head_lane = lax.broadcasted_iota(jnp.int32, (CHUNK, 8), 1)
        row_ref[0:8, span] = jnp.where(here | (head_row != heads), by_row, -1.0)
        end_row = by_row[:, CHUNK - 1 : CHUNK]
        row_seg = by_row[heads : heads + 1]
        row_ref[ROW_ENTER : ROW_ENTER + heads, span] = jnp.where(
            (row_seg == 0.0) & here, jnp.exp(by_row[:heads]), 0.0
        )
        row_ref[ROW_LEAVE : ROW_LEAVE + heads, span] = jnp.where(
            (row_seg == end_row[heads : heads + 1]) & here, jnp.exp(end_row[:heads] - by_row[:heads]), 0.0
        )
        col_ref[span, 0:8] = jnp.where(here_col | (head_lane != heads), by_col, -2.0)
        cum = by_col[:, :heads]
        seg = by_col[:, heads : heads + 1]
        cum_end = by_col[CHUNK - 1 : CHUNK, :heads]
        seg_end = by_col[CHUNK - 1 : CHUNK, heads : heads + 1]
        may_enter = (seg == 0.0) & here_col
        may_leave = (seg == seg_end) & here_col
        enter = jnp.where(may_enter, jnp.exp(cum), 0.0)
        leave = jnp.where(may_leave, jnp.exp(cum_end - cum), 0.0)
        col_ref[span, ENTER_SHUT : ENTER_SHUT + 1] = jnp.where(may_enter, 0.0, NEGATIVE)
        col_ref[span, LEAVE_SHUT : LEAVE_SHUT + 1] = jnp.where(may_leave, 0.0, NEGATIVE)
        col_ref[span, ENTER : ENTER + heads] = enter
        col_ref[span, LEAVE : LEAVE + heads] = leave
        enters.append(enter)
        leaves.append(leave)
        passes.append(jnp.where(seg_end == 0.0, jnp.exp(cum_end), 0.0))
        passing_col = jnp.where(end_row[heads : heads + 1] == 0.0, jnp.exp(end_row[:heads]), 0.0)
        passing_rows_here = jnp.broadcast_to(passing_col, (heads, 128))
        pass_ref[c * heads : (c + 1) * heads, :] = passing_rows_here
        first = (count + c) * heads
        pass_ref[first : first + heads, :] = prefix
        first = (2 * count + c) * heads
        pass_ref[first : first + heads, :] = jnp.broadcast_to(end_row[:heads], (heads, 128))
        prefix = prefix * passing_rows_here
    before = jnp.ones((1, heads), F32)
    for c in range(count):
        span = slice(c * CHUNK, (c + 1) * CHUNK)
        col_ref[span, ENTER_ALL : ENTER_ALL + heads] = enters[c] * before
        before = before * passes[c]
    after = jnp.ones((1, heads), F32)
    for c in reversed(range(count)):
        span = slice(c * CHUNK, (c + 1) * CHUNK)
        col_ref[span, LEAVE_ALL : LEAVE_ALL + heads] = leaves[c] * after
        after = after * passes[c]


def decay_tables(meta, decay, starts):
    heads, rows = decay.shape
    count = rows // CHUNK
    return pl.pallas_call(
        decay_kernel,
        out_shape=(
            jax.ShapeDtypeStruct((16, rows), F32),
            jax.ShapeDtypeStruct((rows, 128), F32),
            jax.ShapeDtypeStruct((3 * count * heads, 128), F32),
        ),
        in_specs=[SMEM, VMEM, VMEM],
        out_specs=(VMEM, VMEM, VMEM),
        compiler_params=params(),
        cost_estimate=cost(4e9, 1e6),
        name="decay_tables",
    )(meta, decay, starts.reshape(1, rows))


def project_kernel(
    frozen_ref, low_ref, up_ref, grad_ref, row_ref, pass_ref,
    moving_ref, before_ref, after_ref, summary_ref, returning, held, sems,
):
    chunks = returning.shape[0]
    rank = up_ref.shape[1]
    features = frozen_ref.shape[2]
    heads = features // 128
    size = heads * 128
    copies = []
    for n in range(frozen_ref.shape[1] // BLOCK):
        rows = pl.ds(n * BLOCK, BLOCK)
        copies.append(pltpu.make_async_copy(frozen_ref.at[:, rows], held.at[:, rows], sems.at[n]))
    for copy in copies[:2]:
        copy.start()
    states = [jnp.zeros((128, 128), F32)] * heads
    for n, copy in enumerate(copies):
        low = load_pieces(low_ref.at[pl.ds(4 * n, 4)])
        lifted = [dot_tn(low[i * rank : (i + 1) * rank, :], up_ref[i]) for i in range(3)]
        copy.wait()
        if n + 2 < len(copies):
            copies[n + 2].start()
        rows = pl.ds(n * BLOCK, BLOCK)
        for i in range(3):
            moving_ref[i, rows, :] = (held[i, rows, :].astype(F32) + lifted[i]).astype(BF16)
        for c in range(n * BLOCK // CHUNK, (n + 1) * BLOCK // CHUNK):
            rows = pl.ds(c * CHUNK, CHUNK)
            for h in range(heads):
                span = slice(h * 128, (h + 1) * 128)
                passing = pass_ref[c * heads + h : c * heads + h + 1, :]
                leave = row_ref[ROW_LEAVE + h : ROW_LEAVE + h + 1, rows]
                enter = row_ref[ROW_ENTER + h : ROW_ENTER + h + 1, rows]
                valued = (moving_ref[2, rows, span].T.astype(F32) * leave).astype(BF16)
                scaled = (moving_ref[0, rows, span].T.astype(F32) * enter).astype(BF16)
                before_ref[c, h] = states[h].astype(BF16)
                states[h] = passing * states[h] + dot_nn(valued, moving_ref[1, rows, span])
                returning[c, h] = dot_nn(scaled, grad_ref[rows, span])
    for h in range(heads):
        back = jnp.zeros((128, 128), F32)
        whole = jnp.ones((1, 128), F32)
        for c in reversed(range(chunks)):
            passing = pass_ref[c * heads + h : c * heads + h + 1, :]
            after_ref[c, h] = back.astype(BF16)
            back = passing * back + returning[c, h]
            whole = whole * passing
        summary_ref[h * 128 : (h + 1) * 128, :] = states[h].astype(BF16)
        summary_ref[size + h * 128 : size + (h + 1) * 128, :] = back.astype(BF16)
        summary_ref[2 * size + 16 * h : 2 * size + 16 * h + 16, :] = passing_rows(whole)


def passing_rows(row):
    first = row.astype(BF16).astype(F32)
    rest = row - first
    second = rest.astype(BF16).astype(F32)
    third = (rest - second).astype(BF16).astype(F32)
    return jnp.concatenate([first, second, third, jnp.zeros((13, 128), F32)], axis=0).astype(BF16)


def project(frozen, low, up, grad, row, passes):
    _, rows, features = frozen.shape
    heads = features // 128
    count = rows // CHUNK
    summary_rows = 2 * features + 16 * heads
    states = jax.ShapeDtypeStruct((count, heads, 128, 128), BF16)
    return pl.pallas_call(
        project_kernel,
        out_shape=(
            jax.ShapeDtypeStruct((3, rows, features), BF16),
            states,
            states,
            jax.ShapeDtypeStruct((summary_rows, 128), BF16),
        ),
        in_specs=[pl.BlockSpec(memory_space=pltpu.HBM)] + [VMEM] * 5,
        out_specs=(VMEM,) * 4,
        scratch_shapes=[
            pltpu.VMEM(states.shape, F32),
            pltpu.VMEM(frozen.shape, BF16),
            pltpu.SemaphoreType.DMA((rows // BLOCK,)),
        ],
        compiler_params=params(),
        cost_estimate=cost(4e9, 10e6),
        name="project",
    )(pltpu.with_memory_space_constraint(frozen, pltpu.HBM), low, up, grad, row, passes)


def passing_of(ref, base):
    return (
        ref[base : base + 1, :].astype(F32)
        + ref[base + 1 : base + 2, :].astype(F32)
        + ref[base + 2 : base + 3, :].astype(F32)
    )


def join_kernel(meta_ref, own_ref, mate_ref, *out_refs):
    y = meta_ref[1]
    core = meta_ref[2]
    total = own_ref.shape[0]
    heads = total // (2 * 128 + 16)
    size = heads * 128
    chips = len(out_refs) + 1
    second = core == 1
    for h in range(heads):
        rows = slice(h * 128, (h + 1) * 128)
        back_rows = slice(size + h * 128, size + (h + 1) * 128)
        base = 2 * size + 16 * h
        own_pass = passing_of(own_ref, base)
        mate_pass = passing_of(mate_ref, base)
        own_state = own_ref[rows, :].astype(F32)
        mate_state = mate_ref[rows, :].astype(F32)
        own_back = own_ref[back_rows, :].astype(F32)
        mate_back = mate_ref[back_rows, :].astype(F32)
        one = jnp.ones_like(own_pass)
        state = jnp.where(second, own_pass, one) * mate_state + jnp.where(second, one, mate_pass) * own_state
        back = jnp.where(second, one, own_pass) * mate_back + jnp.where(second, mate_pass, one) * own_back
        tail = passing_rows(own_pass * mate_pass)
        for k, out_ref in enumerate(out_refs):
            later = y + (k + 1) < chips
            out_ref[rows, :] = jnp.where(later, state, back).astype(BF16)
            out_ref[size + 16 * h : size + 16 * h + 16, :] = tail


def join(meta, own, mate, chips):
    heads = own.shape[0] // (2 * 128 + 16)
    message = jax.ShapeDtypeStruct((heads * (128 + 16), 128), BF16)
    return pl.pallas_call(
        join_kernel,
        out_shape=(message,) * (chips - 1),
        in_specs=[SMEM, VMEM, VMEM],
        out_specs=(VMEM,) * (chips - 1),
        compiler_params=params(),
        name="join",
    )(meta, own, mate)


def inside_kernel(moving_ref, grad_ref, row_ref, col_ref, pass_ref, before_ref, after_ref, part_ref):
    features = moving_ref.shape[2]
    heads = features // 128
    square = (CHUNK, CHUNK)
    row_i = lax.broadcasted_iota(jnp.int32, square, 0)
    col_i = lax.broadcasted_iota(jnp.int32, square, 1)
    end_base = pass_ref.shape[0] // 3 * 2

    def paired(make, h):
        return jnp.concatenate([make(h), make(h + 1)], axis=1)

    @pl.loop(0, moving_ref.shape[1] // CHUNK, unroll=UNROLL)
    def _(c):
        rows = chunk_rows(c)
        col = col_ref[rows, :]
        row = row_ref[0:8, rows]
        same = col[:, SEG : SEG + 1] == row[SEG : SEG + 1, :]
        shut = jnp.where(same & (row_i <= col_i), 0.0, NEGATIVE)
        shut_turned = jnp.where(same & (row_i >= col_i), 0.0, NEGATIVE)
        enter_shut = jnp.broadcast_to(col[:, ENTER_SHUT : ENTER_SHUT + 1], square)
        leave_shut = jnp.broadcast_to(col[:, LEAVE_SHUT : LEAVE_SHUT + 1], square)
        sums = [jnp.broadcast_to(col[:, h : h + 1], square) for h in range(heads)]
        ends = pass_ref[pl.ds(end_base + c * heads, heads), :]
        for h in range(0, heads, 2):
            span = slice(h * 128, (h + 2) * 128)
            q = moving_ref[0, rows, span]
            k = moving_ref[1, rows, span]
            v = moving_ref[2, rows, span]
            g = grad_ref[rows, span]
            weights = paired(lambda i: jnp.exp((row[i : i + 1, :] - sums[i]) + shut), h)
            turned = paired(lambda i: jnp.exp((sums[i] - row[i : i + 1, :]) + shut_turned), h)
            enter = paired(lambda i: jnp.exp(sums[i] + enter_shut), h)
            leave = paired(lambda i: jnp.exp((ends[i : i + 1, :] - sums[i]) + leave_shut), h)
            queries = diagonal_of(q)
            cotangents = diagonal_of(g)
            before = diagonal(before_ref[c, h], before_ref[c, h + 1])
            after = diagonal(after_ref[c, h], after_ref[c, h + 1])
            a = (pair_nt(k, q) * weights).astype(BF16)
            b = (pair_nt(v, g) * weights).astype(BF16)
            b_turned = (pair_nt(g, v) * turned).astype(BF16)
            part_ref[0, rows, span] = dot_nn(b_turned, diagonal_of(k)) + enter * dot_nn(g, before)
            part_ref[1, rows, span] = dot_nn(b, queries) + leave * dot_nt(v, after)
            part_ref[2, rows, span] = dot_nn(a, cotangents) + leave * dot_nn(k, after)


def inside(moving, grad, row, col, passes, before, after):
    return pl.pallas_call(
        inside_kernel,
        out_shape=jax.ShapeDtypeStruct(moving.shape, F32),
        in_specs=[VMEM] * 7,
        out_specs=VMEM,
        compiler_params=params(),
        cost_estimate=cost(12e9, 12e6),
        name="inside",
    )(moving, grad, row, col, passes, before, after)


def late_kernel(
    moving_ref, row_ref, col_ref, pass_ref, before_ref, state_ref, out_ref,
    held, before_held, attn, sems, before_sems, out_sems,
):
    features = moving_ref.shape[2]
    heads = features // 128
    inverse = 1.0 / 128.0
    prefix_base = pass_ref.shape[0] // 3
    square = (CHUNK, CHUNK)
    row_i = lax.broadcasted_iota(jnp.int32, square, 0)
    col_i = lax.broadcasted_iota(jnp.int32, square, 1)
    per_block = BLOCK // CHUNK
    copies, results = [], []
    for n in range(moving_ref.shape[1] // BLOCK):
        rows = pl.ds(n * BLOCK, BLOCK)
        chunks = pl.ds(n * per_block, per_block)
        copies.append(pltpu.make_async_copy(moving_ref.at[:, rows], held.at[:, rows], sems.at[n]))
        copies.append(
            pltpu.make_async_copy(before_ref.at[chunks], before_held.at[chunks], before_sems.at[n])
        )
    for copy in copies[:4]:
        copy.start()
    for n in range(moving_ref.shape[1] // BLOCK):
        copies[2 * n].wait()
        copies[2 * n + 1].wait()
        for copy in copies[2 * n + 4 : 2 * n + 6]:
            copy.start()
        for c in range(n * per_block, (n + 1) * per_block):
            rows = pl.ds(c * CHUNK, CHUNK)
            col = col_ref[rows, :]
            row = row_ref[0:8, rows]
            same = col[:, SEG : SEG + 1] == row[SEG : SEG + 1, :]
            shut = jnp.where(same & (row_i >= col_i), 0.0, NEGATIVE)
            enter_shut = jnp.broadcast_to(col[:, ENTER_SHUT : ENTER_SHUT + 1], square)
            for h in range(0, heads, 2):
                span = slice(h * 128, (h + 2) * 128)
                q = held[0, rows, span]
                k = held[1, rows, span]
                weights, enter, states = [], [], []
                for i in (h, h + 1):
                    sums = jnp.broadcast_to(col[:, i : i + 1], square)
                    weights.append(jnp.exp((sums - row[i : i + 1, :]) + shut))
                    enter.append(jnp.exp(sums + enter_shut))
                    first = prefix_base + c * heads + i
                    prefix = pass_ref[first : first + 1, :]
                    state = before_held[c, i].astype(F32) + prefix * state_ref[i].astype(F32)
                    states.append(state.astype(BF16))
                a = (pair_nt(q, k) * jnp.concatenate(weights, axis=1)).astype(BF16)
                carried = jnp.concatenate(
                    [dot_nt(q[:, :128], states[0]), dot_nt(q[:, 128:], states[1])], axis=1
                )
                out = dot_nn(a, diagonal_of(held[2, rows, span]))
                out = out + jnp.concatenate(enter, axis=1) * carried
                attn[rows, span] = (out * inverse).astype(BF16)
        rows = pl.ds(n * BLOCK, BLOCK)
        results.append(pltpu.make_async_copy(attn.at[rows], out_ref.at[rows], out_sems.at[n]))
        results[n].start()
    for result in results:
        result.wait()


def late(moving, row, col, passes, before, state):
    _, rows, features = moving.shape
    moving, before = (pltpu.with_memory_space_constraint(a, pltpu.HBM) for a in (moving, before))
    far = pl.BlockSpec(memory_space=pltpu.HBM)
    blocks = rows // BLOCK
    return pl.pallas_call(
        late_kernel,
        out_shape=jax.ShapeDtypeStruct((rows, features), BF16),
        in_specs=[far, VMEM, VMEM, VMEM, far, VMEM],
        out_specs=far,
        scratch_shapes=[
            pltpu.VMEM(moving.shape, BF16),
            pltpu.VMEM(before.shape, BF16),
            pltpu.VMEM((rows, features), BF16),
            pltpu.SemaphoreType.DMA((blocks,)),
            pltpu.SemaphoreType.DMA((blocks,)),
            pltpu.SemaphoreType.DMA((blocks,)),
        ],
        compiler_params=params(),
        cost_estimate=cost(6e9, 6e6),
        name="late",
    )(moving, row, col, passes, before, state)


def store_halves(core, total, keep_ref, send_ref):
    half = total.shape[0] // 2
    keep_ref[...] = total[pl.ds(pl.multiple_of(core * half, 16), half), :].astype(BF16)
    send_ref[...] = total[pl.ds(pl.multiple_of((1 - core) * half, 16), half), :].astype(BF16)


def finish_kernel(
    chips, meta_ref, moving_ref, g_ref, part_ref, col_ref, low_ref, up_ref, mate_ref, *refs
):
    message_refs = refs[: chips - 1]
    out_ref, low_grad_ref, state_in, keep_ref, send_ref = refs[chips - 1 : chips + 4]
    back_in, grad_ref, total, sems = refs[chips + 4 :]
    rank = up_ref.shape[1]
    features = moving_ref.shape[2]
    heads = features // 128
    size = heads * 128
    count = moving_ref.shape[1] // BLOCK
    inverse = 1.0 / 128.0
    y = meta_ref[1]
    second = meta_ref[2] == 1
    for h in range(heads):
        rows = slice(h * 128, (h + 1) * 128)
        factor = jnp.ones((1, 128), F32)
        state = jnp.zeros((128, 128), F32)
        for k in range(1, chips):
            ref = message_refs[k - 1]
            state = state + jnp.where(k <= y, factor, 0.0) * ref[rows, :].astype(F32)
            factor = factor * passing_of(ref, size + 16 * h)
        factor = jnp.ones((1, 128), F32)
        back = jnp.zeros((128, 128), F32)
        for k in reversed(range(1, chips)):
            ref = message_refs[k - 1]
            back = back + jnp.where(k > y, factor, 0.0) * ref[rows, :].astype(F32)
            factor = factor * passing_of(ref, size + 16 * h)
        mate_pass = passing_of(mate_ref, 2 * size + 16 * h)
        mate_state = mate_ref[rows, :].astype(F32)
        mate_back = mate_ref[size + h * 128 : size + (h + 1) * 128, :].astype(F32)
        state_in[h] = jnp.where(second, mate_pass * state + mate_state, state).astype(BF16)
        back_in[h] = jnp.where(second, back, mate_pass * back + mate_back).astype(BF16)
    copies = []
    for n in range(count):
        rows = pl.ds(n * BLOCK, BLOCK)
        col = col_ref[rows, :]
        for h in range(0, heads, 2):
            span = slice(h * 128, (h + 2) * 128)
            enter = widen(col, ENTER_ALL + h)
            leave = widen(col, LEAVE_ALL + h)
            state = diagonal(state_in[h], state_in[h + 1])
            back = diagonal(back_in[h], back_in[h + 1])
            query = part_ref[0, rows, span] + enter * dot_nn(g_ref[rows, span], state)
            key = part_ref[1, rows, span] + leave * dot_nt(moving_ref[2, rows, span], back)
            value = part_ref[2, rows, span] + leave * dot_nn(moving_ref[1, rows, span], back)
            for i, result in enumerate((query, key, value)):
                grad_ref[i, rows, span] = (result * inverse).astype(BF16)
        copies.append(pltpu.make_async_copy(grad_ref.at[:, rows], out_ref.at[:, rows], sems.at[n]))
        copies[n].start()
    for n in range(count):
        rows = pl.ds(n * BLOCK, BLOCK)
        low_grad = [dot_nt(up_ref[i], grad_ref[i, rows, :]).astype(BF16) for i in range(3)]
        store_pieces(low_grad_ref.at[pl.ds(4 * n, 4)], jnp.concatenate(low_grad, axis=0))
        low = load_pieces(low_ref.at[pl.ds(4 * n, 4)])
        for i in range(3):
            lanes = slice(i * rank, (i + 1) * rank)
            term = dot_nn(low[lanes, :], grad_ref[i, rows, :])
            total[lanes, :] = term if n == 0 else total[lanes, :] + term
    store_halves(meta_ref[2], total, keep_ref, send_ref)
    for copy in copies:
        copy.wait()


def finish(meta, moving, grad, part, col, low, up, mate, messages):
    _, rows, features = moving.shape
    heads = features // 128
    width = up.shape[0] * up.shape[1]
    half = jax.ShapeDtypeStruct((width // 2, features), BF16)
    chips = len(messages) + 1
    return pl.pallas_call(
        functools.partial(finish_kernel, chips),
        out_shape=(
            jax.ShapeDtypeStruct(moving.shape, BF16),
            jax.ShapeDtypeStruct(piece_shape(rows, width), BF16),
            jax.ShapeDtypeStruct((heads, 128, 128), BF16),
            half,
            half,
        ),
        in_specs=[SMEM] + [VMEM] * (7 + len(messages)),
        out_specs=(pl.BlockSpec(memory_space=pltpu.HBM),) + (VMEM,) * 4,
        scratch_shapes=[
            pltpu.VMEM((heads, 128, 128), BF16),
            pltpu.VMEM(moving.shape, BF16),
            pltpu.VMEM((width, features), F32),
            pltpu.SemaphoreType.DMA((rows // BLOCK,)),
        ],
        compiler_params=params(),
        cost_estimate=cost(4e9, 14e6),
        name="finish",
    )(meta, moving, grad, part, col, low, up, mate, *messages)


def down_kernel(meta_ref, x_ref, grad_ref, keep_ref, send_ref, total):
    value = jnp.zeros(total.shape, F32)
    for c in range(x_ref.shape[0] // BLOCK):
        low_grad = load_pieces(grad_ref.at[pl.ds(4 * c, 4)])
        value = value + dot_nn(low_grad, x_ref[c * BLOCK : (c + 1) * BLOCK, :])
    total[...] = value
    store_halves(meta_ref[2], total, keep_ref, send_ref)


def partial_down(meta, x, low_grad):
    width = 2 * low_grad.shape[1]
    half = jax.ShapeDtypeStruct((width // 2, x.shape[1]), BF16)
    return pl.pallas_call(
        down_kernel,
        out_shape=(half, half),
        in_specs=[SMEM, VMEM, VMEM],
        out_specs=(VMEM, VMEM),
        scratch_shapes=[pltpu.VMEM((width, x.shape[1]), F32)],
        compiler_params=params(),
        name="partial_down",
    )(meta, x, low_grad)


def halves_kernel(meta_ref, own_ref, mate_ref, out_ref):
    core = meta_ref[2]
    half = own_ref.shape[0]
    out_ref[pl.ds(pl.multiple_of(core * half, 8), half), :] = own_ref[...]
    out_ref[pl.ds(pl.multiple_of((1 - core) * half, 8), half), :] = mate_ref[...]


def join_halves(meta, own, mate):
    return pl.pallas_call(
        halves_kernel,
        out_shape=jax.ShapeDtypeStruct((2 * own.shape[0], own.shape[1]), F32),
        in_specs=[SMEM, VMEM, VMEM],
        out_specs=VMEM,
        compiler_params=params(),
        name="join_halves",
    )(meta, own, mate)


def add_kernel(*refs):
    total = refs[0][...].astype(F32)
    for ref in refs[1:-1]:
        total = total + ref[...].astype(F32)
    refs[-1][...] = total.astype(refs[-1].dtype)


def add_all(arrays, dtype):
    return pl.pallas_call(
        add_kernel,
        out_shape=jax.ShapeDtypeStruct(arrays[0].shape, dtype),
        in_specs=[VMEM] * len(arrays),
        out_specs=VMEM,
        compiler_params=params(),
        name="add_all",
    )(*arrays)


def to_mate(a):
    return lax.ppermute(a, "core", [(0, 1), (1, 0)])


def along_y(a, k):
    count = lax.axis_size("y")
    return lax.ppermute(a, "y", [(i, (i + k) % count) for i in range(count)])


def local(inputs, frozen, adapter_down, adapter_up, out_grad, log_decay, doc_start, lengths):
    y, core = lax.axis_index("y"), lax.axis_index("core")
    chips = lax.axis_size("y")
    rank = adapter_up.shape[1]
    meta = jnp.stack([lengths[2 * y + core], y, core]).astype(jnp.int32)
    down = jnp.swapaxes(adapter_down, 1, 2).reshape(3 * rank, inputs.shape[1])
    row, col, passes = decay_tables(meta, log_decay, doc_start)
    low = exchange(sum_spread(exchange(partial_low(inputs, down))))
    moving, before, after, summary = project(frozen, low, adapter_up, out_grad, row, passes)
    mate = to_mate(summary)
    messages = [along_y(m, k + 1) for k, m in enumerate(join(meta, summary, mate, chips))]
    part = inside(moving, out_grad, row, col, passes, before, after)
    grads, low_grad_part, state, up_keep, up_send = finish(
        meta, moving, out_grad, part, col, low, adapter_up, mate, messages
    )
    up_chip = add_all([up_keep, to_mate(up_send)], BF16)
    up_parts = [up_chip] + [along_y(up_chip, k) for k in range(1, chips)]
    pieces, up_chip = lax.optimization_barrier((exchange(low_grad_part), up_chip))
    attn = late(moving, row, col, passes, before, state)
    low_grad, attn, *up_parts = lax.optimization_barrier(
        [exchange(sum_spread(pieces)), attn] + up_parts
    )
    down_keep, down_send = partial_down(meta, inputs, low_grad)
    down_chip = add_all([down_keep, to_mate(down_send)], BF16)
    down_chip, *up_parts = lax.optimization_barrier([down_chip] + up_parts)
    down_parts = [down_chip] + [along_y(down_chip, k) for k in range(1, chips)]
    up_half = add_all(up_parts, F32)
    up_total = join_halves(meta, up_half, to_mate(up_half))
    up_total, *down_parts = lax.optimization_barrier([up_total] + down_parts)
    down_half = add_all(down_parts, F32)
    down_total = join_halves(meta, down_half, to_mate(down_half))
    down_total = jnp.swapaxes(down_total.reshape(3, rank, inputs.shape[1]), 1, 2)
    return (attn, grads, down_total, up_total.reshape(adapter_up.shape))


def solution(mesh):
    seq, head = mesh.shape["seq"], mesh.shape["head"]
    side = 1
    while side * side < head:
        side *= 2
    mesh = jax.sharding.Mesh(
        mesh.devices.reshape(seq // 2, 2, head // side, side), ("y", "core", "z", "x")
    )
    seq, head = ("y", "core"), ("z", "x")
    in_specs = (
        P(seq, head),
        P(None, seq, head),
        P(None, head, None),
        P(None, None, head),
        P(seq, head),
        P(head, seq),
        P(seq),
        P(),
    )
    out_specs = (
        P(seq, head),
        P(None, seq, head),
        P(None, head, None),
        P(None, None, head),
    )
    return jax.shard_map(local, mesh=mesh, in_specs=in_specs, out_specs=out_specs, check_vma=False)
```

```python
import functools

import jax
import jax.numpy as jnp
from jax import lax
from jax.experimental import pallas as pl
from jax.experimental.pallas import tpu as pltpu
from jax.sharding import PartitionSpec as P

F32 = jnp.float32
BF16 = jnp.bfloat16
CHUNK = 128
BLOCK = 256
VMEM_BYTES = 20 * 1024 * 1024
NEGATIVE = -1e30
UNROLL = 8

CUM, SEG, ENTER, LEAVE, ENTER_ALL, LEAVE_ALL, ENTER_SHUT, LEAVE_SHUT = 0, 4, 8, 12, 16, 20, 24, 25
ROW_ENTER, ROW_LEAVE = 8, 12


def dot_nn(a, b):
    return lax.dot_general(a, b, (((1,), (0,)), ((), ())), preferred_element_type=F32)


def dot_nt(a, b):
    return lax.dot_general(a, b, (((1,), (1,)), ((), ())), preferred_element_type=F32)


def dot_tn(a, b):
    return lax.dot_general(a, b, (((0,), (0,)), ((), ())), preferred_element_type=F32)


def params(limit=VMEM_BYTES, **more):
    return pltpu.CompilerParams(vmem_limit_bytes=limit, **more)


def chunk_rows(c):
    return pl.ds(pl.multiple_of(c * CHUNK, CHUNK), CHUNK)


def diagonal(a, b):
    zero = jnp.zeros_like(a)
    return jnp.concatenate(
        [jnp.concatenate([a, zero], axis=1), jnp.concatenate([zero, b], axis=1)], axis=0
    )


def diagonal_of(pair):
    return diagonal(pair[:, :128], pair[:, 128:])


def pair_nt(a, b):
    return jnp.concatenate(
        [dot_nt(a[:, :128], b[:, :128]), dot_nt(a[:, 128:], b[:, 128:])], axis=1
    )


def widen(table, lane):
    shape = (table.shape[0], 128)
    return jnp.concatenate(
        [jnp.broadcast_to(table[:, i : i + 1], shape) for i in (lane, lane + 1)], axis=1
    )


def cost(flops, moved):
    return pl.CostEstimate(flops=int(flops), bytes_accessed=int(moved), transcendentals=0)


VMEM = pl.BlockSpec(memory_space=pltpu.VMEM)
SMEM = pl.BlockSpec(memory_space=pltpu.SMEM)


def store_pieces(out_ref, value):
    half = value.shape[0] // 2
    for r in range(2):
        for l in range(2):
            out_ref[2 * r + l] = value[r * half : (r + 1) * half, l * 128 : (l + 1) * 128]


def load_pieces(ref):
    rows = [jnp.concatenate([ref[2 * r], ref[2 * r + 1]], axis=1) for r in range(2)]
    return jnp.concatenate(rows, axis=0)


def piece_shape(rows, width):
    return (rows // BLOCK * 4, width // 2, BLOCK // 2)


def piece_spec(width):
    return pl.BlockSpec((4, width // 2, BLOCK // 2), lambda i: (i, 0, 0))


def low_kernel(x_ref, down_ref, out_ref, x_held, down_held, out_held, sems, out_sems):
    count = x_ref.shape[0] // BLOCK
    first = pltpu.make_async_copy(down_ref, down_held, sems.at[count])
    first.start()
    copies, results = [], []
    for c in range(count):
        rows = pl.ds(c * BLOCK, BLOCK)
        copies.append(pltpu.make_async_copy(x_ref.at[rows], x_held.at[rows], sems.at[c]))
        copies[c].start()
    first.wait()
    for c in range(count):
        copies[c].wait()
        part = dot_nt(down_held[...], x_held[c * BLOCK : (c + 1) * BLOCK, :]).astype(BF16)
        pieces = pl.ds(4 * c, 4)
        store_pieces(out_held.at[pieces], part)
        results.append(pltpu.make_async_copy(out_held.at[pieces], out_ref.at[pieces], out_sems.at[c]))
        results[c].start()
    for result in results:
        result.wait()


def partial_low(x, down):
    rows, _ = x.shape
    far = pl.BlockSpec(memory_space=pltpu.HBM)
    shape = piece_shape(rows, down.shape[0])
    return pl.pallas_call(
        low_kernel,
        out_shape=jax.ShapeDtypeStruct(shape, BF16),
        in_specs=[far, far],
        out_specs=far,
        scratch_shapes=[
            pltpu.VMEM(x.shape, BF16),
            pltpu.VMEM(down.shape, BF16),
            pltpu.VMEM(shape, BF16),
            pltpu.SemaphoreType.DMA((rows // BLOCK + 1,)),
            pltpu.SemaphoreType.DMA((rows // BLOCK,)),
        ],
        compiler_params=params(),
        name="partial_low",
    )(*(pltpu.with_memory_space_constraint(a, pltpu.HBM) for a in (x, down)))


def sum_spread_kernel(in_ref, out_ref):
    count = in_ref.shape[0]
    total = in_ref[0].astype(F32)
    for i in range(1, count):
        total = total + in_ref[i].astype(F32)
    total = total.astype(BF16)
    for i in range(count):
        out_ref[i] = total


def exchange(pieces):
    return lax.all_to_all(pieces, ("z", "x"), 0, 0)


def sum_spread(pieces):
    return pl.pallas_call(
        sum_spread_kernel,
        out_shape=jax.ShapeDtypeStruct(pieces.shape, BF16),
        in_specs=[VMEM],
        out_specs=VMEM,
        compiler_params=params(),
        name="sum_spread",
    )(pieces)


def decay_kernel(meta_ref, decay_ref, start_ref, row_ref, col_ref, pass_ref):
    heads, rows = decay_ref.shape
    live = meta_ref[0]
    slot = lax.broadcasted_iota(jnp.int32, (1, rows), 1)
    keep = slot < live
    decay = jnp.where(keep, decay_ref[...].astype(F32), 0.0)
    starts = jnp.where(keep, start_ref[...].astype(F32), 0.0)
    both = jnp.concatenate([decay, starts, jnp.zeros((8 - heads - 1, rows), F32)], axis=0)
    both = both.astype(BF16)
    row_i = lax.broadcasted_iota(jnp.int32, (CHUNK, CHUNK), 0)
    col_i = lax.broadcasted_iota(jnp.int32, (CHUNK, CHUNK), 1)
    upper = jnp.where(row_i <= col_i, 1.0, 0.0).astype(BF16)
    lower = jnp.where(row_i >= col_i, 1.0, 0.0).astype(BF16)
    count = rows // CHUNK
    enters, leaves, passes = [], [], []
    prefix = jnp.ones((heads, 128), F32)
    for c in range(count):
        span = slice(c * CHUNK, (c + 1) * CHUNK)
        piece = both[:, span]
        by_row = dot_nn(piece, upper)
        by_col = dot_nt(lower, piece)
        here = keep[:, span]
        here_col = c * CHUNK + lax.broadcasted_iota(jnp.int32, (CHUNK, 1), 0) < live
        head_row = lax.broadcasted_iota(jnp.int32, (8, CHUNK), 0)
        head_lane = lax.broadcasted_iota(jnp.int32, (CHUNK, 8), 1)
        row_ref[0:8, span] = jnp.where(here | (head_row != heads), by_row, -1.0)
        end_row = by_row[:, CHUNK - 1 : CHUNK]
        row_seg = by_row[heads : heads + 1]
        row_ref[ROW_ENTER : ROW_ENTER + heads, span] = jnp.where(
            (row_seg == 0.0) & here, jnp.exp(by_row[:heads]), 0.0
        )
        row_ref[ROW_LEAVE : ROW_LEAVE + heads, span] = jnp.where(
            (row_seg == end_row[heads : heads + 1]) & here, jnp.exp(end_row[:heads] - by_row[:heads]), 0.0
        )
        col_ref[span, 0:8] = jnp.where(here_col | (head_lane != heads), by_col, -2.0)
        cum = by_col[:, :heads]
        seg = by_col[:, heads : heads + 1]
        cum_end = by_col[CHUNK - 1 : CHUNK, :heads]
        seg_end = by_col[CHUNK - 1 : CHUNK, heads : heads + 1]
        may_enter = (seg == 0.0) & here_col
        may_leave = (seg == seg_end) & here_col
        enter = jnp.where(may_enter, jnp.exp(cum), 0.0)
        leave = jnp.where(may_leave, jnp.exp(cum_end - cum), 0.0)
        col_ref[span, ENTER_SHUT : ENTER_SHUT + 1] = jnp.where(may_enter, 0.0, NEGATIVE)
        col_ref[span, LEAVE_SHUT : LEAVE_SHUT + 1] = jnp.where(may_leave, 0.0, NEGATIVE)
        col_ref[span, ENTER : ENTER + heads] = enter
        col_ref[span, LEAVE : LEAVE + heads] = leave
        enters.append(enter)
        leaves.append(leave)
        passes.append(jnp.where(seg_end == 0.0, jnp.exp(cum_end), 0.0))
        passing_col = jnp.where(end_row[heads : heads + 1] == 0.0, jnp.exp(end_row[:heads]), 0.0)
        passing_rows_here = jnp.broadcast_to(passing_col, (heads, 128))
        pass_ref[c * heads : (c + 1) * heads, :] = passing_rows_here
        first = (count + c) * heads
        pass_ref[first : first + heads, :] = prefix
        first = (2 * count + c) * heads
        pass_ref[first : first + heads, :] = jnp.broadcast_to(end_row[:heads], (heads, 128))
        prefix = prefix * passing_rows_here
    before = jnp.ones((1, heads), F32)
    for c in range(count):
        span = slice(c * CHUNK, (c + 1) * CHUNK)
        col_ref[span, ENTER_ALL : ENTER_ALL + heads] = enters[c] * before
        before = before * passes[c]
    after = jnp.ones((1, heads), F32)
    for c in reversed(range(count)):
        span = slice(c * CHUNK, (c + 1) * CHUNK)
        col_ref[span, LEAVE_ALL : LEAVE_ALL + heads] = leaves[c] * after
        after = after * passes[c]


def decay_tables(meta, decay, starts):
    heads, rows = decay.shape
    count = rows // CHUNK
    return pl.pallas_call(
        decay_kernel,
        out_shape=(
            jax.ShapeDtypeStruct((16, rows), F32),
            jax.ShapeDtypeStruct((rows, 128), F32),
            jax.ShapeDtypeStruct((3 * count * heads, 128), F32),
        ),
        in_specs=[SMEM, VMEM, VMEM],
        out_specs=(VMEM, VMEM, VMEM),
        compiler_params=params(),
        cost_estimate=cost(4e9, 1e6),
        name="decay_tables",
    )(meta, decay, starts.reshape(1, rows))


def project_kernel(
    frozen_ref, low_ref, up_ref, grad_ref, row_ref, pass_ref,
    moving_ref, before_ref, after_ref, summary_ref, returning, held, sems,
):
    chunks = returning.shape[0]
    rank = up_ref.shape[1]
    features = frozen_ref.shape[2]
    heads = features // 128
    size = heads * 128
    copies = []
    for n in range(frozen_ref.shape[1] // BLOCK):
        rows = pl.ds(n * BLOCK, BLOCK)
        copies.append(pltpu.make_async_copy(frozen_ref.at[:, rows], held.at[:, rows], sems.at[n]))
    for copy in copies[:2]:
        copy.start()
    states = [jnp.zeros((128, 128), F32)] * heads
    for n, copy in enumerate(copies):
        low = load_pieces(low_ref.at[pl.ds(4 * n, 4)])
        lifted = [dot_tn(low[i * rank : (i + 1) * rank, :], up_ref[i]) for i in range(3)]
        copy.wait()
        if n + 2 < len(copies):
            copies[n + 2].start()
        rows = pl.ds(n * BLOCK, BLOCK)
        for i in range(3):
            moving_ref[i, rows, :] = (held[i, rows, :].astype(F32) + lifted[i]).astype(BF16)
        for c in range(n * BLOCK // CHUNK, (n + 1) * BLOCK // CHUNK):
            rows = pl.ds(c * CHUNK, CHUNK)
            for h in range(heads):
                span = slice(h * 128, (h + 1) * 128)
                passing = pass_ref[c * heads + h : c * heads + h + 1, :]
                leave = row_ref[ROW_LEAVE + h : ROW_LEAVE + h + 1, rows]
                enter = row_ref[ROW_ENTER + h : ROW_ENTER + h + 1, rows]
                valued = (moving_ref[2, rows, span].T.astype(F32) * leave).astype(BF16)
                scaled = (moving_ref[0, rows, span].T.astype(F32) * enter).astype(BF16)
                before_ref[c, h] = states[h].astype(BF16)
                states[h] = passing * states[h] + dot_nn(valued, moving_ref[1, rows, span])
                returning[c, h] = dot_nn(scaled, grad_ref[rows, span])
    tails = []
    for h in range(heads):
        back = jnp.zeros((128, 128), F32)
        whole = jnp.ones((1, 128), F32)
        for c in reversed(range(chunks)):
            passing = pass_ref[c * heads + h : c * heads + h + 1, :]
            after_ref[c, h] = back.astype(BF16)
            back = passing * back + returning[c, h]
            whole = whole * passing
        summary_ref[h * 128 : (h + 1) * 128, :] = states[h].astype(BF16)
        summary_ref[size + h * 128 : size + (h + 1) * 128, :] = back.astype(BF16)
        tails.append(passing_rows(whole))
    summary_ref[2 * size : 2 * size + 4 * heads, :] = jnp.concatenate(tails, axis=0).astype(BF16)


def passing_rows(row):
    first = row.astype(BF16).astype(F32)
    rest = row - first
    second = rest.astype(BF16).astype(F32)
    third = (rest - second).astype(BF16).astype(F32)
    return jnp.concatenate([first, second, third, jnp.zeros((1, 128), F32)], axis=0)


def project(frozen, low, up, grad, row, passes):
    _, rows, features = frozen.shape
    heads = features // 128
    count = rows // CHUNK
    summary_rows = 2 * features + 4 * heads
    states = jax.ShapeDtypeStruct((count, heads, 128, 128), BF16)
    return pl.pallas_call(
        project_kernel,
        out_shape=(
            jax.ShapeDtypeStruct((3, rows, features), BF16),
            states,
            states,
            jax.ShapeDtypeStruct((summary_rows, 128), BF16),
        ),
        in_specs=[pl.BlockSpec(memory_space=pltpu.HBM)] + [VMEM] * 5,
        out_specs=(VMEM,) * 4,
        scratch_shapes=[
            pltpu.VMEM(states.shape, F32),
            pltpu.VMEM(frozen.shape, BF16),
            pltpu.SemaphoreType.DMA((rows // BLOCK,)),
        ],
        compiler_params=params(),
        cost_estimate=cost(4e9, 10e6),
        name="project",
    )(pltpu.with_memory_space_constraint(frozen, pltpu.HBM), low, up, grad, row, passes)


def passing_of(ref, base):
    return (
        ref[base : base + 1, :].astype(F32)
        + ref[base + 1 : base + 2, :].astype(F32)
        + ref[base + 2 : base + 3, :].astype(F32)
    )


def join_kernel(meta_ref, own_ref, mate_ref, *out_refs):
    y = meta_ref[1]
    core = meta_ref[2]
    total = own_ref.shape[0]
    heads = total // (2 * 128 + 4)
    size = heads * 128
    chips = len(out_refs) + 1
    second = core == 1
    tails = []
    for h in range(heads):
        rows = slice(h * 128, (h + 1) * 128)
        back_rows = slice(size + h * 128, size + (h + 1) * 128)
        base = 2 * size + 4 * h
        own_pass = passing_of(own_ref, base)
        mate_pass = passing_of(mate_ref, base)
        own_state = own_ref[rows, :].astype(F32)
        mate_state = mate_ref[rows, :].astype(F32)
        own_back = own_ref[back_rows, :].astype(F32)
        mate_back = mate_ref[back_rows, :].astype(F32)
        one = jnp.ones_like(own_pass)
        state = jnp.where(second, own_pass, one) * mate_state + jnp.where(second, one, mate_pass) * own_state
        back = jnp.where(second, one, own_pass) * mate_back + jnp.where(second, mate_pass, one) * own_back
        tails.append(passing_rows(own_pass * mate_pass))
        for k, out_ref in enumerate(out_refs):
            later = y + (k + 1) < chips
            out_ref[rows, :] = jnp.where(later, state, back).astype(BF16)
    tail = jnp.concatenate(tails, axis=0).astype(BF16)
    for out_ref in out_refs:
        out_ref[size : size + 4 * heads, :] = tail


def join(meta, own, mate, chips):
    heads = own.shape[0] // (2 * 128 + 4)
    message = jax.ShapeDtypeStruct((heads * (128 + 4), 128), BF16)
    return pl.pallas_call(
        join_kernel,
        out_shape=(message,) * (chips - 1),
        in_specs=[SMEM, VMEM, VMEM],
        out_specs=(VMEM,) * (chips - 1),
        compiler_params=params(),
        name="join",
    )(meta, own, mate)


def inside_kernel(moving_ref, grad_ref, row_ref, col_ref, pass_ref, before_ref, after_ref, part_ref):
    features = moving_ref.shape[2]
    heads = features // 128
    square = (CHUNK, CHUNK)
    row_i = lax.broadcasted_iota(jnp.int32, square, 0)
    col_i = lax.broadcasted_iota(jnp.int32, square, 1)
    end_base = pass_ref.shape[0] // 3 * 2

    def paired(make, h):
        return jnp.concatenate([make(h), make(h + 1)], axis=1)

    @pl.loop(0, moving_ref.shape[1] // CHUNK, unroll=UNROLL)
    def _(c):
        rows = chunk_rows(c)
        col = col_ref[rows, :]
        row = row_ref[0:8, rows]
        same = col[:, SEG : SEG + 1] == row[SEG : SEG + 1, :]
        shut = jnp.where(same & (row_i <= col_i), 0.0, NEGATIVE)
        shut_turned = jnp.where(same & (row_i >= col_i), 0.0, NEGATIVE)
        enter_shut = jnp.broadcast_to(col[:, ENTER_SHUT : ENTER_SHUT + 1], square)
        leave_shut = jnp.broadcast_to(col[:, LEAVE_SHUT : LEAVE_SHUT + 1], square)
        sums = [jnp.broadcast_to(col[:, h : h + 1], square) for h in range(heads)]
        ends = pass_ref[pl.ds(end_base + c * heads, heads), :]
        for h in range(0, heads, 2):
            span = slice(h * 128, (h + 2) * 128)
            q = moving_ref[0, rows, span]
            k = moving_ref[1, rows, span]
            v = moving_ref[2, rows, span]
            g = grad_ref[rows, span]
            weights = paired(lambda i: jnp.exp((row[i : i + 1, :] - sums[i]) + shut), h)
            turned = paired(lambda i: jnp.exp((sums[i] - row[i : i + 1, :]) + shut_turned), h)
            enter = paired(lambda i: jnp.exp(sums[i] + enter_shut), h)
            leave = paired(lambda i: jnp.exp((ends[i : i + 1, :] - sums[i]) + leave_shut), h)
            queries = diagonal_of(q)
            cotangents = diagonal_of(g)
            before = diagonal(before_ref[c, h], before_ref[c, h + 1])
            after = diagonal(after_ref[c, h], after_ref[c, h + 1])
            a = (pair_nt(k, q) * weights).astype(BF16)
            b = (pair_nt(v, g) * weights).astype(BF16)
            b_turned = (pair_nt(g, v) * turned).astype(BF16)
            part_ref[0, rows, span] = dot_nn(b_turned, diagonal_of(k)) + enter * dot_nn(g, before)
            part_ref[1, rows, span] = dot_nn(b, queries) + leave * dot_nt(v, after)
            part_ref[2, rows, span] = dot_nn(a, cotangents) + leave * dot_nn(k, after)


def inside(moving, grad, row, col, passes, before, after):
    return pl.pallas_call(
        inside_kernel,
        out_shape=jax.ShapeDtypeStruct(moving.shape, F32),
        in_specs=[VMEM] * 7,
        out_specs=VMEM,
        compiler_params=params(),
        cost_estimate=cost(12e9, 12e6),
        name="inside",
    )(moving, grad, row, col, passes, before, after)


def late_kernel(
    moving_ref, row_ref, col_ref, pass_ref, before_ref, state_ref, out_ref,
    held, before_held, attn, sems, before_sems, out_sems,
):
    features = moving_ref.shape[2]
    heads = features // 128
    inverse = 1.0 / 128.0
    prefix_base = pass_ref.shape[0] // 3
    square = (CHUNK, CHUNK)
    row_i = lax.broadcasted_iota(jnp.int32, square, 0)
    col_i = lax.broadcasted_iota(jnp.int32, square, 1)
    per_block = BLOCK // CHUNK
    copies, results = [], []
    for n in range(moving_ref.shape[1] // BLOCK):
        rows = pl.ds(n * BLOCK, BLOCK)
        chunks = pl.ds(n * per_block, per_block)
        copies.append(pltpu.make_async_copy(moving_ref.at[:, rows], held.at[:, rows], sems.at[n]))
        copies.append(
            pltpu.make_async_copy(before_ref.at[chunks], before_held.at[chunks], before_sems.at[n])
        )
    for copy in copies[:4]:
        copy.start()
    for n in range(moving_ref.shape[1] // BLOCK):
        copies[2 * n].wait()
        copies[2 * n + 1].wait()
        for copy in copies[2 * n + 4 : 2 * n + 6]:
            copy.start()
        for c in range(n * per_block, (n + 1) * per_block):
            rows = pl.ds(c * CHUNK, CHUNK)
            col = col_ref[rows, :]
            row = row_ref[0:8, rows]
            same = col[:, SEG : SEG + 1] == row[SEG : SEG + 1, :]
            shut = jnp.where(same & (row_i >= col_i), 0.0, NEGATIVE)
            enter_shut = jnp.broadcast_to(col[:, ENTER_SHUT : ENTER_SHUT + 1], square)
            for h in range(0, heads, 2):
                span = slice(h * 128, (h + 2) * 128)
                q = held[0, rows, span]
                k = held[1, rows, span]
                weights, enter, states = [], [], []
                for i in (h, h + 1):
                    sums = jnp.broadcast_to(col[:, i : i + 1], square)
                    weights.append(jnp.exp((sums - row[i : i + 1, :]) + shut))
                    enter.append(jnp.exp(sums + enter_shut))
                    first = prefix_base + c * heads + i
                    prefix = pass_ref[first : first + 1, :]
                    state = before_held[c, i].astype(F32) + prefix * state_ref[i].astype(F32)
                    states.append(state.astype(BF16))
                a = (pair_nt(q, k) * jnp.concatenate(weights, axis=1)).astype(BF16)
                carried = jnp.concatenate(
                    [dot_nt(q[:, :128], states[0]), dot_nt(q[:, 128:], states[1])], axis=1
                )
                out = dot_nn(a, diagonal_of(held[2, rows, span]))
                out = out + jnp.concatenate(enter, axis=1) * carried
                attn[rows, span] = (out * inverse).astype(BF16)
        rows = pl.ds(n * BLOCK, BLOCK)
        results.append(pltpu.make_async_copy(attn.at[rows], out_ref.at[rows], out_sems.at[n]))
        results[n].start()
    for result in results:
        result.wait()


def late(moving, row, col, passes, before, state):
    _, rows, features = moving.shape
    moving, before = (pltpu.with_memory_space_constraint(a, pltpu.HBM) for a in (moving, before))
    far = pl.BlockSpec(memory_space=pltpu.HBM)
    blocks = rows // BLOCK
    return pl.pallas_call(
        late_kernel,
        out_shape=jax.ShapeDtypeStruct((rows, features), BF16),
        in_specs=[far, VMEM, VMEM, VMEM, far, VMEM],
        out_specs=far,
        scratch_shapes=[
            pltpu.VMEM(moving.shape, BF16),
            pltpu.VMEM(before.shape, BF16),
            pltpu.VMEM((rows, features), BF16),
            pltpu.SemaphoreType.DMA((blocks,)),
            pltpu.SemaphoreType.DMA((blocks,)),
            pltpu.SemaphoreType.DMA((blocks,)),
        ],
        compiler_params=params(),
        cost_estimate=cost(6e9, 6e6),
        name="late",
    )(moving, row, col, passes, before, state)


def store_halves(core, total, keep_ref, send_ref):
    half = total.shape[0] // 2
    keep_ref[...] = total[pl.ds(pl.multiple_of(core * half, 16), half), :].astype(BF16)
    send_ref[...] = total[pl.ds(pl.multiple_of((1 - core) * half, 16), half), :].astype(BF16)


def finish_kernel(
    chips, meta_ref, moving_ref, g_ref, part_ref, col_ref, low_ref, up_ref, mate_ref, *refs
):
    message_refs = refs[: chips - 1]
    out_ref, low_grad_ref, state_in, keep_ref, send_ref = refs[chips - 1 : chips + 4]
    back_in, grad_ref, total, sems = refs[chips + 4 :]
    rank = up_ref.shape[1]
    features = moving_ref.shape[2]
    heads = features // 128
    size = heads * 128
    count = moving_ref.shape[1] // BLOCK
    inverse = 1.0 / 128.0
    y = meta_ref[1]
    second = meta_ref[2] == 1
    for h in range(heads):
        rows = slice(h * 128, (h + 1) * 128)
        factor = jnp.ones((1, 128), F32)
        state = jnp.zeros((128, 128), F32)
        for k in range(1, chips):
            ref = message_refs[k - 1]
            state = state + jnp.where(k <= y, factor, 0.0) * ref[rows, :].astype(F32)
            factor = factor * passing_of(ref, size + 4 * h)
        factor = jnp.ones((1, 128), F32)
        back = jnp.zeros((128, 128), F32)
        for k in reversed(range(1, chips)):
            ref = message_refs[k - 1]
            back = back + jnp.where(k > y, factor, 0.0) * ref[rows, :].astype(F32)
            factor = factor * passing_of(ref, size + 4 * h)
        mate_pass = passing_of(mate_ref, 2 * size + 4 * h)
        mate_state = mate_ref[rows, :].astype(F32)
        mate_back = mate_ref[size + h * 128 : size + (h + 1) * 128, :].astype(F32)
        state_in[h] = jnp.where(second, mate_pass * state + mate_state, state).astype(BF16)
        back_in[h] = jnp.where(second, back, mate_pass * back + mate_back).astype(BF16)
    copies = []
    for n in range(count):
        rows = pl.ds(n * BLOCK, BLOCK)
        col = col_ref[rows, :]
        for h in range(0, heads, 2):
            span = slice(h * 128, (h + 2) * 128)
            enter = widen(col, ENTER_ALL + h)
            leave = widen(col, LEAVE_ALL + h)
            state = diagonal(state_in[h], state_in[h + 1])
            back = diagonal(back_in[h], back_in[h + 1])
            query = part_ref[0, rows, span] + enter * dot_nn(g_ref[rows, span], state)
            key = part_ref[1, rows, span] + leave * dot_nt(moving_ref[2, rows, span], back)
            value = part_ref[2, rows, span] + leave * dot_nn(moving_ref[1, rows, span], back)
            for i, result in enumerate((query, key, value)):
                grad_ref[i, rows, span] = (result * inverse).astype(BF16)
        copies.append(pltpu.make_async_copy(grad_ref.at[:, rows], out_ref.at[:, rows], sems.at[n]))
        copies[n].start()
    for n in range(count):
        rows = pl.ds(n * BLOCK, BLOCK)
        low_grad = [dot_nt(up_ref[i], grad_ref[i, rows, :]).astype(BF16) for i in range(3)]
        store_pieces(low_grad_ref.at[pl.ds(4 * n, 4)], jnp.concatenate(low_grad, axis=0))
        low = load_pieces(low_ref.at[pl.ds(4 * n, 4)])
        for i in range(3):
            lanes = slice(i * rank, (i + 1) * rank)
            term = dot_nn(low[lanes, :], grad_ref[i, rows, :])
            total[lanes, :] = term if n == 0 else total[lanes, :] + term
    store_halves(meta_ref[2], total, keep_ref, send_ref)
    for copy in copies:
        copy.wait()


def finish(meta, moving, grad, part, col, low, up, mate, messages):
    _, rows, features = moving.shape
    heads = features // 128
    width = up.shape[0] * up.shape[1]
    half = jax.ShapeDtypeStruct((width // 2, features), BF16)
    chips = len(messages) + 1
    return pl.pallas_call(
        functools.partial(finish_kernel, chips),
        out_shape=(
            jax.ShapeDtypeStruct(moving.shape, BF16),
            jax.ShapeDtypeStruct(piece_shape(rows, width), BF16),
            jax.ShapeDtypeStruct((heads, 128, 128), BF16),
            half,
            half,
        ),
        in_specs=[SMEM] + [VMEM] * (7 + len(messages)),
        out_specs=(pl.BlockSpec(memory_space=pltpu.HBM),) + (VMEM,) * 4,
        scratch_shapes=[
            pltpu.VMEM((heads, 128, 128), BF16),
            pltpu.VMEM(moving.shape, BF16),
            pltpu.VMEM((width, features), F32),
            pltpu.SemaphoreType.DMA((rows // BLOCK,)),
        ],
        compiler_params=params(),
        cost_estimate=cost(4e9, 14e6),
        name="finish",
    )(meta, moving, grad, part, col, low, up, mate, *messages)


def down_kernel(meta_ref, x_ref, grad_ref, keep_ref, send_ref, total):
    value = jnp.zeros(total.shape, F32)
    for c in range(x_ref.shape[0] // BLOCK):
        low_grad = load_pieces(grad_ref.at[pl.ds(4 * c, 4)])
        value = value + dot_nn(low_grad, x_ref[c * BLOCK : (c + 1) * BLOCK, :])
    total[...] = value
    store_halves(meta_ref[2], total, keep_ref, send_ref)


def partial_down(meta, x, low_grad):
    width = 2 * low_grad.shape[1]
    half = jax.ShapeDtypeStruct((width // 2, x.shape[1]), BF16)
    return pl.pallas_call(
        down_kernel,
        out_shape=(half, half),
        in_specs=[SMEM, VMEM, VMEM],
        out_specs=(VMEM, VMEM),
        scratch_shapes=[pltpu.VMEM((width, x.shape[1]), F32)],
        compiler_params=params(),
        name="partial_down",
    )(meta, x, low_grad)


def halves_kernel(meta_ref, own_ref, mate_ref, out_ref):
    core = meta_ref[2]
    half = own_ref.shape[0]
    out_ref[pl.ds(pl.multiple_of(core * half, 8), half), :] = own_ref[...]
    out_ref[pl.ds(pl.multiple_of((1 - core) * half, 8), half), :] = mate_ref[...]


def join_halves(meta, own, mate):
    return pl.pallas_call(
        halves_kernel,
        out_shape=jax.ShapeDtypeStruct((2 * own.shape[0], own.shape[1]), F32),
        in_specs=[SMEM, VMEM, VMEM],
        out_specs=VMEM,
        compiler_params=params(),
        name="join_halves",
    )(meta, own, mate)


def add_kernel(*refs):
    total = refs[0][...].astype(F32)
    for ref in refs[1:-1]:
        total = total + ref[...].astype(F32)
    refs[-1][...] = total.astype(refs[-1].dtype)


def add_all(arrays, dtype):
    return pl.pallas_call(
        add_kernel,
        out_shape=jax.ShapeDtypeStruct(arrays[0].shape, dtype),
        in_specs=[VMEM] * len(arrays),
        out_specs=VMEM,
        compiler_params=params(),
        name="add_all",
    )(*arrays)


def to_mate(a):
    return lax.ppermute(a, "core", [(0, 1), (1, 0)])


def along_y(a, k):
    count = lax.axis_size("y")
    return lax.ppermute(a, "y", [(i, (i + k) % count) for i in range(count)])


def local(inputs, frozen, adapter_down, adapter_up, out_grad, log_decay, doc_start, lengths):
    y, core = lax.axis_index("y"), lax.axis_index("core")
    chips = lax.axis_size("y")
    rank = adapter_up.shape[1]
    meta = jnp.stack([lengths[2 * y + core], y, core]).astype(jnp.int32)
    down = jnp.swapaxes(adapter_down, 1, 2).reshape(3 * rank, inputs.shape[1])
    row, col, passes = decay_tables(meta, log_decay, doc_start)
    low = exchange(sum_spread(exchange(partial_low(inputs, down))))
    moving, before, after, summary = project(frozen, low, adapter_up, out_grad, row, passes)
    mate = to_mate(summary)
    messages = [along_y(m, k + 1) for k, m in enumerate(join(meta, summary, mate, chips))]
    part = inside(moving, out_grad, row, col, passes, before, after)
    grads, low_grad_part, state, up_keep, up_send = finish(
        meta, moving, out_grad, part, col, low, adapter_up, mate, messages
    )
    up_chip = add_all([up_keep, to_mate(up_send)], BF16)
    up_parts = [up_chip] + [along_y(up_chip, k) for k in range(1, chips)]
    pieces, up_chip = lax.optimization_barrier((exchange(low_grad_part), up_chip))
    attn = late(moving, row, col, passes, before, state)
    low_grad, attn, *up_parts = lax.optimization_barrier(
        [exchange(sum_spread(pieces)), attn] + up_parts
    )
    down_keep, down_send = partial_down(meta, inputs, low_grad)
    down_chip = add_all([down_keep, to_mate(down_send)], BF16)
    down_chip, *up_parts = lax.optimization_barrier([down_chip] + up_parts)
    down_parts = [down_chip] + [along_y(down_chip, k) for k in range(1, chips)]
    up_half = add_all(up_parts, F32)
    up_total = join_halves(meta, up_half, to_mate(up_half))
    up_total, *down_parts = lax.optimization_barrier([up_total] + down_parts)
    down_half = add_all(down_parts, F32)
    down_total = join_halves(meta, down_half, to_mate(down_half))
    down_total = jnp.swapaxes(down_total.reshape(3, rank, inputs.shape[1]), 1, 2)
    return (attn, grads, down_total, up_total.reshape(adapter_up.shape))


def solution(mesh):
    seq, head = mesh.shape["seq"], mesh.shape["head"]
    side = 1
    while side * side < head:
        side *= 2
    mesh = jax.sharding.Mesh(
        mesh.devices.reshape(seq // 2, 2, head // side, side), ("y", "core", "z", "x")
    )
    seq, head = ("y", "core"), ("z", "x")
    in_specs = (
        P(seq, head),
        P(None, seq, head),
        P(None, head, None),
        P(None, None, head),
        P(seq, head),
        P(head, seq),
        P(seq),
        P(),
    )
    out_specs = (
        P(seq, head),
        P(None, seq, head),
        P(None, head, None),
        P(None, None, head),
    )
    return jax.shard_map(local, mesh=mesh, in_specs=in_specs, out_specs=out_specs, check_vma=False)
```

```python
import functools

import jax
import jax.numpy as jnp
from jax import lax
from jax.experimental import pallas as pl
from jax.experimental.pallas import tpu as pltpu
from jax.sharding import PartitionSpec as P

F32 = jnp.float32
BF16 = jnp.bfloat16
CHUNK = 128
BLOCK = 256
VMEM_BYTES = 20 * 1024 * 1024
NEGATIVE = -1e30
UNROLL = 8

CUM, SEG, ENTER, LEAVE, ENTER_ALL, LEAVE_ALL, ENTER_SHUT, LEAVE_SHUT = 0, 4, 8, 12, 16, 20, 24, 25
ROW_ENTER, ROW_LEAVE = 8, 12


def dot_nn(a, b):
    return lax.dot_general(a, b, (((1,), (0,)), ((), ())), preferred_element_type=F32)


def dot_nt(a, b):
    return lax.dot_general(a, b, (((1,), (1,)), ((), ())), preferred_element_type=F32)


def dot_tn(a, b):
    return lax.dot_general(a, b, (((0,), (0,)), ((), ())), preferred_element_type=F32)


def params(limit=VMEM_BYTES, **more):
    return pltpu.CompilerParams(vmem_limit_bytes=limit, **more)


def chunk_rows(c):
    return pl.ds(pl.multiple_of(c * CHUNK, CHUNK), CHUNK)


def diagonal(a, b):
    zero = jnp.zeros_like(a)
    return jnp.concatenate(
        [jnp.concatenate([a, zero], axis=1), jnp.concatenate([zero, b], axis=1)], axis=0
    )


def diagonal_of(pair):
    return diagonal(pair[:, :128], pair[:, 128:])


def pair_nt(a, b):
    return jnp.concatenate(
        [dot_nt(a[:, :128], b[:, :128]), dot_nt(a[:, 128:], b[:, 128:])], axis=1
    )


def widen(table, lane):
    shape = (table.shape[0], 128)
    return jnp.concatenate(
        [jnp.broadcast_to(table[:, i : i + 1], shape) for i in (lane, lane + 1)], axis=1
    )


def cost(flops, moved):
    return pl.CostEstimate(flops=int(flops), bytes_accessed=int(moved), transcendentals=0)


VMEM = pl.BlockSpec(memory_space=pltpu.VMEM)
SMEM = pl.BlockSpec(memory_space=pltpu.SMEM)


def store_pieces(out_ref, value):
    half = value.shape[0] // 2
    for r in range(2):
        for l in range(2):
            out_ref[2 * r + l] = value[r * half : (r + 1) * half, l * 128 : (l + 1) * 128]


def load_pieces(ref):
    rows = [jnp.concatenate([ref[2 * r], ref[2 * r + 1]], axis=1) for r in range(2)]
    return jnp.concatenate(rows, axis=0)


def piece_shape(rows, width):
    return (rows // BLOCK * 4, width // 2, BLOCK // 2)


def piece_spec(width):
    return pl.BlockSpec((4, width // 2, BLOCK // 2), lambda i: (i, 0, 0))


def low_kernel(x_ref, down_ref, out_ref, x_held, down_held, out_held, sems, out_sems):
    count = x_ref.shape[0] // BLOCK
    first = pltpu.make_async_copy(down_ref, down_held, sems.at[count])
    first.start()
    copies, results = [], []
    for c in range(count):
        rows = pl.ds(c * BLOCK, BLOCK)
        copies.append(pltpu.make_async_copy(x_ref.at[rows], x_held.at[rows], sems.at[c]))
        copies[c].start()
    first.wait()
    for c in range(count):
        copies[c].wait()
        part = dot_nt(down_held[...], x_held[c * BLOCK : (c + 1) * BLOCK, :]).astype(BF16)
        pieces = pl.ds(4 * c, 4)
        store_pieces(out_held.at[pieces], part)
        results.append(pltpu.make_async_copy(out_held.at[pieces], out_ref.at[pieces], out_sems.at[c]))
        results[c].start()
    for result in results:
        result.wait()


def partial_low(x, down):
    rows, _ = x.shape
    far = pl.BlockSpec(memory_space=pltpu.HBM)
    shape = piece_shape(rows, down.shape[0])
    return pl.pallas_call(
        low_kernel,
        out_shape=jax.ShapeDtypeStruct(shape, BF16),
        in_specs=[far, far],
        out_specs=far,
        scratch_shapes=[
            pltpu.VMEM(x.shape, BF16),
            pltpu.VMEM(down.shape, BF16),
            pltpu.VMEM(shape, BF16),
            pltpu.SemaphoreType.DMA((rows // BLOCK + 1,)),
            pltpu.SemaphoreType.DMA((rows // BLOCK,)),
        ],
        compiler_params=params(),
        name="partial_low",
    )(*(pltpu.with_memory_space_constraint(a, pltpu.HBM) for a in (x, down)))


def sum_spread_kernel(in_ref, out_ref):
    count = in_ref.shape[0]
    total = in_ref[0].astype(F32)
    for i in range(1, count):
        total = total + in_ref[i].astype(F32)
    total = total.astype(BF16)
    for i in range(count):
        out_ref[i] = total


def exchange(pieces):
    return lax.all_to_all(pieces, ("z", "x"), 0, 0)


def sum_spread(pieces):
    return pl.pallas_call(
        sum_spread_kernel,
        out_shape=jax.ShapeDtypeStruct(pieces.shape, BF16),
        in_specs=[VMEM],
        out_specs=VMEM,
        compiler_params=params(),
        name="sum_spread",
    )(pieces)


def decay_kernel(meta_ref, decay_ref, start_ref, row_ref, col_ref, pass_ref):
    heads, rows = decay_ref.shape
    live = meta_ref[0]
    slot = lax.broadcasted_iota(jnp.int32, (1, rows), 1)
    keep = slot < live
    decay = jnp.where(keep, decay_ref[...].astype(F32), 0.0)
    starts = jnp.where(keep, start_ref[...].astype(F32), 0.0)
    both = jnp.concatenate([decay, starts, jnp.zeros((8 - heads - 1, rows), F32)], axis=0)
    both = both.astype(BF16)
    row_i = lax.broadcasted_iota(jnp.int32, (CHUNK, CHUNK), 0)
    col_i = lax.broadcasted_iota(jnp.int32, (CHUNK, CHUNK), 1)
    upper = jnp.where(row_i <= col_i, 1.0, 0.0).astype(BF16)
    lower = jnp.where(row_i >= col_i, 1.0, 0.0).astype(BF16)
    count = rows // CHUNK
    enters, leaves, passes = [], [], []
    prefix = jnp.ones((heads, 128), F32)
    for c in range(count):
        span = slice(c * CHUNK, (c + 1) * CHUNK)
        piece = both[:, span]
        by_row = dot_nn(piece, upper)
        by_col = dot_nt(lower, piece)
        here = keep[:, span]
        here_col = c * CHUNK + lax.broadcasted_iota(jnp.int32, (CHUNK, 1), 0) < live
        head_row = lax.broadcasted_iota(jnp.int32, (8, CHUNK), 0)
        head_lane = lax.broadcasted_iota(jnp.int32, (CHUNK, 8), 1)
        row_ref[0:8, span] = jnp.where(here | (head_row != heads), by_row, -1.0)
        end_row = by_row[:, CHUNK - 1 : CHUNK]
        row_seg = by_row[heads : heads + 1]
        row_ref[ROW_ENTER : ROW_ENTER + heads, span] = jnp.where(
            (row_seg == 0.0) & here, jnp.exp(by_row[:heads]), 0.0
        )
        row_ref[ROW_LEAVE : ROW_LEAVE + heads, span] = jnp.where(
            (row_seg == end_row[heads : heads + 1]) & here, jnp.exp(end_row[:heads] - by_row[:heads]), 0.0
        )
        col_ref[span, 0:8] = jnp.where(here_col | (head_lane != heads), by_col, -2.0)
        cum = by_col[:, :heads]
        seg = by_col[:, heads : heads + 1]
        cum_end = by_col[CHUNK - 1 : CHUNK, :heads]
        seg_end = by_col[CHUNK - 1 : CHUNK, heads : heads + 1]
        may_enter = (seg == 0.0) & here_col
        may_leave = (seg == seg_end) & here_col
        enter = jnp.where(may_enter, jnp.exp(cum), 0.0)
        leave = jnp.where(may_leave, jnp.exp(cum_end - cum), 0.0)
        col_ref[span, ENTER_SHUT : ENTER_SHUT + 1] = jnp.where(may_enter, 0.0, NEGATIVE)
        col_ref[span, LEAVE_SHUT : LEAVE_SHUT + 1] = jnp.where(may_leave, 0.0, NEGATIVE)
        col_ref[span, ENTER : ENTER + heads] = enter
        col_ref[span, LEAVE : LEAVE + heads] = leave
        enters.append(enter)
        leaves.append(leave)
        passes.append(jnp.where(seg_end == 0.0, jnp.exp(cum_end), 0.0))
        passing_col = jnp.where(end_row[heads : heads + 1] == 0.0, jnp.exp(end_row[:heads]), 0.0)
        passing_rows_here = jnp.broadcast_to(passing_col, (heads, 128))
        pass_ref[c * heads : (c + 1) * heads, :] = passing_rows_here
        first = (count + c) * heads
        pass_ref[first : first + heads, :] = prefix
        first = (2 * count + c) * heads
        pass_ref[first : first + heads, :] = jnp.broadcast_to(end_row[:heads], (heads, 128))
        prefix = prefix * passing_rows_here
    before = jnp.ones((1, heads), F32)
    for c in range(count):
        span = slice(c * CHUNK, (c + 1) * CHUNK)
        col_ref[span, ENTER_ALL : ENTER_ALL + heads] = enters[c] * before
        before = before * passes[c]
    after = jnp.ones((1, heads), F32)
    for c in reversed(range(count)):
        span = slice(c * CHUNK, (c + 1) * CHUNK)
        col_ref[span, LEAVE_ALL : LEAVE_ALL + heads] = leaves[c] * after
        after = after * passes[c]


def decay_tables(meta, decay, starts):
    heads, rows = decay.shape
    count = rows // CHUNK
    return pl.pallas_call(
        decay_kernel,
        out_shape=(
            jax.ShapeDtypeStruct((16, rows), F32),
            jax.ShapeDtypeStruct((rows, 128), F32),
            jax.ShapeDtypeStruct((3 * count * heads, 128), F32),
        ),
        in_specs=[SMEM, VMEM, VMEM],
        out_specs=(VMEM, VMEM, VMEM),
        compiler_params=params(),
        cost_estimate=cost(4e9, 1e6),
        name="decay_tables",
    )(meta, decay, starts.reshape(1, rows))


def project_kernel(
    frozen_ref, low_ref, up_ref, grad_ref, row_ref, pass_ref,
    moving_ref, before_ref, after_ref, summary_ref, returning, held, sems,
):
    chunks = returning.shape[0]
    rank = up_ref.shape[1]
    features = frozen_ref.shape[2]
    heads = features // 128
    size = heads * 128
    copies = []
    for n in range(frozen_ref.shape[1] // BLOCK):
        rows = pl.ds(n * BLOCK, BLOCK)
        copies.append(pltpu.make_async_copy(frozen_ref.at[:, rows], held.at[:, rows], sems.at[n]))
    for copy in copies[:2]:
        copy.start()
    states = [jnp.zeros((128, 128), F32)] * heads
    for n, copy in enumerate(copies):
        low = load_pieces(low_ref.at[pl.ds(4 * n, 4)])
        lifted = [dot_tn(low[i * rank : (i + 1) * rank, :], up_ref[i]) for i in range(3)]
        copy.wait()
        if n + 2 < len(copies):
            copies[n + 2].start()
        rows = pl.ds(n * BLOCK, BLOCK)
        for i in range(3):
            moving_ref[i, rows, :] = (held[i, rows, :].astype(F32) + lifted[i]).astype(BF16)
        for c in range(n * BLOCK // CHUNK, (n + 1) * BLOCK // CHUNK):
            rows = pl.ds(c * CHUNK, CHUNK)
            for h in range(heads):
                span = slice(h * 128, (h + 1) * 128)
                passing = pass_ref[c * heads + h : c * heads + h + 1, :]
                leave = row_ref[ROW_LEAVE + h : ROW_LEAVE + h + 1, rows]
                enter = row_ref[ROW_ENTER + h : ROW_ENTER + h + 1, rows]
                valued = (moving_ref[2, rows, span].T.astype(F32) * leave).astype(BF16)
                scaled = (moving_ref[0, rows, span].T.astype(F32) * enter).astype(BF16)
                before_ref[c, h] = states[h].astype(BF16)
                states[h] = passing * states[h] + dot_nn(valued, moving_ref[1, rows, span])
                returning[c, h] = dot_nn(scaled, grad_ref[rows, span])
    tails = []
    for h in range(heads):
        back = jnp.zeros((128, 128), F32)
        whole = jnp.ones((1, 128), F32)
        for c in reversed(range(chunks)):
            passing = pass_ref[c * heads + h : c * heads + h + 1, :]
            after_ref[c, h] = back.astype(BF16)
            back = passing * back + returning[c, h]
            whole = whole * passing
        summary_ref[h * 128 : (h + 1) * 128, :] = states[h].astype(BF16)
        summary_ref[size + h * 128 : size + (h + 1) * 128, :] = back.astype(BF16)
        tails.append(passing_rows(whole))
    summary_ref[2 * size : 2 * size + 4 * heads, :] = jnp.concatenate(tails, axis=0).astype(BF16)


def passing_rows(row):
    first = row.astype(BF16).astype(F32)
    rest = row - first
    second = rest.astype(BF16).astype(F32)
    third = (rest - second).astype(BF16).astype(F32)
    return jnp.concatenate([first, second, third, jnp.zeros((1, 128), F32)], axis=0)


def project(frozen, low, up, grad, row, passes):
    _, rows, features = frozen.shape
    heads = features // 128
    count = rows // CHUNK
    summary_rows = 2 * features + 4 * heads
    states = jax.ShapeDtypeStruct((count, heads, 128, 128), BF16)
    return pl.pallas_call(
        project_kernel,
        out_shape=(
            jax.ShapeDtypeStruct((3, rows, features), BF16),
            states,
            states,
            jax.ShapeDtypeStruct((summary_rows, 128), BF16),
        ),
        in_specs=[pl.BlockSpec(memory_space=pltpu.HBM)] + [VMEM] * 5,
        out_specs=(VMEM,) * 4,
        scratch_shapes=[
            pltpu.VMEM(states.shape, F32),
            pltpu.VMEM(frozen.shape, BF16),
            pltpu.SemaphoreType.DMA((rows // BLOCK,)),
        ],
        compiler_params=params(),
        cost_estimate=cost(4e9, 10e6),
        name="project",
    )(pltpu.with_memory_space_constraint(frozen, pltpu.HBM), low, up, grad, row, passes)


def passing_of(ref, base):
    return (
        ref[base : base + 1, :].astype(F32)
        + ref[base + 1 : base + 2, :].astype(F32)
        + ref[base + 2 : base + 3, :].astype(F32)
    )


def join_kernel(meta_ref, own_ref, mate_ref, *out_refs):
    y = meta_ref[1]
    core = meta_ref[2]
    total = own_ref.shape[0]
    heads = total // (2 * 128 + 4)
    size = heads * 128
    chips = len(out_refs) + 1
    second = core == 1
    tails = []
    for h in range(heads):
        rows = slice(h * 128, (h + 1) * 128)
        back_rows = slice(size + h * 128, size + (h + 1) * 128)
        base = 2 * size + 4 * h
        own_pass = passing_of(own_ref, base)
        mate_pass = passing_of(mate_ref, base)
        own_state = own_ref[rows, :].astype(F32)
        mate_state = mate_ref[rows, :].astype(F32)
        own_back = own_ref[back_rows, :].astype(F32)
        mate_back = mate_ref[back_rows, :].astype(F32)
        one = jnp.ones_like(own_pass)
        state = jnp.where(second, own_pass, one) * mate_state + jnp.where(second, one, mate_pass) * own_state
        back = jnp.where(second, one, own_pass) * mate_back + jnp.where(second, mate_pass, one) * own_back
        tails.append(passing_rows(own_pass * mate_pass))
        for k, out_ref in enumerate(out_refs):
            later = y + (k + 1) < chips
            out_ref[rows, :] = jnp.where(later, state, back).astype(BF16)
    tail = jnp.concatenate(tails, axis=0).astype(BF16)
    for out_ref in out_refs:
        out_ref[size : size + 4 * heads, :] = tail


def join(meta, own, mate, chips):
    heads = own.shape[0] // (2 * 128 + 4)
    message = jax.ShapeDtypeStruct((heads * (128 + 4), 128), BF16)
    return pl.pallas_call(
        join_kernel,
        out_shape=(message,) * (chips - 1),
        in_specs=[SMEM, VMEM, VMEM],
        out_specs=(VMEM,) * (chips - 1),
        compiler_params=params(),
        name="join",
    )(meta, own, mate)


def inside_kernel(moving_ref, grad_ref, row_ref, col_ref, pass_ref, before_ref, after_ref, part_ref):
    features = moving_ref.shape[2]
    heads = features // 128
    square = (CHUNK, CHUNK)
    row_i = lax.broadcasted_iota(jnp.int32, square, 0)
    col_i = lax.broadcasted_iota(jnp.int32, square, 1)
    end_base = pass_ref.shape[0] // 3 * 2

    def paired(make, h):
        return jnp.concatenate([make(h), make(h + 1)], axis=1)

    @pl.loop(0, moving_ref.shape[1] // CHUNK, unroll=UNROLL)
    def _(c):
        rows = chunk_rows(c)
        col = col_ref[rows, :]
        row = row_ref[0:8, rows]
        same = col[:, SEG : SEG + 1] == row[SEG : SEG + 1, :]
        shut = jnp.where(same & (row_i <= col_i), 0.0, NEGATIVE)
        shut_turned = jnp.where(same & (row_i >= col_i), 0.0, NEGATIVE)
        enter_shut = jnp.broadcast_to(col[:, ENTER_SHUT : ENTER_SHUT + 1], square)
        leave_shut = jnp.broadcast_to(col[:, LEAVE_SHUT : LEAVE_SHUT + 1], square)
        sums = [jnp.broadcast_to(col[:, h : h + 1], square) for h in range(heads)]
        ends = pass_ref[pl.ds(end_base + c * heads, heads), :]
        for h in range(0, heads, 2):
            span = slice(h * 128, (h + 2) * 128)
            q = moving_ref[0, rows, span]
            k = moving_ref[1, rows, span]
            v = moving_ref[2, rows, span]
            g = grad_ref[rows, span]
            weights = paired(lambda i: jnp.exp((row[i : i + 1, :] - sums[i]) + shut), h)
            turned = paired(lambda i: jnp.exp((sums[i] - row[i : i + 1, :]) + shut_turned), h)
            enter = paired(lambda i: jnp.exp(sums[i] + enter_shut), h)
            leave = paired(lambda i: jnp.exp((ends[i : i + 1, :] - sums[i]) + leave_shut), h)
            queries = diagonal_of(q)
            cotangents = diagonal_of(g)
            before = diagonal(before_ref[c, h], before_ref[c, h + 1])
            after = diagonal(after_ref[c, h], after_ref[c, h + 1])
            a = (pair_nt(k, q) * weights).astype(BF16)
            b = (pair_nt(v, g) * weights).astype(BF16)
            b_turned = (pair_nt(g, v) * turned).astype(BF16)
            part_ref[0, rows, span] = dot_nn(b_turned, diagonal_of(k)) + enter * dot_nn(g, before)
            part_ref[1, rows, span] = dot_nn(b, queries) + leave * dot_nt(v, after)
            part_ref[2, rows, span] = dot_nn(a, cotangents) + leave * dot_nn(k, after)


def inside(moving, grad, row, col, passes, before, after):
    return pl.pallas_call(
        inside_kernel,
        out_shape=jax.ShapeDtypeStruct(moving.shape, F32),
        in_specs=[VMEM] * 7,
        out_specs=VMEM,
        compiler_params=params(),
        cost_estimate=cost(12e9, 12e6),
        name="inside",
    )(moving, grad, row, col, passes, before, after)


def late_kernel(
    moving_ref, row_ref, col_ref, pass_ref, before_ref, state_ref, out_ref,
    held, before_held, attn, sems, before_sems, out_sems,
):
    features = moving_ref.shape[2]
    heads = features // 128
    inverse = 1.0 / 128.0
    prefix_base = pass_ref.shape[0] // 3
    square = (CHUNK, CHUNK)
    row_i = lax.broadcasted_iota(jnp.int32, square, 0)
    col_i = lax.broadcasted_iota(jnp.int32, square, 1)
    per_block = BLOCK // CHUNK
    copies, results = [], []
    for n in range(moving_ref.shape[1] // BLOCK):
        rows = pl.ds(n * BLOCK, BLOCK)
        chunks = pl.ds(n * per_block, per_block)
        copies.append(pltpu.make_async_copy(moving_ref.at[:, rows], held.at[:, rows], sems.at[n]))
        copies.append(
            pltpu.make_async_copy(before_ref.at[chunks], before_held.at[chunks], before_sems.at[n])
        )
    for copy in copies[:4]:
        copy.start()
    for n in range(moving_ref.shape[1] // BLOCK):
        copies[2 * n].wait()
        copies[2 * n + 1].wait()
        for copy in copies[2 * n + 4 : 2 * n + 6]:
            copy.start()
        for c in range(n * per_block, (n + 1) * per_block):
            rows = pl.ds(c * CHUNK, CHUNK)
            col = col_ref[rows, :]
            row = row_ref[0:8, rows]
            same = col[:, SEG : SEG + 1] == row[SEG : SEG + 1, :]
            shut = jnp.where(same & (row_i >= col_i), 0.0, NEGATIVE)
            enter_shut = jnp.broadcast_to(col[:, ENTER_SHUT : ENTER_SHUT + 1], square)
            for h in range(0, heads, 2):
                span = slice(h * 128, (h + 2) * 128)
                q = held[0, rows, span]
                k = held[1, rows, span]
                weights, enter, states = [], [], []
                for i in (h, h + 1):
                    sums = jnp.broadcast_to(col[:, i : i + 1], square)
                    weights.append(jnp.exp((sums - row[i : i + 1, :]) + shut))
                    enter.append(jnp.exp(sums + enter_shut))
                    first = prefix_base + c * heads + i
                    prefix = pass_ref[first : first + 1, :]
                    state = before_held[c, i].astype(F32) + prefix * state_ref[i].astype(F32)
                    states.append(state.astype(BF16))
                a = (pair_nt(q, k) * jnp.concatenate(weights, axis=1)).astype(BF16)
                carried = jnp.concatenate(
                    [dot_nt(q[:, :128], states[0]), dot_nt(q[:, 128:], states[1])], axis=1
                )
                out = dot_nn(a, diagonal_of(held[2, rows, span]))
                out = out + jnp.concatenate(enter, axis=1) * carried
                attn[rows, span] = (out * inverse).astype(BF16)
        rows = pl.ds(n * BLOCK, BLOCK)
        results.append(pltpu.make_async_copy(attn.at[rows], out_ref.at[rows], out_sems.at[n]))
        results[n].start()
    for result in results:
        result.wait()


def late(moving, row, col, passes, before, state):
    _, rows, features = moving.shape
    moving, before = (pltpu.with_memory_space_constraint(a, pltpu.HBM) for a in (moving, before))
    far = pl.BlockSpec(memory_space=pltpu.HBM)
    blocks = rows // BLOCK
    return pl.pallas_call(
        late_kernel,
        out_shape=jax.ShapeDtypeStruct((rows, features), BF16),
        in_specs=[far, VMEM, VMEM, VMEM, far, VMEM],
        out_specs=far,
        scratch_shapes=[
            pltpu.VMEM(moving.shape, BF16),
            pltpu.VMEM(before.shape, BF16),
            pltpu.VMEM((rows, features), BF16),
            pltpu.SemaphoreType.DMA((blocks,)),
            pltpu.SemaphoreType.DMA((blocks,)),
            pltpu.SemaphoreType.DMA((blocks,)),
        ],
        compiler_params=params(),
        cost_estimate=cost(6e9, 6e6),
        name="late",
    )(moving, row, col, passes, before, state)


def store_halves(core, total, keep_ref, send_ref):
    half = total.shape[0] // 2
    keep_ref[...] = total[pl.ds(pl.multiple_of(core * half, 16), half), :].astype(BF16)
    send_ref[...] = total[pl.ds(pl.multiple_of((1 - core) * half, 16), half), :].astype(BF16)


def finish_kernel(
    chips, meta_ref, moving_ref, g_ref, part_ref, col_ref, low_ref, up_ref, mate_ref, *refs
):
    message_refs = refs[: chips - 1]
    out_ref, low_grad_ref, state_in, keep_ref, send_ref = refs[chips - 1 : chips + 4]
    back_in, grad_ref, total, sems = refs[chips + 4 :]
    rank = up_ref.shape[1]
    features = moving_ref.shape[2]
    heads = features // 128
    size = heads * 128
    count = moving_ref.shape[1] // BLOCK
    inverse = 1.0 / 128.0
    y = meta_ref[1]
    second = meta_ref[2] == 1
    for h in range(heads):
        rows = slice(h * 128, (h + 1) * 128)
        factor = jnp.ones((1, 128), F32)
        state = jnp.zeros((128, 128), F32)
        for k in range(1, chips):
            ref = message_refs[k - 1]
            state = state + jnp.where(k <= y, factor, 0.0) * ref[rows, :].astype(F32)
            factor = factor * passing_of(ref, size + 4 * h)
        factor = jnp.ones((1, 128), F32)
        back = jnp.zeros((128, 128), F32)
        for k in reversed(range(1, chips)):
            ref = message_refs[k - 1]
            back = back + jnp.where(k > y, factor, 0.0) * ref[rows, :].astype(F32)
            factor = factor * passing_of(ref, size + 4 * h)
        mate_pass = passing_of(mate_ref, 2 * size + 4 * h)
        mate_state = mate_ref[rows, :].astype(F32)
        mate_back = mate_ref[size + h * 128 : size + (h + 1) * 128, :].astype(F32)
        state_in[h] = jnp.where(second, mate_pass * state + mate_state, state).astype(BF16)
        back_in[h] = jnp.where(second, back, mate_pass * back + mate_back).astype(BF16)
    copies = []
    for n in range(count):
        rows = pl.ds(n * BLOCK, BLOCK)
        col = col_ref[rows, :]
        for h in range(0, heads, 2):
            span = slice(h * 128, (h + 2) * 128)
            enter = widen(col, ENTER_ALL + h)
            leave = widen(col, LEAVE_ALL + h)
            state = diagonal(state_in[h], state_in[h + 1])
            back = diagonal(back_in[h], back_in[h + 1])
            query = part_ref[0, rows, span] + enter * dot_nn(g_ref[rows, span], state)
            key = part_ref[1, rows, span] + leave * dot_nt(moving_ref[2, rows, span], back)
            value = part_ref[2, rows, span] + leave * dot_nn(moving_ref[1, rows, span], back)
            for i, result in enumerate((query, key, value)):
                grad_ref[i, rows, span] = (result * inverse).astype(BF16)
            part = (slice(None), rows, pl.ds(h * 128, 256))
            copies.append(
                pltpu.make_async_copy(grad_ref.at[part], out_ref.at[part], sems.at[n * heads // 2 + h // 2])
            )
            copies[-1].start()
    for n in range(count):
        rows = pl.ds(n * BLOCK, BLOCK)
        low_grad = [dot_nt(up_ref[i], grad_ref[i, rows, :]).astype(BF16) for i in range(3)]
        store_pieces(low_grad_ref.at[pl.ds(4 * n, 4)], jnp.concatenate(low_grad, axis=0))
        low = load_pieces(low_ref.at[pl.ds(4 * n, 4)])
        for i in range(3):
            lanes = slice(i * rank, (i + 1) * rank)
            term = dot_nn(low[lanes, :], grad_ref[i, rows, :])
            total[lanes, :] = term if n == 0 else total[lanes, :] + term
    store_halves(meta_ref[2], total, keep_ref, send_ref)
    for copy in copies:
        copy.wait()


def finish(meta, moving, grad, part, col, low, up, mate, messages):
    _, rows, features = moving.shape
    heads = features // 128
    width = up.shape[0] * up.shape[1]
    half = jax.ShapeDtypeStruct((width // 2, features), BF16)
    chips = len(messages) + 1
    return pl.pallas_call(
        functools.partial(finish_kernel, chips),
        out_shape=(
            jax.ShapeDtypeStruct(moving.shape, BF16),
            jax.ShapeDtypeStruct(piece_shape(rows, width), BF16),
            jax.ShapeDtypeStruct((heads, 128, 128), BF16),
            half,
            half,
        ),
        in_specs=[SMEM] + [VMEM] * (7 + len(messages)),
        out_specs=(pl.BlockSpec(memory_space=pltpu.HBM),) + (VMEM,) * 4,
        scratch_shapes=[
            pltpu.VMEM((heads, 128, 128), BF16),
            pltpu.VMEM(moving.shape, BF16),
            pltpu.VMEM((width, features), F32),
            pltpu.SemaphoreType.DMA((rows // BLOCK * heads // 2,)),
        ],
        compiler_params=params(),
        cost_estimate=cost(4e9, 14e6),
        name="finish",
    )(meta, moving, grad, part, col, low, up, mate, *messages)


def down_kernel(meta_ref, x_ref, grad_ref, keep_ref, send_ref, total):
    value = jnp.zeros(total.shape, F32)
    for c in range(x_ref.shape[0] // BLOCK):
        low_grad = load_pieces(grad_ref.at[pl.ds(4 * c, 4)])
        value = value + dot_nn(low_grad, x_ref[c * BLOCK : (c + 1) * BLOCK, :])
    total[...] = value
    store_halves(meta_ref[2], total, keep_ref, send_ref)


def partial_down(meta, x, low_grad):
    width = 2 * low_grad.shape[1]
    half = jax.ShapeDtypeStruct((width // 2, x.shape[1]), BF16)
    return pl.pallas_call(
        down_kernel,
        out_shape=(half, half),
        in_specs=[SMEM, VMEM, VMEM],
        out_specs=(VMEM, VMEM),
        scratch_shapes=[pltpu.VMEM((width, x.shape[1]), F32)],
        compiler_params=params(),
        name="partial_down",
    )(meta, x, low_grad)


def halves_kernel(meta_ref, own_ref, mate_ref, out_ref):
    core = meta_ref[2]
    half = own_ref.shape[0]
    out_ref[pl.ds(pl.multiple_of(core * half, 8), half), :] = own_ref[...]
    out_ref[pl.ds(pl.multiple_of((1 - core) * half, 8), half), :] = mate_ref[...]


def join_halves(meta, own, mate):
    return pl.pallas_call(
        halves_kernel,
        out_shape=jax.ShapeDtypeStruct((2 * own.shape[0], own.shape[1]), F32),
        in_specs=[SMEM, VMEM, VMEM],
        out_specs=VMEM,
        compiler_params=params(),
        name="join_halves",
    )(meta, own, mate)


def add_kernel(*refs):
    total = refs[0][...].astype(F32)
    for ref in refs[1:-1]:
        total = total + ref[...].astype(F32)
    refs[-1][...] = total.astype(refs[-1].dtype)


def add_all(arrays, dtype):
    return pl.pallas_call(
        add_kernel,
        out_shape=jax.ShapeDtypeStruct(arrays[0].shape, dtype),
        in_specs=[VMEM] * len(arrays),
        out_specs=VMEM,
        compiler_params=params(),
        name="add_all",
    )(*arrays)


def to_mate(a):
    return lax.ppermute(a, "core", [(0, 1), (1, 0)])


def along_y(a, k):
    count = lax.axis_size("y")
    return lax.ppermute(a, "y", [(i, (i + k) % count) for i in range(count)])


def local(inputs, frozen, adapter_down, adapter_up, out_grad, log_decay, doc_start, lengths):
    y, core = lax.axis_index("y"), lax.axis_index("core")
    chips = lax.axis_size("y")
    rank = adapter_up.shape[1]
    meta = jnp.stack([lengths[2 * y + core], y, core]).astype(jnp.int32)
    down = jnp.swapaxes(adapter_down, 1, 2).reshape(3 * rank, inputs.shape[1])
    row, col, passes = decay_tables(meta, log_decay, doc_start)
    low = exchange(sum_spread(exchange(partial_low(inputs, down))))
    moving, before, after, summary = project(frozen, low, adapter_up, out_grad, row, passes)
    mate = to_mate(summary)
    messages = [along_y(m, k + 1) for k, m in enumerate(join(meta, summary, mate, chips))]
    part = inside(moving, out_grad, row, col, passes, before, after)
    grads, low_grad_part, state, up_keep, up_send = finish(
        meta, moving, out_grad, part, col, low, adapter_up, mate, messages
    )
    up_chip = add_all([up_keep, to_mate(up_send)], BF16)
    up_parts = [up_chip] + [along_y(up_chip, k) for k in range(1, chips)]
    pieces, up_chip = lax.optimization_barrier((exchange(low_grad_part), up_chip))
    attn = late(moving, row, col, passes, before, state)
    low_grad, attn, *up_parts = lax.optimization_barrier(
        [exchange(sum_spread(pieces)), attn] + up_parts
    )
    down_keep, down_send = partial_down(meta, inputs, low_grad)
    down_chip = add_all([down_keep, to_mate(down_send)], BF16)
    down_chip, *up_parts = lax.optimization_barrier([down_chip] + up_parts)
    down_parts = [down_chip] + [along_y(down_chip, k) for k in range(1, chips)]
    up_half = add_all(up_parts, F32)
    up_total = join_halves(meta, up_half, to_mate(up_half))
    up_total, *down_parts = lax.optimization_barrier([up_total] + down_parts)
    down_half = add_all(down_parts, F32)
    down_total = join_halves(meta, down_half, to_mate(down_half))
    down_total = jnp.swapaxes(down_total.reshape(3, rank, inputs.shape[1]), 1, 2)
    return (attn, grads, down_total, up_total.reshape(adapter_up.shape))


def solution(mesh):
    seq, head = mesh.shape["seq"], mesh.shape["head"]
    side = 1
    while side * side < head:
        side *= 2
    mesh = jax.sharding.Mesh(
        mesh.devices.reshape(seq // 2, 2, head // side, side), ("y", "core", "z", "x")
    )
    seq, head = ("y", "core"), ("z", "x")
    in_specs = (
        P(seq, head),
        P(None, seq, head),
        P(None, head, None),
        P(None, None, head),
        P(seq, head),
        P(head, seq),
        P(seq),
        P(),
    )
    out_specs = (
        P(seq, head),
        P(None, seq, head),
        P(None, head, None),
        P(None, None, head),
    )
    return jax.shard_map(local, mesh=mesh, in_specs=in_specs, out_specs=out_specs, check_vma=False)
```
